128 devices in a mesh: dp: 16 (over z_hi, y, core), fsdp: 8 (over x, z_lo).
Axes of the slice: x: 4, y: 4, z: 4 (z_hi: 2, z_lo: 2; z = z_hi * 2 + z_lo), core: 2. Of those that a mesh axis runs over, the one named last changes fastest.
Arguments:
- tokens: bfloat16 [16384, 640], P(('dp', 'fsdp')), may hold values from -6 to 6
- w_query: bfloat16 [640, 1024], P(('dp', 'fsdp')), may hold values from -0.25 to 0.25
- w_key: bfloat16 [640, 256], P(('dp', 'fsdp')), may hold values from -0.25 to 0.25
- w_value: bfloat16 [640, 256], P(('dp', 'fsdp')), may hold values from -0.25 to 0.25
- w_out: bfloat16 [1024, 640], P(('dp', 'fsdp')), may hold values from -0.75 to 0.75
- w_gate: bfloat16 [640, 2048], P(('dp', 'fsdp')), may hold values from -0.25 to 0.25
- w_up: bfloat16 [640, 2048], P(('dp', 'fsdp')), may hold values from -0.25 to 0.25
- w_down: bfloat16 [2048, 640], P(('dp', 'fsdp')), may hold values from -0.125 to 0.125
- attn_gain: bfloat16 [640], P(('dp', 'fsdp')), may hold values from 0.5 to 1.5
- ffn_gain: bfloat16 [640], P(('dp', 'fsdp')), may hold values from 0.5 to 1.5
- head_gains: bfloat16 [512], P(('dp', 'fsdp')), may hold values from 0.8984375 to 1.59375
- lengths: int32 [16, 2], P('dp'), may hold values from 0 to 1024, as said below
- cotangent: bfloat16 [16384, 640], P(('dp', 'fsdp')), may hold values from -6 to 6
Outputs:
- block_out: bfloat16 [16384, 640], P(('dp', 'fsdp'))
- input_grad: float32 [16384, 640], P(('dp', 'fsdp'))
- grad_query: float32 [640, 1024], P(('dp', 'fsdp'))
- grad_key: float32 [640, 256], P(('dp', 'fsdp'))
- grad_value: float32 [640, 256], P(('dp', 'fsdp'))
- grad_out: float32 [1024, 640], P(('dp', 'fsdp'))
- grad_gate: float32 [640, 2048], P(('dp', 'fsdp'))
- grad_up: float32 [640, 2048], P(('dp', 'fsdp'))
- grad_down: float32 [2048, 640], P(('dp', 'fsdp'))
- grad_attn_gain: float32 [640], P(('dp', 'fsdp'))
- grad_ffn_gain: float32 [640], P(('dp', 'fsdp'))
- grad_head_gains: float32 [512], P(('dp', 'fsdp'))
The draws below stay inside these ranges and needn't reach their ends.
Inputs may be any that keep to these rules, and one draw needn't show every extreme that they name: `lengths`: each row is either one sequence of the whole group (1024, then 0) or two sequences of half the group each; in every draw at least one row, drawn from the seed, is a single sequence.
All inputs are finite; a program needn't handle non-finite values.
Results may differ from the reference program's by a relative error of at most 0.035.
Values may be sent and summed in bfloat16 or wider, within the bound.
A program may use at most 128 MiB of HBM per device.

```python
import math
import jax
import jax.numpy as jnp
from jax import lax

D = 640
H = 4
KV = 1
HD = 256
FF = 2048
TOK_DEV = 128
TOKENS = 16384
N_DP = 16
N_FSDP = 8


def draw_lengths(key, part):
    key = jax.random.fold_in(key, 11)
    group_rows = TOK_DEV * N_FSDP
    half_rows = group_rows // 2
    split_key, pick_key = jax.random.split(key)
    split_bits = jax.random.randint(split_key, (N_DP,), 0, 2).astype(jnp.int32)
    single_group = jax.random.randint(pick_key, (), 0, N_DP)
    group_ids = jnp.arange(N_DP, dtype=jnp.int32)
    split_bits = jnp.where(group_ids == single_group, 0, split_bits).astype(jnp.int32)
    first_len = jnp.where(split_bits == 1, half_rows, group_rows).astype(jnp.int32)
    second_len = jnp.where(split_bits == 1, half_rows, 0).astype(jnp.int32)
    return jnp.stack([first_len, second_len], axis=1).astype(jnp.int32)


def block_scale(own_key, extent, cuts, smallest, high):
    loudness = 1.0
    for position, parts in cuts:
        steps = jax.random.uniform(jax.random.fold_in(jax.random.fold_in(own_key, 6), position), (parts,), jnp.float32, smallest / len(cuts), high / len(cuts))
        loudness = loudness * jnp.repeat(jnp.exp(steps), extent[position] // parts).reshape((-1,) + (1,) * (len(extent) - 1 - position))
    return loudness


def scatter_about(stream_key, dims, scale, limit, pieces=(), kind=jnp.bfloat16):
    values = scale * jax.random.normal(stream_key, dims, jnp.float32)
    if pieces:
        values = values * block_scale(stream_key, dims, pieces, -0.22, 0.18)
    return jnp.clip(values, -limit, limit).astype(kind)


def setup_inputs(seed: int = 0) -> dict:
    key_list = jax.random.split(jax.random.key(seed), 14)
    tokens = scatter_about(key_list[0], (TOKENS, D), 1.0, 6.0, ((0, 128),))
    w_query = scatter_about(key_list[1], (D, H * HD), D ** -0.5, 0.25, ((0, 128),))
    w_key = scatter_about(key_list[2], (D, KV * HD), D ** -0.5, 0.25, ((0, 128),))
    w_value = scatter_about(key_list[3], (D, KV * HD), D ** -0.5, 0.25, ((0, 128),))
    w_out = scatter_about(key_list[4], (H * HD, D), (H * HD // 16) ** -0.5, 0.75, ((0, 128),))
    w_gate = scatter_about(key_list[5], (D, FF), D ** -0.5, 0.25, ((0, 128),))
    w_up = scatter_about(key_list[6], (D, FF), D ** -0.5, 0.25, ((0, 128),))
    w_down = scatter_about(key_list[7], (FF, D), FF ** -0.5, 0.125, ((0, 128),))
    attn_gain = jnp.clip(1.0 + 0.1 * jax.random.normal(key_list[8], (D,), jnp.float32), 0.5, 1.5).astype(jnp.bfloat16)
    ffn_gain = jnp.clip(1.0 + 0.1 * jax.random.normal(key_list[9], (D,), jnp.float32), 0.5, 1.5).astype(jnp.bfloat16)
    head_gains = jnp.clip(0.8984375 + 0.6953125 * jax.random.uniform(key_list[10], (2 * HD,), jnp.float32) ** block_scale(key_list[10], (2 * HD,), ((0, 128),), -0.2, 0.2), 0.8984375, 1.59375).astype(jnp.bfloat16)
    lengths = draw_lengths(jax.random.fold_in(key_list[13], 71), 0)
    cotangent = scatter_about(key_list[12], (TOKENS, D), 1.0, 6.0, ((0, 128),))
    return dict(tokens=tokens, w_query=w_query, w_key=w_key, w_value=w_value, w_out=w_out, w_gate=w_gate, w_up=w_up, w_down=w_down, attn_gain=attn_gain, ffn_gain=ffn_gain, head_gains=head_gains, lengths=lengths, cotangent=cotangent)


@jax.custom_vjp
def low(v):
    return lax.optimization_barrier(v.astype(jnp.bfloat16)).astype(jnp.float32)

@jax.custom_vjp
def low_back(v):
    return v

def low_keep(v):
    return (low(v), None)

def low_pass(kept, grad):
    return (grad,)

def back_keep(v):
    return (v, None)

def back_low(kept, grad):
    return (low(grad),)
low.defvjp(low_keep, low_pass)
low_back.defvjp(back_keep, back_low)
eps_norm = 1e-05
rope_base = 1000000.0
neg_large = -1e+30

def rms_scale(values):
    return lax.rsqrt(lax.optimization_barrier(jnp.mean(values * values, axis=-1, keepdims=True)) + eps_norm)

def matmul(left, right):
    return jnp.dot(left, right, precision=lax.Precision.HIGHEST, preferred_element_type=jnp.float32)

def rope_tables(positions):
    half_dim = HD // 2
    exponents = jnp.arange(half_dim, dtype=jnp.float32) * (2.0 / HD)
    frequencies = jnp.exp(-exponents * math.log(rope_base))
    angles = positions.astype(jnp.float32)[:, None] * frequencies[None, :]
    return (jnp.cos(angles)[:, None, :], jnp.sin(angles)[:, None, :])

def rotate(values, cosines, sine_table):
    half_dim = HD // 2
    first_half = values[..., :half_dim]
    second = values[..., half_dim:]
    return jnp.concatenate([first_half * cosines - second * sine_table, second * cosines + first_half * sine_table], axis=-1)

def seg_start(token_ids, seq_lengths):
    seq_ends = jnp.cumsum(seq_lengths).astype(jnp.int32)
    past_end = (token_ids[:, None] >= seq_ends[None, :]).astype(jnp.int32)
    segment = lax.optimization_barrier(jnp.sum(past_end, axis=1)).astype(jnp.int32)
    seq_start = lax.optimization_barrier(jnp.sum(past_end * seq_lengths[None, :], axis=1)).astype(jnp.int32)
    return (segment, token_ids - seq_start)

def attend(queries, key_rows, value_rows, segment):
    row_count = queries.shape[0]
    block_rows = math.gcd(row_count, 512)
    block_count = row_count // block_rows
    group_ratio = H // KV
    score_scale = 1.0 / math.sqrt(HD)
    query_blocks = queries.reshape(block_count, block_rows, KV, group_ratio, HD)
    first_rows = jnp.arange(block_count, dtype=jnp.int32) * block_rows
    key_ids = jnp.arange(row_count, dtype=jnp.int32)

    def one_block(block_item):
        query_block, first_row = block_item
        row_ids = first_row + jnp.arange(block_rows, dtype=jnp.int32)
        row_seg = lax.dynamic_slice_in_dim(segment, first_row, block_rows)
        allowed = (row_seg[:, None] == segment[None, :]) & (key_ids[None, :] <= row_ids[:, None])
        scores = jnp.einsum('qkgd,nkd->kgqn', query_block, key_rows, precision=lax.Precision.HIGHEST) * score_scale
        scores = low_back(scores)
        masked = jnp.where(allowed, scores, neg_large)
        row_max = lax.optimization_barrier(jnp.max(masked, axis=-1, keepdims=True))
        expd = jnp.where(allowed, jnp.exp(masked - row_max), 0.0)
        softmax_rows = expd / lax.optimization_barrier(jnp.sum(expd, axis=-1, keepdims=True))
        result = jnp.einsum('kgqn,nkd->qkgd', low(softmax_rows), value_rows, precision=lax.Precision.HIGHEST)
        return result.reshape(block_rows, H * HD)
    outputs = lax.map(jax.checkpoint(one_block), (query_blocks, first_rows))
    return outputs.reshape(row_count, H * HD)

def group_forward(params, inputs, seq_lengths):
    query_mat, key_mat, value_mat, output_mat, gate_mat, up_mat, down_mat, norm_one, norm_two, head_norm = params
    row_count = inputs.shape[0]
    segment, positions = seg_start(jnp.arange(row_count, dtype=jnp.int32), seq_lengths)
    normed = low(inputs * rms_scale(inputs) * norm_one)
    query_raw = low_back(matmul(normed, query_mat)).reshape(row_count, H, HD)
    key_raw = low_back(matmul(normed, key_mat)).reshape(row_count, KV, HD)
    value_rows = low(low_back(matmul(normed, value_mat))).reshape(row_count, KV, HD)
    cosines, sine_table = rope_tables(positions)
    queries = low(rotate(query_raw * rms_scale(query_raw) * head_norm[:HD], cosines, sine_table))
    key_rows = low(rotate(key_raw * rms_scale(key_raw) * head_norm[HD:], cosines, sine_table))
    attended = attend(queries.reshape(row_count, KV, H // KV, HD), key_rows, value_rows, segment)
    branch = low_back(matmul(low(low_back(attended)), output_mat))
    middle = inputs + branch
    ffn_in = low(middle * rms_scale(middle) * norm_two)
    gate_pre = low_back(matmul(ffn_in, gate_mat))
    up_pre = low_back(matmul(ffn_in, up_mat))
    hidden = low(jax.nn.gelu(gate_pre, approximate=True) * up_pre)
    return middle + low_back(matmul(hidden, down_mat))

def reference(tokens, w_query, w_key, w_value, w_out, w_gate, w_up, w_down, attn_gain, ffn_gain, head_gains, lengths, cotangent):
    params = tuple((weight.astype(jnp.float32) for weight in (w_query, w_key, w_value, w_out, w_gate, w_up, w_down, attn_gain, ffn_gain, head_gains)))
    group_rows = TOK_DEV * N_FSDP
    inputs = tokens.astype(jnp.float32).reshape(N_DP, group_rows, D)
    upstream = cotangent.astype(jnp.float32).reshape(N_DP, group_rows, D)

    def run(param_set, input_set):

        def step(carry, block_item):
            group_in, seq_lengths = block_item
            return (carry, jax.checkpoint(group_forward)(param_set, group_in, seq_lengths))
        unused, outputs = lax.scan(step, jnp.zeros((), jnp.float32), (input_set, lengths))
        return outputs
    outputs, pullback = jax.vjp(run, params, inputs)
    param_grads, input_grads = pullback(upstream)
    block_out = outputs.reshape(TOKENS, D).astype(jnp.bfloat16)
    input_grad = input_grads.reshape(TOKENS, D)
    return (block_out, input_grad, param_grads[0], param_grads[1], param_grads[2], param_grads[3], param_grads[4], param_grads[5], param_grads[6], param_grads[7], param_grads[8], param_grads[9])
```

```python
import functools
import math

import jax
import jax.numpy as jnp
from jax import lax
from jax.experimental import pallas as pl
from jax.experimental.pallas import tpu as pltpu
from jax.sharding import PartitionSpec as P

H = 4
KV = 1
HD = 256

MESH = pl.DeviceIdType.MESH
VMEM_BYTES = 56 * 1024 * 1024

ORDERS = ((0, 1, 2), (1, 2, 0), (2, 0, 1))
ROWS = (128, 112, 128)


def coords():
    dp = lax.axis_index("dp")
    fsdp = lax.axis_index("fsdp")
    return (fsdp // 2, (dp // 2) % 4, (dp // 8) * 2 + fsdp % 2, dp % 2)


def device(place):
    x, y, z, core = place
    return ((z // 2) * 8 + y * 2 + core, x * 2 + z % 2)


def shifted(place, axis, step):
    moved = list(place)
    moved[axis] = (place[axis] + step) % 4
    return tuple(moved)


def sibling(place):
    return place[:3] + (1 - place[3],)


def meet(partners):
    barrier = pltpu.get_barrier_semaphore()
    for partner in partners:
        pl.semaphore_signal(barrier, inc=1, device_id=device(partner), device_id_type=MESH)
    pl.semaphore_wait(barrier, len(partners))


def torus_partners(place):
    partners = [shifted(place, axis, step) for axis in range(3) for step in (1, 2, 3)]
    return partners + [sibling(place)]


def gather_kernel(in0, in1, in2, out0, out1, out2, send, recv, local):
    place = coords()
    core = place[3]
    ins, outs = (in0, in1, in2), (out0, out1, out2)
    keep = []
    for s in range(3):
        ka, kb, kc = (place[axis] for axis in ORDERS[s])
        copy = pltpu.make_async_copy(ins[s], outs[s].at[core, kc, kb, ka], local.at[s])
        copy.start()
        keep.append(copy)
    meet(torus_partners(place))

    def remote(s, slot, src, dst, to):
        return pltpu.make_async_remote_copy(
            src_ref=src,
            dst_ref=dst,
            send_sem=send.at[s, slot],
            recv_sem=recv.at[s, slot],
            device_id=device(to),
            device_id_type=MESH,
        )

    def same(s, slot, ref, to):
        return remote(s, slot, ref, ref, to)

    sent = []
    first = []
    for s in range(3):
        axis = ORDERS[s][0]
        ka, kb, kc = (place[a] for a in ORDERS[s])
        own = outs[s].at[core, kc, kb, ka]
        copies = [
            remote(s, step - 1, ins[s], own, shifted(place, axis, step)) for step in (1, 3, 2)
        ]
        for copy in copies:
            copy.start()
        first.append(copies)
        sent += copies

    def spread(s, base, axis, whole, part):
        k = place[axis]
        right, left = shifted(place, axis, 1), shifted(place, axis, 3)
        to_right = same(s, base, whole(k), right)
        to_left = same(s, base + 1, whole(k), left)
        to_right.start()
        to_left.start()

        def forward():
            to_right.wait_recv()
            on_right = same(s, base + 2, part((k + 3) % 4, 0), right)
            on_right.start()
            to_left.wait_recv()
            on_left = same(s, base + 3, part((k + 1) % 4, 1), left)
            on_left.start()
            sent.extend([to_right, to_left, on_right, on_left])
            return on_right, on_left

        return forward

    forwards = []
    for s in range(3):
        keep[s].wait()
        for copy in first[s]:
            copy.wait_recv()
        ka, kb, kc = (place[a] for a in ORDERS[s])
        out = outs[s]
        forwards.append(
            spread(
                s,
                3,
                ORDERS[s][1],
                lambda k, out=out, kc=kc: out.at[core, kc, k],
                lambda k, half, out=out, kc=kc: out.at[core, kc, k, pl.ds(2 * half, 2)],
            )
        )
    tails = [forward() for forward in forwards]
    forwards = []
    siblings = []
    for s in range(3):
        for copy in tails[s]:
            copy.wait_recv()
        ka, kb, kc = (place[a] for a in ORDERS[s])
        out = outs[s]
        forwards.append(
            spread(
                s,
                7,
                ORDERS[s][2],
                lambda k, out=out: out.at[core, k],
                lambda k, half, out=out: out.at[core, k, pl.ds(2 * half, 2)],
            )
        )
        copy = same(s, 11, out.at[core, kc], sibling(place))
        copy.start()
        siblings.append(copy)
    tails = []
    for s in range(3):
        tails.append(forwards[s]())
        kc = place[ORDERS[s][2]]
        for slot, k in ((12, (kc + 3) % 4), (13, (kc + 1) % 4)):
            copy = same(s, slot, outs[s].at[core, k], sibling(place))
            copy.start()
            siblings.append(copy)
    for s in range(3):
        kc = place[ORDERS[s][2]]
        for half in range(2):
            tails[s][half].wait_recv()
            ref = outs[s].at[core, (kc + 2) % 4, pl.ds(2 * half, 2)]
            copy = same(s, 14 + half, ref, sibling(place))
            copy.start()
            siblings.append(copy)
    for copy in siblings:
        copy.wait()
    for copy in sent:
        copy.wait_send()


def gather_blocks(parts):
    return pl.pallas_call(
        gather_kernel,
        out_shape=[jax.ShapeDtypeStruct((2, 4, 4, 4, rows, 128), jnp.bfloat16) for rows in ROWS],
        in_specs=[pl.BlockSpec(memory_space=pl.ANY)] * 3,
        out_specs=[pl.BlockSpec(memory_space=pl.ANY)] * 3,
        scratch_shapes=[
            pltpu.SemaphoreType.DMA((3, 16)),
            pltpu.SemaphoreType.DMA((3, 16)),
            pltpu.SemaphoreType.DMA((3,)),
        ],
        compiler_params=pltpu.CompilerParams(collective_id=0, has_side_effects=True),
        name="gather_blocks",
    )(*parts)


def add_blocks(total, count, first, *others):
    def step(i, carry):
        value = total[first + i].astype(jnp.float32)
        for other in others:
            value = value + other(i).astype(jnp.float32)
        total[first + i] = value.astype(total.dtype)
        return carry

    lax.fori_loop(0, count, step, 0)


def scatter_kernel(in0, in1, in2, out0, out1, out2, *scratch):
    place = coords()
    core = place[3]
    ins, outs = (in0, in1, in2), (out0, out1, out2)
    own, pair, far, mid, near, send, recv, local = (
        scratch[0:3],
        scratch[3:6],
        scratch[6:9],
        scratch[9:12],
        scratch[12:15],
        scratch[15],
        scratch[16],
        scratch[17],
    )
    loads = []
    for s in range(3):
        copy = pltpu.make_async_copy(ins[s].at[core], own[s], local.at[s])
        copy.start()
        loads.append(copy)
    meet(torus_partners(place))
    sent = []

    def remote(s, slot, src, dst, to):
        copy = pltpu.make_async_remote_copy(
            src_ref=src,
            dst_ref=dst,
            send_sem=send.at[s, slot],
            recv_sem=recv.at[s, slot],
            device_id=device(to),
            device_id_type=MESH,
        )
        copy.start()
        sent.append(copy)
        return copy

    pairs = {}
    for offset in (2, 1, 3, 0):
        for s in range(3):
            kc = place[ORDERS[s][2]]
            rows = pl.ds(((kc + offset) % 4) * 16, 16)
            pairs[s, offset] = remote(
                s, offset, ins[s].at[1 - core, rows], pair[s].at[rows], sibling(place)
            )
    for s in range(3):
        loads[s].wait()

    def reduce_axis(s, axis, base, size, source, inbox, prepare):
        k = place[axis]
        right, left = shifted(place, axis, 1), shifted(place, axis, 3)
        half = size // 2

        def begin():
            prepare(2)
            start = ((k + 2) % 4) * size
            a = remote(s, base, source.at[pl.ds(start, half)], inbox.at[pl.ds(0, half)], right)
            b = remote(
                s, base + 1, source.at[pl.ds(start + half, half)], inbox.at[pl.ds(half, half)], left
            )
            return a, b

        def middle(pending):
            a, b = pending
            prepare(1)
            start = ((k + 1) % 4) * size
            a.wait_recv()
            add_blocks(source, half, start, lambda i: inbox[i])
            c = remote(
                s, base + 2, source.at[pl.ds(start, size)], inbox.at[pl.ds(size, size)], right
            )
            prepare(3)
            start = ((k + 3) % 4) * size
            b.wait_recv()
            add_blocks(source, half, start + half, lambda i: inbox[half + i])
            d = remote(
                s, base + 3, source.at[pl.ds(start, size)], inbox.at[pl.ds(2 * size, size)], left
            )
            return c, d

        def end(pending):
            c, d = pending
            prepare(0)
            c.wait_recv()
            d.wait_recv()
            add_blocks(
                source, size, k * size, lambda i: inbox[size + i], lambda i: inbox[2 * size + i]
            )

        return begin, middle, end

    def prepare_pair(s):
        def prepare(offset):
            pairs[s, offset].wait_recv()
            start = ((place[ORDERS[s][2]] + offset) % 4) * 16
            add_blocks(own[s], 16, start, lambda i: pair[s][start + i])

        return prepare

    phases = [
        reduce_axis(s, ORDERS[s][2], 4, 16, own[s], far[s], prepare_pair(s)) for s in range(3)
    ]
    state = [phases[s][0]() for s in range(3)]
    state = [phases[s][1](state[s]) for s in range(3)]
    for s in range(3):
        phases[s][2](state[s])
    phases = [
        reduce_axis(
            s,
            ORDERS[s][1],
            8,
            4,
            own[s].at[pl.ds(place[ORDERS[s][2]] * 16, 16)],
            mid[s],
            lambda offset: None,
        )
        for s in range(3)
    ]
    state = [phases[s][0]() for s in range(3)]
    state = [phases[s][1](state[s]) for s in range(3)]
    for s in range(3):
        phases[s][2](state[s])
    last = []
    for s in range(3):
        axis = ORDERS[s][0]
        ka, kb, kc = (place[a] for a in ORDERS[s])
        for step in (1, 3, 2):
            block = own[s].at[kc * 16 + kb * 4 + (ka + step) % 4]
            last.append(remote(s, 11 + step, block, near[s].at[step - 1], shifted(place, axis, step)))
    for s in range(3):
        ka, kb, kc = (place[a] for a in ORDERS[s])
        for copy in last[3 * s : 3 * s + 3]:
            copy.wait_recv()
        value = own[s][kc * 16 + kb * 4 + ka].astype(jnp.float32)
        for step in range(3):
            value = value + near[s][step].astype(jnp.float32)
        outs[s][...] = value
    for copy in sent:
        copy.wait_send()


def scatter_blocks(parts):
    def buffers(count):
        return [pltpu.VMEM((count, rows, 128), jnp.bfloat16) for rows in ROWS]

    return pl.pallas_call(
        scatter_kernel,
        out_shape=[jax.ShapeDtypeStruct((rows, 128), jnp.float32) for rows in ROWS],
        in_specs=[pl.BlockSpec(memory_space=pl.ANY)] * 3,
        out_specs=[pl.BlockSpec(memory_space=pltpu.VMEM)] * 3,
        scratch_shapes=buffers(64)
        + buffers(64)
        + buffers(48)
        + buffers(12)
        + buffers(3)
        + [
            pltpu.SemaphoreType.DMA((3, 15)),
            pltpu.SemaphoreType.DMA((3, 15)),
            pltpu.SemaphoreType.DMA((3,)),
        ],
        compiler_params=pltpu.CompilerParams(
            collective_id=1, has_side_effects=True, vmem_limit_bytes=VMEM_BYTES
        ),
        name="scatter_blocks",
    )(*parts)


def group_member(place, index):
    return (index // 2, place[1], (place[2] // 2) * 2 + index % 2, place[3])


def group_gather_kernel(block, out, send, recv, local):
    place = coords()
    me = lax.axis_index("fsdp")
    partners = [(lax.axis_index("dp"), (me + step) % 8) for step in range(1, 8)]
    keep = pltpu.make_async_copy(block, out.at[me], local)
    keep.start()
    barrier = pltpu.get_barrier_semaphore()
    for partner in partners:
        pl.semaphore_signal(barrier, inc=1, device_id=partner, device_id_type=MESH)
    pl.semaphore_wait(barrier, 7)
    copies = []
    for step in range(7):
        copy = pltpu.make_async_remote_copy(
            src_ref=block,
            dst_ref=out.at[me],
            send_sem=send.at[step],
            recv_sem=recv.at[step],
            device_id=partners[step],
            device_id_type=MESH,
        )
        copy.start()
        copies.append(copy)
    keep.wait()
    for copy in copies:
        copy.wait()


def group_gather(block):
    return pl.pallas_call(
        group_gather_kernel,
        out_shape=jax.ShapeDtypeStruct((8,) + block.shape, block.dtype),
        in_specs=[pl.BlockSpec(memory_space=pl.ANY)],
        out_specs=pl.BlockSpec(memory_space=pl.ANY),
        scratch_shapes=[
            pltpu.SemaphoreType.DMA((7,)),
            pltpu.SemaphoreType.DMA((7,)),
            pltpu.SemaphoreType.DMA,
        ],
        compiler_params=pltpu.CompilerParams(collective_id=2, has_side_effects=True),
        name="group_gather",
    )(block)


def group_scatter_kernel(blocks, out, inbox, send, recv):
    me = lax.axis_index("fsdp")
    partners = [(lax.axis_index("dp"), (me + step) % 8) for step in range(1, 8)]
    barrier = pltpu.get_barrier_semaphore()
    for partner in partners:
        pl.semaphore_signal(barrier, inc=1, device_id=partner, device_id_type=MESH)
    pl.semaphore_wait(barrier, 7)
    copies = []
    for step in range(7):
        copy = pltpu.make_async_remote_copy(
            src_ref=blocks.at[(me + step + 1) % 8],
            dst_ref=inbox.at[step],
            send_sem=send.at[step],
            recv_sem=recv.at[step],
            device_id=partners[step],
            device_id_type=MESH,
        )
        copy.start()
        copies.append(copy)
    out[...] = blocks[me].astype(jnp.float32)
    for step in range(7):
        copies[step].wait_recv()
        out[...] += inbox[step].astype(jnp.float32)
    for copy in copies:
        copy.wait_send()


def group_scatter(blocks):
    rows = blocks.shape[1:]
    return pl.pallas_call(
        group_scatter_kernel,
        out_shape=jax.ShapeDtypeStruct(rows, jnp.float32),
        in_specs=[pl.BlockSpec(memory_space=pltpu.VMEM)],
        out_specs=pl.BlockSpec(memory_space=pltpu.VMEM),
        scratch_shapes=[
            pltpu.VMEM((7,) + rows, blocks.dtype),
            pltpu.SemaphoreType.DMA((7,)),
            pltpu.SemaphoreType.DMA((7,)),
        ],
        compiler_params=pltpu.CompilerParams(
            collective_id=3, has_side_effects=True, vmem_limit_bytes=VMEM_BYTES
        ),
        name="group_scatter",
    )(blocks)


def to_devices(blocks, s):
    rows = blocks.shape[-2]
    where = {ORDERS[s][0]: 3, ORDERS[s][1]: 2, ORDERS[s][2]: 1}
    by_place = blocks.transpose(where[2], where[1], 0, where[0], 4, 5)
    by_place = by_place.reshape(2, 2, 4, 2, 4, rows, 128)
    return by_place.transpose(0, 2, 3, 4, 1, 5, 6).reshape(128, rows, 128)


def from_devices(blocks, s):
    rows = blocks.shape[-2]
    by_place = blocks.reshape(2, 4, 2, 4, 2, rows, 128)
    by_place = by_place.transpose(0, 4, 1, 2, 3, 5, 6).reshape(4, 4, 2, 4, rows, 128)
    where = {2: 0, 1: 1, 0: 3}
    a, b, c = (where[axis] for axis in ORDERS[s])
    return by_place.transpose(2, c, b, a, 4, 5).reshape(2, 64, rows, 128)


def lines(block, rows=None):
    flat = block.reshape(-1)
    count = -(-flat.shape[0] // 128) if rows is None else rows
    return jnp.pad(flat, (0, count * 128 - flat.shape[0])).reshape(count, 128)


def column_lines(block):
    r, columns = block.shape
    return block.reshape(r, columns // 128, 128).transpose(1, 0, 2).reshape(-1, 128)


def column_blocks(blocks, r):
    devices, count, _ = blocks.shape
    n = count // r
    return (
        blocks.reshape(devices, n, r, 128).transpose(0, 2, 1, 3).reshape(devices * r, 128 * n)
    )


def split_columns(matrix, devices):
    r, n = matrix.shape[0] // devices, matrix.shape[1] // 128
    return matrix.reshape(devices, r, n, 128).transpose(0, 2, 1, 3).reshape(devices, n * r, 128)


def gather_weights(shards):
    query, key, value, output, gate, up, down, norm_one, norm_two, head_norm = shards
    vectors = jnp.concatenate([norm_one, norm_two, head_norm])
    parts = (
        jnp.concatenate([lines(gate), lines(query), lines(vectors, 8)]),
        jnp.concatenate([lines(up), lines(key), lines(value), jnp.zeros((12, 128), up.dtype)]),
        jnp.concatenate([column_lines(down), column_lines(output), jnp.zeros((8, 128), up.dtype)]),
    )
    first, second, third = (to_devices(b, s) for s, b in enumerate(gather_blocks(parts)))
    flat = first[:, 120, :]
    return (
        first[:, 80:120].reshape(640, 1024),
        second[:, 80:90].reshape(640, 256),
        second[:, 90:100].reshape(640, 256),
        column_blocks(third[:, 80:120], 8),
        first[:, :80].reshape(640, 2048),
        second[:, :80].reshape(640, 2048),
        column_blocks(third[:, :80], 16),
        flat[:, 0:5].reshape(640),
        flat[:, 5:10].reshape(640),
        flat[:, 10:14].reshape(512),
    )


def scatter_gradients(grads):
    query, key, value, output, gate, up, down, norm_one, norm_two, head_norm = (
        grad.astype(jnp.bfloat16) for grad in grads
    )
    vectors = jnp.concatenate(
        [norm_one.reshape(128, 5), norm_two.reshape(128, 5), head_norm.reshape(128, 4)], axis=1
    )
    vectors = jnp.pad(vectors, ((0, 0), (0, 114)))[:, None, :]
    parts = (
        jnp.concatenate(
            [
                gate.reshape(128, 80, 128),
                query.reshape(128, 40, 128),
                vectors,
                jnp.zeros((128, 7, 128), jnp.bfloat16),
            ],
            axis=1,
        ),
        jnp.concatenate(
            [
                up.reshape(128, 80, 128),
                key.reshape(128, 10, 128),
                value.reshape(128, 10, 128),
                jnp.zeros((128, 12, 128), jnp.bfloat16),
            ],
            axis=1,
        ),
        jnp.concatenate(
            [
                split_columns(down, 128),
                split_columns(output, 128),
                jnp.zeros((128, 8, 128), jnp.bfloat16),
            ],
            axis=1,
        ),
    )
    first, second, third = scatter_blocks([from_devices(p, s) for s, p in enumerate(parts)])
    flat = first[120]
    return (
        first[80:120].reshape(5, 1024),
        second[80:90].reshape(5, 256),
        second[90:100].reshape(5, 256),
        column_blocks(third[None, 80:120], 8),
        first[:80].reshape(5, 2048),
        second[:80].reshape(5, 2048),
        column_blocks(third[None, :80], 16),
        flat[0:5],
        flat[5:10],
        flat[10:14],
    )

eps_norm = 1e-05
rope_base = 1000000.0
neg_large = -1e30


def rms_scale(values):
    return lax.rsqrt(jnp.mean(values * values, axis=-1, keepdims=True) + eps_norm)


def gelu_tanh(values):
    return jax.nn.gelu(values, approximate=True)


def rope_tables(positions):
    half_dim = HD // 2
    exponents = jnp.arange(half_dim, dtype=jnp.float32) * (2.0 / HD)
    frequencies = jnp.exp(-exponents * math.log(rope_base))
    angles = positions.astype(jnp.float32)[:, None] * frequencies[None, :]
    return (jnp.cos(angles)[:, None, :], jnp.sin(angles)[:, None, :])


def rotate(values, cosines, sine_table):
    half_dim = HD // 2
    first_half = values[..., :half_dim]
    second = values[..., half_dim:]
    return jnp.concatenate(
        [first_half * cosines - second * sine_table, second * cosines + first_half * sine_table],
        axis=-1,
    )


def rotate_back(grads, cosines, sine_table):
    half_dim = HD // 2
    first_half = grads[..., :half_dim]
    second = grads[..., half_dim:]
    return jnp.concatenate(
        [first_half * cosines + second * sine_table, second * cosines - first_half * sine_table],
        axis=-1,
    )


def seg_start(token_ids, seq_lengths):
    seq_ends = jnp.cumsum(seq_lengths)
    past_end = (token_ids[:, None] >= seq_ends[None, :]).astype(jnp.int32)
    segment = jnp.sum(past_end, axis=1)
    seq_start = jnp.sum(past_end * seq_lengths[None, :], axis=1)
    return (segment, token_ids - seq_start)


def norm_back(grad_normed, raw_values, inverse_rms, gain_values, gain_axes):
    scaled = grad_normed * gain_values
    raw_grad = inverse_rms * scaled - raw_values * inverse_rms**3 * jnp.mean(
        scaled * raw_values, axis=-1, keepdims=True
    )
    gain_grad = jnp.sum(grad_normed * raw_values * inverse_rms, axis=gain_axes)
    return (raw_grad, gain_grad)


def contract_rows(left, right):
    return lax.dot_general(
        left, right, (((0,), (0,)), ((), ())), preferred_element_type=jnp.float32
    )


def times_transposed(left, right):
    return lax.dot_general(
        left, right, (((1,), (1,)), ((), ())), preferred_element_type=jnp.float32
    )


def body(
    tokens,
    w_query,
    w_key,
    w_value,
    w_out,
    w_gate,
    w_up,
    w_down,
    attn_gain,
    ffn_gain,
    head_gains,
    lengths,
    cotangent,
):
    shards = (w_query, w_key, w_value, w_out, w_gate, w_up, w_down, attn_gain, ffn_gain, head_gains)
    weights = gather_weights(shards)
    (
        query_mat,
        key_mat,
        value_mat,
        output_mat,
        gate_mat,
        up_mat,
        down_mat,
        norm_one,
        norm_two,
        head_norm,
    ) = weights
    tok_rows = tokens.shape[0]
    group_size = lax.axis_size("fsdp")
    member = lax.axis_index("fsdp")
    group_rows = tok_rows * group_size
    group_ratio = H // KV
    score_scale = 1.0 / math.sqrt(HD)
    seq_lengths = lengths[0]
    local_ids = member * tok_rows + jnp.arange(tok_rows, dtype=jnp.int32)
    local_seg, local_pos = seg_start(local_ids, seq_lengths)
    cosines, sine_table = rope_tables(local_pos)
    inputs = tokens.astype(jnp.float32)
    gain_one = norm_one.astype(jnp.float32)
    gain_two = norm_two.astype(jnp.float32)
    gain_heads = head_norm.astype(jnp.float32)
    scale_one = rms_scale(inputs)
    normed = (inputs * scale_one * gain_one).astype(jnp.bfloat16)
    query_raw = jnp.dot(normed, query_mat, preferred_element_type=jnp.float32).reshape(
        tok_rows, H, HD
    )
    key_raw = jnp.dot(normed, key_mat, preferred_element_type=jnp.float32).reshape(tok_rows, KV, HD)
    value_flat = jnp.dot(normed, value_mat, preferred_element_type=jnp.float32).astype(jnp.bfloat16)
    query_scale = rms_scale(query_raw)
    key_scale = rms_scale(key_raw)
    query_rot = rotate(query_raw * query_scale * gain_heads[:HD], cosines, sine_table).astype(
        jnp.bfloat16
    )
    key_rot = rotate(key_raw * key_scale * gain_heads[HD:], cosines, sine_table).astype(
        jnp.bfloat16
    )
    queries = query_rot.reshape(tok_rows, KV, group_ratio, HD).transpose(1, 2, 0, 3)
    key_flat = key_rot.reshape(tok_rows, KV * HD)

    def masked_scores(key_piece, first_key):
        key_count = key_piece.shape[0]
        key_ids = first_key + jnp.arange(key_count, dtype=jnp.int32)
        key_seg, unused = seg_start(key_ids, seq_lengths)
        allowed = (local_seg[:, None] == key_seg[None, :]) & (
            key_ids[None, :] <= local_ids[:, None]
        )
        scores = (
            jnp.einsum(
                "kgqd,nkd->kgqn",
                queries,
                key_piece.reshape(key_count, KV, HD),
                preferred_element_type=jnp.float32,
            )
            * score_scale
        )
        return (jnp.where(allowed, scores, neg_large), allowed)

    run_max = jnp.full((KV, group_ratio, tok_rows), neg_large, jnp.float32)
    group_kv = group_gather(jnp.concatenate([key_flat, value_flat], axis=1))
    group_kv = group_kv.reshape(group_rows, 2 * KV * HD)
    key_piece, value_piece = group_kv[:, : KV * HD], group_kv[:, KV * HD :]
    key_count = key_piece.shape[0]
    scores, allowed = masked_scores(key_piece, jnp.int32(0))
    new_max = jnp.maximum(run_max, jnp.max(scores, axis=-1))
    softmax_rows = jnp.where(allowed, jnp.exp(scores - new_max[..., None]), 0.0)
    run_total = jnp.sum(softmax_rows, axis=-1)
    run_acc = jnp.einsum(
        "kgqn,nkd->kgqd",
        softmax_rows.astype(jnp.bfloat16),
        value_piece.reshape(key_count, KV, HD),
        preferred_element_type=jnp.float32,
    )
    run_max, run_total, run_acc = (new_max, run_total, run_acc)
    attended = run_acc / run_total[..., None]
    log_sum = run_max + jnp.log(run_total)
    attended_low = attended.transpose(2, 0, 1, 3).reshape(tok_rows, H * HD).astype(jnp.bfloat16)
    middle = inputs + jnp.dot(attended_low, output_mat, preferred_element_type=jnp.float32)
    scale_two = rms_scale(middle)
    ffn_in = (middle * scale_two * gain_two).astype(jnp.bfloat16)
    gate_pre = jnp.dot(ffn_in, gate_mat, preferred_element_type=jnp.float32)
    up_pre = jnp.dot(ffn_in, up_mat, preferred_element_type=jnp.float32)
    gate_act, gate_pullback = jax.vjp(gelu_tanh, gate_pre)
    hidden = (gate_act * up_pre).astype(jnp.bfloat16)
    block_out = (middle + jnp.dot(hidden, down_mat, preferred_element_type=jnp.float32)).astype(
        jnp.bfloat16
    )
    grad_down = contract_rows(hidden, cotangent)
    d_hidden = times_transposed(cotangent, down_mat)
    d_gate = gate_pullback(d_hidden * up_pre)[0].astype(jnp.bfloat16)
    d_up = (d_hidden * gate_act).astype(jnp.bfloat16)
    grad_gate = contract_rows(ffn_in, d_gate)
    grad_up = contract_rows(ffn_in, d_up)
    d_ffn = times_transposed(d_gate, gate_mat) + times_transposed(d_up, up_mat)
    d_norm_two, grad_two = norm_back(d_ffn, middle, scale_two, gain_two, (0,))
    d_middle = cotangent.astype(jnp.float32) + d_norm_two
    d_branch = d_middle.astype(jnp.bfloat16)
    grad_output = contract_rows(attended_low, d_branch)
    d_attended = (
        times_transposed(d_branch, output_mat)
        .astype(jnp.bfloat16)
        .reshape(tok_rows, KV, group_ratio, HD)
        .transpose(1, 2, 0, 3)
    )
    deltas = jnp.sum(d_attended.astype(jnp.float32) * attended, axis=-1)
    key_all, value_all = key_piece, value_piece
    key_block = math.gcd(group_rows, 512)
    block_count = group_rows // key_block
    key_blocks = key_all.reshape(block_count, key_block, KV * HD)
    value_blocks = value_all.reshape(block_count, key_block, KV * HD)
    block_firsts = jnp.arange(block_count, dtype=jnp.int32) * key_block

    def back_block(grad_queries, block_item):
        key_piece, value_piece, first_key = block_item
        scores, allowed = masked_scores(key_piece, first_key)
        softmax_rows = jnp.where(allowed, jnp.exp(scores - log_sum[..., None]), 0.0)
        key_three = key_piece.reshape(key_block, KV, HD)
        d_probs = jnp.einsum(
            "kgqd,nkd->kgqn",
            d_attended,
            value_piece.reshape(key_block, KV, HD),
            preferred_element_type=jnp.float32,
        )
        d_scores = (softmax_rows * (d_probs - deltas[..., None])).astype(jnp.bfloat16)
        grad_queries = (
            grad_queries
            + jnp.einsum("kgqn,nkd->kgqd", d_scores, key_three, preferred_element_type=jnp.float32)
            * score_scale
        )
        d_keys = (
            jnp.einsum("kgqn,kgqd->nkd", d_scores, queries, preferred_element_type=jnp.float32)
            * score_scale
        )
        d_values = jnp.einsum(
            "kgqn,kgqd->nkd",
            softmax_rows.astype(jnp.bfloat16),
            d_attended,
            preferred_element_type=jnp.float32,
        )
        return (
            grad_queries,
            jnp.concatenate(
                [d_keys.reshape(key_block, KV * HD), d_values.reshape(key_block, KV * HD)], axis=-1
            ),
        )

    grad_queries, kv_terms = lax.scan(
        back_block,
        jnp.zeros((KV, group_ratio, tok_rows, HD), jnp.float32),
        (key_blocks, value_blocks, block_firsts),
    )
    kv_sums = group_scatter(
        kv_terms.reshape(group_size, tok_rows, 2 * KV * HD).astype(jnp.bfloat16)
    )
    d_query_rot = grad_queries.transpose(2, 0, 1, 3).reshape(tok_rows, H, HD)
    d_query_raw, grad_query_gain = norm_back(
        rotate_back(d_query_rot, cosines, sine_table),
        query_raw,
        query_scale,
        gain_heads[:HD],
        (0, 1),
    )
    d_key_rot = kv_sums[:, : KV * HD].reshape(tok_rows, KV, HD)
    d_key_raw, grad_key_gain = norm_back(
        rotate_back(d_key_rot, cosines, sine_table), key_raw, key_scale, gain_heads[HD:], (0, 1)
    )
    d_query_low = d_query_raw.reshape(tok_rows, H * HD).astype(jnp.bfloat16)
    d_key_low = d_key_raw.reshape(tok_rows, KV * HD).astype(jnp.bfloat16)
    d_value_low = kv_sums[:, KV * HD :].astype(jnp.bfloat16)
    grad_query_mat = contract_rows(normed, d_query_low)
    grad_key_mat = contract_rows(normed, d_key_low)
    grad_value_mat = contract_rows(normed, d_value_low)
    d_normed = (
        times_transposed(d_query_low, query_mat)
        + times_transposed(d_key_low, key_mat)
        + times_transposed(d_value_low, value_mat)
    )
    d_norm_one, grad_one = norm_back(d_normed, inputs, scale_one, gain_one, (0,))
    input_grad = d_middle + d_norm_one
    grad_heads = jnp.concatenate([grad_query_gain, grad_key_gain])
    all_sums = scatter_gradients(
        (
            grad_query_mat,
            grad_key_mat,
            grad_value_mat,
            grad_output,
            grad_gate,
            grad_up,
            grad_down,
            grad_one,
            grad_two,
            grad_heads,
        )
    )
    (
        sum_query,
        sum_key,
        sum_value,
        sum_output,
        sum_gate,
        sum_up,
        sum_down,
        sum_one,
        sum_two,
        sum_heads,
    ) = all_sums
    return (
        block_out,
        input_grad,
        sum_query,
        sum_key,
        sum_value,
        sum_output,
        sum_gate,
        sum_up,
        sum_down,
        sum_one,
        sum_two,
        sum_heads,
    )


def solution(mesh):
    in_specs = (
        P(("dp", "fsdp"), None),
        P(("dp", "fsdp"), None),
        P(("dp", "fsdp"), None),
        P(("dp", "fsdp"), None),
        P(("dp", "fsdp"), None),
        P(("dp", "fsdp"), None),
        P(("dp", "fsdp"), None),
        P(("dp", "fsdp"), None),
        P(("dp", "fsdp")),
        P(("dp", "fsdp")),
        P(("dp", "fsdp")),
        P("dp", None),
        P(("dp", "fsdp"), None),
    )
    out_specs = (
        P(("dp", "fsdp"), None),
        P(("dp", "fsdp"), None),
        P(("dp", "fsdp"), None),
        P(("dp", "fsdp"), None),
        P(("dp", "fsdp"), None),
        P(("dp", "fsdp"), None),
        P(("dp", "fsdp"), None),
        P(("dp", "fsdp"), None),
        P(("dp", "fsdp"), None),
        P(("dp", "fsdp")),
        P(("dp", "fsdp")),
        P(("dp", "fsdp")),
    )
    return jax.shard_map(body, mesh=mesh, in_specs=in_specs, out_specs=out_specs, check_vma=False)
```

```python
import math

import jax
import jax.numpy as jnp
from jax import lax
from jax.experimental import pallas as pl
from jax.experimental.pallas import tpu as pltpu
from jax.sharding import PartitionSpec as P

H = 4
HD = 256
D = 640
FF = 2048
TOK = 128
GROUP = 8
KEYS = TOK * GROUP
EPS = 1e-05
ROPE_BASE = 1000000.0
NEG = -1e30
SCORE_SCALE = 1.0 / math.sqrt(HD)
F32 = jnp.float32
BF16 = jnp.bfloat16

MESH = pl.DeviceIdType.MESH
VMEM_BYTES = 60 * 1024 * 1024

ORDERS = ((0, 1, 2), (1, 2, 0), (2, 0, 1))
ROWS = ((48, 32, 48), (80, 80, 80))
GAIN_ROW = 40


def coords():
    dp = lax.axis_index("dp")
    fsdp = lax.axis_index("fsdp")
    return (fsdp // 2, (dp // 2) % 4, (dp // 8) * 2 + fsdp % 2, dp % 2)


def device(place):
    x, y, z, core = place
    return ((z // 2) * 8 + y * 2 + core, x * 2 + z % 2)


def shifted(place, axis, step):
    moved = list(place)
    moved[axis] = (place[axis] + step) % 4
    return tuple(moved)


def sibling(place):
    return place[:3] + (1 - place[3],)


def group_partner(step):
    return (lax.axis_index("dp"), (lax.axis_index("fsdp") + step) % GROUP)


def meet(place):
    partners = [device(shifted(place, axis, step)) for axis in range(3) for step in (1, 2, 3)]
    partners.append(device(sibling(place)))
    x, y, z, core = place
    flipped = (x, y, (z // 2) * 2 + (1 - z % 2), core)
    partners += [device(shifted(flipped, 0, step)) for step in (1, 2, 3)]
    barrier = pltpu.get_barrier_semaphore()
    for partner in partners:
        pl.semaphore_signal(barrier, inc=1, device_id=partner, device_id_type=MESH)
    pl.semaphore_wait(barrier, len(partners))


def remote(src, dst, send, recv, to):
    copy = pltpu.make_async_remote_copy(
        src_ref=src, dst_ref=dst, send_sem=send, recv_sem=recv, device_id=to, device_id_type=MESH
    )
    copy.start()
    return copy


class Gather:
    def __init__(self, place, bufs, send, recv):
        self.place, self.bufs, self.send, self.recv = place, bufs, send, recv
        self.sent, self.pair = [], []
        self.kept = [None] * 3

    def copy(self, s, slot, ref, to, keep=None):
        copy = remote(ref, ref, self.send.at[s, slot], self.recv.at[s, slot], device(to))
        (self.sent if keep is None else keep).append(copy)
        return copy

    def at(self, s):
        return tuple(self.place[axis] for axis in ORDERS[s])

    def blocks(self, s, first, count):
        return self.bufs[s].at[self.place[3], pl.ds(first, count)]

    def own(self):
        for s in range(3):
            ka, kb, kc = self.at(s)
            ref = self.blocks(s, kc * 16 + kb * 4 + ka, 1)
            axis = ORDERS[s][0]
            self.kept[s] = [
                self.copy(s, step - 1, ref, shifted(self.place, axis, step)) for step in (1, 3, 2)
            ]

    def to_both(self, s, slot, axis, ref):
        return [
            self.copy(s, slot, ref, shifted(self.place, axis, 1)),
            self.copy(s, slot + 1, ref, shifted(self.place, axis, 3)),
        ]

    def second(self):
        for s in range(3):
            for copy in self.kept[s]:
                copy.wait_recv()
            ka, kb, kc = self.at(s)
            self.kept[s] = self.to_both(s, 3, ORDERS[s][1], self.blocks(s, kc * 16 + kb * 4, 4))

    def second_on(self):
        for s in range(3):
            ka, kb, kc = self.at(s)
            axis = ORDERS[s][1]
            from_left, from_right = self.kept[s]
            from_left.wait_recv()
            right = self.copy(
                s, 5, self.blocks(s, kc * 16 + (kb + 3) % 4 * 4, 2), shifted(self.place, axis, 1)
            )
            from_right.wait_recv()
            left = self.copy(
                s,
                6,
                self.blocks(s, kc * 16 + (kb + 1) % 4 * 4 + 2, 2),
                shifted(self.place, axis, 3),
            )
            self.kept[s] = [right, left]

    def third(self):
        for s in range(3):
            for copy in self.kept[s]:
                copy.wait_recv()
            ka, kb, kc = self.at(s)
            ref = self.blocks(s, kc * 16, 16)
            self.kept[s] = self.to_both(s, 7, ORDERS[s][2], ref)
            self.copy(s, 11, ref, sibling(self.place), self.pair)

    def third_on(self):
        for s in range(3):
            ka, kb, kc = self.at(s)
            axis = ORDERS[s][2]
            from_left, from_right = self.kept[s]
            from_left.wait_recv()
            start = (kc + 3) % 4 * 16
            right = self.copy(s, 9, self.blocks(s, start, 8), shifted(self.place, axis, 1))
            self.copy(s, 12, self.blocks(s, start, 16), sibling(self.place), self.pair)
            from_right.wait_recv()
            start = (kc + 1) % 4 * 16
            left = self.copy(s, 10, self.blocks(s, start + 8, 8), shifted(self.place, axis, 3))
            self.copy(s, 13, self.blocks(s, start, 16), sibling(self.place), self.pair)
            self.kept[s] = [right, left]

    def last(self):
        for s in range(3):
            ka, kb, kc = self.at(s)
            for half in range(2):
                self.kept[s][half].wait_recv()
                ref = self.blocks(s, (kc + 2) % 4 * 16 + 8 * half, 8)
                self.copy(s, 14 + half, ref, sibling(self.place), self.pair)

    def finish(self):
        for copy in self.pair:
            copy.wait()
        for copy in self.sent:
            copy.wait_send()


def add_blocks(total, count, first, other):
    def step(i, carry):
        total[first + i] = total[first + i] + other(i)
        return carry

    lax.fori_loop(0, count, step, 0, unroll=4)


def add_two(total, count, first, one, two):
    def step(i, carry):
        value = total[first + i].astype(F32) + one(i).astype(F32) + two(i).astype(F32)
        total[first + i] = value.astype(BF16)
        return carry

    lax.fori_loop(0, count, step, 0, unroll=4)


class Scatter:
    def __init__(self, place, bufs, pair, far, mid, near, outs, send, recv):
        self.place, self.bufs, self.pair_in = place, bufs, pair
        self.far_in, self.mid_in, self.near_in, self.outs = far, mid, near, outs
        self.send, self.recv = send, recv
        self.sent, self.pairs = [], {}
        self.kept = [None] * 3

    def copy(self, s, slot, src, dst, to):
        copy = remote(src, dst, self.send.at[s, slot], self.recv.at[s, slot], device(to))
        self.sent.append(copy)
        return copy

    def at(self, s):
        return tuple(self.place[axis] for axis in ORDERS[s])

    def own(self, s):
        return self.bufs[s].at[self.place[3]]

    def to_pair(self, streams=(0, 1, 2)):
        core = self.place[3]
        for offset in (2, 1, 3, 0):
            for s in streams:
                rows = pl.ds((self.at(s)[2] + offset) % 4 * 16, 16)
                self.pairs[s, offset] = self.copy(
                    s,
                    offset,
                    self.bufs[s].at[1 - core, rows],
                    self.pair_in[s].at[rows],
                    sibling(self.place),
                )

    def add_pair(self, s, offset):
        self.pairs[s, offset].wait_recv()
        start = (self.at(s)[2] + offset) % 4 * 16
        pair = self.pair_in[s]
        add_blocks(self.own(s), 16, start, lambda i: pair[start + i])

    def level(self, s, far):
        ka, kb, kc = self.at(s)
        if far:
            return ORDERS[s][2], kc, 0, 16, 4, self.far_in[s]
        return ORDERS[s][1], kb, kc * 16, 4, 8, self.mid_in[s]

    def begin(self, far):
        for s in range(3):
            axis, k, base, size, slot, inbox = self.level(s, far)
            half = size // 2
            if far:
                self.add_pair(s, 2)
            start = base + (k + 2) % 4 * size
            own = self.own(s)
            self.kept[s] = (
                self.copy(
                    s,
                    slot,
                    own.at[pl.ds(start, half)],
                    inbox.at[pl.ds(0, half)],
                    shifted(self.place, axis, 1),
                ),
                self.copy(
                    s,
                    slot + 1,
                    own.at[pl.ds(start + half, half)],
                    inbox.at[pl.ds(half, half)],
                    shifted(self.place, axis, 3),
                ),
            )

    def middle(self, far):
        for s in range(3):
            axis, k, base, size, slot, inbox = self.level(s, far)
            half = size // 2
            own = self.own(s)
            if far:
                self.add_pair(s, 1)
            start = base + (k + 1) % 4 * size
            self.kept[s][0].wait_recv()
            add_blocks(own, half, start, lambda i: inbox[i])
            right = self.copy(
                s,
                slot + 2,
                own.at[pl.ds(start, size)],
                inbox.at[pl.ds(size, size)],
                shifted(self.place, axis, 1),
            )
            if far:
                self.add_pair(s, 3)
            start = base + (k + 3) % 4 * size
            self.kept[s][1].wait_recv()
            add_blocks(own, half, start + half, lambda i: inbox[half + i])
            left = self.copy(
                s,
                slot + 3,
                own.at[pl.ds(start, size)],
                inbox.at[pl.ds(2 * size, size)],
                shifted(self.place, axis, 3),
            )
            self.kept[s] = (right, left)

    def end(self, far):
        for s in range(3):
            axis, k, base, size, slot, inbox = self.level(s, far)
            if far:
                self.add_pair(s, 0)
            for copy in self.kept[s]:
                copy.wait_recv()
            add_two(
                self.own(s),
                size,
                base + k * size,
                lambda i: inbox[size + i],
                lambda i: inbox[2 * size + i],
            )

    def to_owners(self):
        for s in range(3):
            ka, kb, kc = self.at(s)
            axis = ORDERS[s][0]
            own = self.own(s)
            self.kept[s] = [
                self.copy(
                    s,
                    11 + step,
                    own.at[kc * 16 + kb * 4 + (ka + step) % 4],
                    self.near_in[s].at[step - 1],
                    shifted(self.place, axis, step),
                )
                for step in (1, 3, 2)
            ]

    def finish(self):
        for s in range(3):
            ka, kb, kc = self.at(s)
            for copy in self.kept[s]:
                copy.wait_recv()
            value = self.own(s)[kc * 16 + kb * 4 + ka].astype(F32)
            for step in range(3):
                value = value + self.near_in[s][step].astype(F32)
            self.outs[s][...] = value
        for copy in self.sent:
            copy.wait_send()


def one_hot(rows, columns, pick):
    i = lax.broadcasted_iota(jnp.int32, (rows, columns), 0)
    j = lax.broadcasted_iota(jnp.int32, (rows, columns), 1)
    return jnp.where(pick(i) == j, 1.0, 0.0)


def dot(left, right):
    return jnp.dot(left, right, preferred_element_type=F32)


def dot_nt(left, right):
    return lax.dot_general(left, right, (((1,), (1,)), ((), ())), preferred_element_type=F32)


def dot_tn(left, right):
    return lax.dot_general(left, right, (((0,), (0,)), ((), ())), preferred_element_type=F32)


def stack_columns(shard):
    r, columns = shard.shape
    value = shard.astype(F32)
    pad = [jnp.zeros((8 - r, 128), F32)] if r < 8 else []
    pieces = []
    for c in range(columns // 128):
        pieces += [value[:, c * 128 : (c + 1) * 128]] + pad
    return jnp.concatenate(pieces, axis=0)


def row_order(rows, n):
    shift = n.bit_length() - 1
    return one_hot(rows, 8 * n, lambda i: jnp.where(i < 5 * n, (i & (n - 1)) * 8 + (i >> shift), -1))


def block_index(s, g, d):
    z_hi, y = g // 4, g % 4
    core, x, z_lo = d // 8, (d // 2) % 4, d % 2
    place = (x, y, z_hi * 2 + z_lo)
    a, b, c = (place[axis] for axis in ORDERS[s])
    return core, c * 16 + b * 4 + a


def rms(value):
    return lax.rsqrt(jnp.mean(value * value, axis=-1, keepdims=True) + EPS)


def rotate(value, cosines, sines):
    half = HD // 2
    u, w = value[:, :half], value[:, half:]
    return jnp.concatenate([u * cosines - w * sines, w * cosines + u * sines], axis=1)


def norm_back(grad, value, scale, gain):
    scaled = grad * gain
    back = scale * scaled - value * scale**3 * jnp.mean(scaled * value, axis=-1, keepdims=True)
    return back, jnp.sum(grad * value * scale, axis=0, keepdims=True)


def split_dot_nt(value, matrix):
    high = value.astype(BF16)
    low = (value - high.astype(F32)).astype(BF16)
    return dot_nt(high, matrix) + dot_nt(low, matrix)


def block_kernel(
    tokens,
    cotangent,
    lengths,
    w_query,
    w_key,
    w_value,
    w_out,
    w_gate,
    w_up,
    w_down,
    gains,
    block_out,
    input_grad,
    sum_a0,
    sum_a1,
    sum_a2,
    sum_b0,
    sum_b1,
    sum_b2,
    a0,
    a1,
    a2,
    b0,
    b1,
    b2,
    *scratch,
):
    it = iter(scratch)

    def take(count):
        return [next(it) for _ in range(count)]

    pair_a, pair_b = take(3), take(3)
    far_a, far_b = take(3), take(3)
    mid_a, mid_b = take(3), take(3)
    near_a, near_b = take(3), take(3)
    q_mat, kv_mat, o_mat, g_mat, u_mat, d_mat = take(6)
    perm, flip, pick, gain_cols, gain_rows = take(5)
    cos_ref, sin_ref, allowed_ref = take(3)
    normed, ffn_in, middle = take(3)
    q_raw, kv_raw, queries, kv_all = take(4)
    probs, attended, attended_low, d_attended, d_scores = take(5)
    hidden, d_gate, d_up, d_acc = take(4)
    d_kv, kv_in, d_q_low, d_kv_low = take(4)
    gather_send, gather_recv, scatter_send, scatter_recv = take(4)
    kv_send, kv_recv, dkv_send, dkv_recv = take(4)

    place = coords()
    core = place[3]
    me = lax.axis_index("fsdp")
    bufs_a, bufs_b = (a0, a1, a2), (b0, b1, b2)

    def own_ref(bufs, s):
        ka, kb, kc = (place[axis] for axis in ORDERS[s])
        return bufs[s].at[core, kc * 16 + kb * 4 + ka]

    packed = dot(row_order(48, 8).astype(BF16), stack_columns(w_query[...]).astype(BF16))
    packed = jnp.concatenate([packed[:GAIN_ROW], gains[...]], axis=0)
    own_ref(bufs_a, 0)[...] = packed.astype(BF16)
    both = jnp.concatenate([stack_columns(w_key[...]), stack_columns(w_value[...])], axis=0)
    own_ref(bufs_a, 1)[...] = dot(row_order(32, 4).astype(BF16), both.astype(BF16)).astype(BF16)
    packed = jnp.concatenate([stack_columns(w_out[...]), jnp.zeros((8, 128), F32)], axis=0)
    own_ref(bufs_a, 2)[...] = packed.astype(BF16)
    order = row_order(80, 16).astype(BF16)
    own_ref(bufs_b, 0)[...] = dot(order, stack_columns(w_gate[...]).astype(BF16)).astype(BF16)
    own_ref(bufs_b, 1)[...] = dot(order, stack_columns(w_up[...]).astype(BF16)).astype(BF16)
    down = w_down[...]
    own_ref(bufs_b, 2)[...] = jnp.concatenate(
        [down[:, c * 128 : (c + 1) * 128] for c in range(5)], axis=0
    )

    meet(place)
    ga = Gather(place, bufs_a, gather_send.at[0], gather_recv.at[0])
    gb = Gather(place, bufs_b, gather_send.at[1], gather_recv.at[1])
    sa = Scatter(
        place,
        bufs_a,
        pair_a,
        far_a,
        mid_a,
        near_a,
        (sum_a0, sum_a1, sum_a2),
        scatter_send.at[0],
        scatter_recv.at[0],
    )
    sb = Scatter(
        place,
        bufs_b,
        pair_b,
        far_b,
        mid_b,
        near_b,
        (sum_b0, sum_b1, sum_b2),
        scatter_send.at[1],
        scatter_recv.at[1],
    )

    ga.own()
    gb.own()

    perm[...] = one_hot(256, 256, lambda i: (i & 15) * 16 + (i >> 4)).astype(BF16)
    flip[...] = one_hot(
        256, 256, lambda i: ((i & 127) >> 3) * 16 + (i >> 7) * 8 + (i & 7)
    ).astype(BF16)
    row = lax.broadcasted_iota(jnp.int32, (D, D), 0)
    column = lax.broadcasted_iota(jnp.int32, (D, D), 1)
    pick[...] = jnp.where(row == 5 * (column & 127) + (column >> 7), 1.0, 0.0).astype(BF16)
    ga.second()
    first_len, second_len = lengths[0, 0], lengths[0, 1]
    first_end, second_end = first_len, first_len + second_len

    def segment(ids):
        past_one = jnp.where(ids >= first_end, 1, 0)
        past_two = jnp.where(ids >= second_end, 1, 0)
        return past_one + past_two, ids - past_one * first_len - past_two * second_len

    ids = me * TOK + lax.broadcasted_iota(jnp.int32, (TOK, HD // 2), 0)
    lane = lax.broadcasted_iota(jnp.int32, (TOK, HD // 2), 1).astype(F32)
    angles = segment(ids)[1].astype(F32) * jnp.exp(lane * (2.0 / HD) * (-math.log(ROPE_BASE)))
    cos_ref[...] = jnp.cos(angles)
    sin_ref[...] = jnp.sin(angles)
    ga.second_on()
    row_ids = me * TOK + lax.broadcasted_iota(jnp.int32, (TOK, KEYS), 0)
    key_ids = lax.broadcasted_iota(jnp.int32, (TOK, KEYS), 1)
    same = segment(row_ids)[0] == segment(key_ids)[0]
    allowed_ref[...] = jnp.where(same & (key_ids <= row_ids), 1.0, 0.0)
    ga.third()
    gb.second()
    inputs = tokens[...].astype(F32)
    scale_one = rms(inputs)
    ga.third_on()
    ga.last()
    gb.second_on()
    ga.finish()

    def slab(bufs, s, g, j):
        tiles = []
        for d in range(16):
            c, index = block_index(s, g, d)
            tiles.append(bufs[s][c, index, pl.ds(j * 16, 16), :])
        return jnp.concatenate(tiles, axis=0)

    def turn(matrix, parts):
        out = dot(matrix, jnp.concatenate(parts, axis=1)).astype(BF16)
        return [out[:, i * 128 : (i + 1) * 128] for i in range(len(parts))]

    def tiles_wide(block, first, count):
        return jnp.concatenate(
            [block[(first + i) * 16 : (first + i + 1) * 16] for i in range(count)], axis=1
        )

    def unpack_a(g, carry):
        at = pl.ds(pl.multiple_of(g * 16, 16), 16)

        def rows(r):
            return pl.ds(pl.multiple_of(r * 128 + g * 16, 16), 16)

        q0, q1 = turn(perm[...], [slab(bufs_a, 0, g, 0), slab(bufs_a, 0, g, 1)])
        q2, kv0 = turn(perm[...], [slab(bufs_a, 0, g, 2), slab(bufs_a, 1, g, 0)])
        (kv1,) = turn(perm[...], [slab(bufs_a, 1, g, 1)])
        for r, (block, first) in enumerate(((q0, 0), (q0, 8), (q1, 0), (q1, 8), (q2, 0))):
            q_mat[rows(r), :] = tiles_wide(block, first, 8)
        gain_cols[at, :] = q2[8 * 16 : 9 * 16].astype(F32)
        for r in range(4):
            kv_mat[rows(r), :] = tiles_wide(kv0, 4 * r, 4)
        kv_mat[rows(4), :] = tiles_wide(kv1, 0, 4)
        return carry

    lax.fori_loop(0, 8, unpack_a, 0)

    def unpack_out(g, carry):
        o0, o1 = turn(flip[...], [slab(bufs_a, 2, g, 0), slab(bufs_a, 2, g, 1)])
        (o2,) = turn(flip[...], [slab(bufs_a, 2, g, 2)])
        o_mat[pl.ds(pl.multiple_of(g * 128, 128), 128), :] = jnp.concatenate(
            [o0[:128], o0[128:], o1[:128], o1[128:], o2[:128]], axis=1
        )
        return carry

    turned = gain_cols[...].T

    def natural(first, count):
        spread = jnp.concatenate([turned[first + i : first + i + 1] for i in range(count)], axis=1)
        return spread.astype(BF16)

    gain_rows[0:1, :] = dot_nt(natural(0, 5), pick[...])
    gain_rows[1:2, :] = dot_nt(natural(5, 5), pick[...])
    head_row = lax.broadcasted_iota(jnp.int32, (512, 512), 0)
    head_column = lax.broadcasted_iota(jnp.int32, (512, 512), 1)
    head_pick = jnp.where(
        head_row == 4 * (head_column & 127) + (head_column >> 7), 1.0, 0.0
    ).astype(BF16)
    gain_rows[2:3, 0:512] = dot_nt(natural(10, 4), head_pick)

    normed_nat = (inputs * scale_one * gain_rows[0:1, :]).astype(BF16)
    normed[...] = dot(normed_nat, pick[...]).astype(BF16)
    kv_raw[...] = dot(normed[...], kv_mat[...])
    key_gain = gain_rows[2:3, HD : 2 * HD]
    query_gain = gain_rows[2:3, 0:HD]
    cosines, sines = cos_ref[...], sin_ref[...]
    key_raw = kv_raw[:, 0:HD]
    key_rot = rotate(key_raw * rms(key_raw) * key_gain, cosines, sines)
    mine = pl.ds(pl.multiple_of(me * TOK, TOK), TOK)
    kv_all[mine, :] = jnp.concatenate([key_rot, kv_raw[:, HD:]], axis=1).astype(BF16)
    kv_copies = [
        remote(
            kv_all.at[mine],
            kv_all.at[mine],
            kv_send.at[step - 1],
            kv_recv.at[step - 1],
            group_partner(step),
        )
        for step in range(1, GROUP)
    ]
    gb.third()
    q_raw[...] = dot(normed[...], q_mat[...])
    for h in range(H):
        raw = q_raw[:, h * HD : (h + 1) * HD]
        rot = rotate(raw * rms(raw) * query_gain, cosines, sines)
        queries[h * TOK : (h + 1) * TOK, :] = rot.astype(BF16)
    lax.fori_loop(0, 8, unpack_out, 0)
    for copy in kv_copies:
        copy.wait()
    gb.third_on()

    def attend(h, carry):
        rows = pl.ds(pl.multiple_of(h * TOK, TOK), TOK)
        allowed = allowed_ref[...]
        scores = dot_nt(queries[rows, :], kv_all[:, 0:HD]) * SCORE_SCALE
        scores = jnp.where(allowed > 0.0, scores, NEG)
        peak = jnp.max(scores, axis=-1, keepdims=True)
        expd = jnp.exp(scores - peak) * allowed
        low = (expd * (1.0 / jnp.sum(expd, axis=-1, keepdims=True))).astype(BF16)
        probs[rows, :] = low
        value = dot(low, kv_all[:, HD : 2 * HD])
        attended[rows, :] = value
        attended_low[:, pl.ds(pl.multiple_of(h * HD, HD), HD)] = value.astype(BF16)
        return carry

    lax.fori_loop(0, H, attend, 0)
    gb.last()
    middle[...] = inputs + dot(attended_low[...], o_mat[...])
    scale_two = rms(middle[...])
    ffn_nat = (middle[...] * scale_two * gain_rows[1:2, :]).astype(BF16)
    ffn_in[...] = dot(ffn_nat, pick[...]).astype(BF16)
    gb.finish()

    def unpack_b(g, carry):
        for mat, s in ((g_mat, 0), (u_mat, 1)):
            slabs = [slab(bufs_b, s, g, j) for j in range(5)]
            turned_slabs = turn(perm[...], slabs[0:2])
            turned_slabs += turn(perm[...], slabs[2:4])
            turned_slabs += turn(perm[...], slabs[4:5])
            for r in range(5):
                mat[pl.ds(pl.multiple_of(r * 128 + g * 16, 16), 16), :] = tiles_wide(
                    turned_slabs[r], 0, 16
                )
        for d in range(16):
            c, index = block_index(2, g, d)
            block = bufs_b[2][c, index]
            d_mat[pl.ds(pl.multiple_of(g * 256 + d * 16, 16), 16), :] = tiles_wide(block, 0, 5)
        return carry

    lax.fori_loop(0, 8, unpack_b, 0)

    block_out[...] = middle[...]
    d_acc[...] = jnp.zeros_like(d_acc)
    root = math.sqrt(2.0 / math.pi)

    def feed(n, carry):
        at = pl.ds(pl.multiple_of(n * 512, 512), 512)
        gate = dot(ffn_in[...], g_mat[:, at])
        up = dot(ffn_in[...], u_mat[:, at])
        d_hidden = dot_nt(cotangent[...], d_mat[at, :])
        square = gate * gate
        tanh = jnp.tanh(root * gate * (1.0 + 0.044715 * square))
        lift = 0.5 * (1.0 + tanh)
        act = gate * lift
        slope = lift + 0.5 * gate * (1.0 - tanh * tanh) * root * (1.0 + 3 * 0.044715 * square)
        hid = (act * up).astype(BF16)
        dg = (d_hidden * up * slope).astype(BF16)
        du = (d_hidden * act).astype(BF16)
        hidden[:, at] = hid
        d_gate[:, at] = dg
        d_up[:, at] = du
        block_out[...] += dot(hid, d_mat[at, :])
        d_acc[...] += dot_nt(dg, g_mat[:, at]) + dot_nt(du, u_mat[:, at])
        return carry

    lax.fori_loop(0, 4, feed, 0)

    def put(bufs, s, g, j, block):
        for d in range(16):
            c, index = block_index(s, g, d)
            bufs[s][c, index, pl.ds(j * 16, 16), :] = block[d * 16 : (d + 1) * 16]

    def down_grads(g, carry):
        at = pl.ds(pl.multiple_of(g * 256, 256), 256)
        grad = dot_tn(hidden[:, at], cotangent[...]).astype(BF16)
        for d in range(16):
            c, index = block_index(2, g, d)
            rows = grad[d * 16 : (d + 1) * 16]
            bufs_b[2][c, index] = jnp.concatenate(
                [rows[:, i * 128 : (i + 1) * 128] for i in range(5)], axis=0
            )
        return carry

    def stack(grad, g, count):
        rows = grad[g * 16 : (g + 1) * 16]
        return [rows[:, i * 128 : (i + 1) * 128] for i in range(count)]

    def wide_grads(s, source):
        def step(r, carry):
            at = pl.ds(pl.multiple_of(r * 128, 128), 128)
            grad = dot_tn(ffn_in[:, at], source[...]).astype(BF16)
            for g in range(0, 8, 2):
                one, two = turn(
                    perm[...],
                    [jnp.concatenate(stack(grad, g + i, 16), axis=0) for i in range(2)],
                )
                put(bufs_b, s, g, r, one)
                put(bufs_b, s, g + 1, r, two)
            return carry

        lax.fori_loop(0, 5, step, 0)

    lax.fori_loop(0, 8, down_grads, 0)
    sb.to_pair((2,))
    wide_grads(0, d_gate)
    sb.to_pair((0,))
    wide_grads(1, d_up)
    sb.to_pair((1,))

    d_ffn = split_dot_nt(d_acc[...], pick[...])
    d_norm, grad_two = norm_back(d_ffn, middle[...], scale_two, gain_rows[1:2, :])
    d_middle = cotangent[...].astype(F32) + d_norm
    input_grad[...] = d_middle
    d_branch = d_middle.astype(BF16)
    d_attended_flat = dot_nt(d_branch, o_mat[...]).astype(BF16)
    for h in range(H):
        d_attended[h * TOK : (h + 1) * TOK, :] = d_attended_flat[:, h * HD : (h + 1) * HD]
    sb.begin(True)

    def scores_back(h, carry):
        rows = pl.ds(pl.multiple_of(h * TOK, TOK), TOK)
        upstream = d_attended[rows, :]
        delta = jnp.sum(upstream.astype(F32) * attended[rows, :], axis=-1, keepdims=True)
        d_probs = dot_nt(upstream, kv_all[:, HD : 2 * HD])
        d_scores[rows, :] = (probs[rows, :].astype(F32) * (d_probs - delta)).astype(BF16)
        return carry

    lax.fori_loop(0, H, scores_back, 0)

    def keys_back(n, carry):
        at = pl.ds(pl.multiple_of(n * 256, 256), 256)
        d_keys = dot_tn(d_scores[:, at], queries[...]) * SCORE_SCALE
        d_values = dot_tn(probs[:, at], d_attended[...])
        d_kv[at, :] = jnp.concatenate([d_keys, d_values], axis=1).astype(BF16)
        return carry

    lax.fori_loop(0, KEYS // 256, keys_back, 0)
    dkv_copies = [
        remote(
            d_kv.at[pl.ds(pl.multiple_of((me + step) % GROUP * TOK, TOK), TOK)],
            kv_in.at[step - 1],
            dkv_send.at[step - 1],
            dkv_recv.at[step - 1],
            group_partner(step),
        )
        for step in range(1, GROUP)
    ]
    sb.middle(True)

    def back_rotated(grad):
        return rotate(grad, cosines, -sines)

    query_gain_grad = jnp.zeros((1, HD), F32)
    for h in range(H):
        rows = slice(h * TOK, (h + 1) * TOK)
        d_rot = dot(d_scores[rows, :], kv_all[:, 0:HD]) * SCORE_SCALE
        raw = q_raw[:, h * HD : (h + 1) * HD]
        d_raw, gain_grad = norm_back(back_rotated(d_rot), raw, rms(raw), query_gain)
        query_gain_grad = query_gain_grad + gain_grad
        d_q_low[:, h * HD : (h + 1) * HD] = d_raw.astype(BF16)

    def out_grads(g, carry):
        at = pl.ds(pl.multiple_of(g * 128, 128), 128)
        grad = dot_tn(attended_low[:, at], d_branch).astype(BF16)
        cols = [grad[:, i * 128 : (i + 1) * 128] for i in range(5)]
        slabs = [
            jnp.concatenate(cols[0:2], axis=0),
            jnp.concatenate(cols[2:4], axis=0),
            jnp.concatenate([cols[4], jnp.zeros((128, 128), BF16)], axis=0),
        ]
        turned_back = dot_tn(flip[...], jnp.concatenate(slabs, axis=1)).astype(BF16)
        for j in range(3):
            put(bufs_a, 2, g, j, turned_back[:, j * 128 : (j + 1) * 128])
        return carry

    lax.fori_loop(0, 8, out_grads, 0)
    sa.to_pair((2,))
    sb.end(True)
    sb.begin(False)

    total = d_kv[mine, :].astype(F32)
    for step in range(GROUP - 1):
        dkv_copies[step].wait_recv()
        total = total + kv_in[step].astype(F32)
    key_raw = kv_raw[:, 0:HD]
    d_key_raw, key_gain_grad = norm_back(
        back_rotated(total[:, 0:HD]), key_raw, rms(key_raw), key_gain
    )
    d_kv_low[...] = jnp.concatenate([d_key_raw, total[:, HD:]], axis=1).astype(BF16)
    sb.middle(False)
    d_normed = split_dot_nt(
        dot_nt(d_q_low[...], q_mat[...]) + dot_nt(d_kv_low[...], kv_mat[...]), pick[...]
    )
    d_norm, grad_one = norm_back(d_normed, inputs, scale_one, gain_rows[0:1, :])
    input_grad[...] += d_norm

    def by_device(row, count, matrix):
        turned_row = dot(row.astype(BF16), matrix)
        return [turned_row[:, i * 128 : (i + 1) * 128] for i in range(count)]

    heads = jnp.concatenate([query_gain_grad, key_gain_grad], axis=1)
    gain_parts = by_device(grad_one, 5, pick[...]) + by_device(grad_two, 5, pick[...])
    gain_parts += by_device(heads, 4, head_pick)
    gain_parts.append(jnp.zeros((114, 128), F32))
    gain_cols[...] = jnp.concatenate(gain_parts, axis=0).T

    def grads_a(g, carry):
        at = pl.ds(pl.multiple_of(g * 16, 16), 16)
        q_rows, kv_rows = [], []
        for r in range(5):
            rows = pl.ds(pl.multiple_of(r * 128 + g * 16, 16), 16)
            q_row, kv_row = q_mat[rows, :], kv_mat[rows, :]
            q_rows += [q_row[:, i * 128 : (i + 1) * 128] for i in range(8)]
            kv_rows += [kv_row[:, i * 128 : (i + 1) * 128] for i in range(4)]
        zero = jnp.zeros((16, 128), BF16)
        q_rows += [gain_cols[at, :].astype(BF16)] + [zero] * 7
        kv_rows += [zero] * 12
        slabs = [jnp.concatenate(q_rows[i * 16 : (i + 1) * 16], axis=0) for i in range(3)]
        slabs += [jnp.concatenate(kv_rows[i * 16 : (i + 1) * 16], axis=0) for i in range(2)]
        out = turn(perm[...], slabs[0:2]) + turn(perm[...], slabs[2:4]) + turn(perm[...], slabs[4:5])
        for j in range(3):
            put(bufs_a, 0, g, j, out[j])
        for j in range(2):
            put(bufs_a, 1, g, j, out[3 + j])
        return carry

    q_mat[...] = dot_tn(normed[...], d_q_low[...]).astype(BF16)
    kv_mat[...] = dot_tn(normed[...], d_kv_low[...]).astype(BF16)
    lax.fori_loop(0, 8, grads_a, 0)
    sa.to_pair((0, 1))
    sb.end(False)
    sb.to_owners()
    sa.begin(True)
    sa.middle(True)
    sb.finish()
    sa.end(True)
    sa.begin(False)
    sa.middle(False)
    sa.end(False)
    sa.to_owners()
    for copy in dkv_copies:
        copy.wait_send()
    sa.finish()


def finish_kernel(a0, a1, a2, b0, b1, b2, out, grad, block_out, input_grad, *outs):
    query, key, value, output, gate, up, down, vectors = outs
    block_out[...] = out[...].astype(BF16)
    input_grad[...] = grad[...]

    def exact(order, block):
        return lax.dot_general(
            order,
            block,
            (((0,), (0,)), ((), ())),
            precision=lax.Precision.HIGHEST,
            preferred_element_type=F32,
        )

    def spread(ref, stacked, first, count):
        for c in range(count):
            ref[:, c * 128 : (c + 1) * 128] = stacked[(first + c) * 8 : (first + c) * 8 + 5]

    spread(query, exact(row_order(48, 8), a0[...]), 0, 8)
    stacked = exact(row_order(32, 4), a1[...])
    spread(key, stacked, 0, 2)
    spread(value, stacked, 2, 2)
    for c in range(5):
        output[:, c * 128 : (c + 1) * 128] = a2[c * 8 : (c + 1) * 8]
        down[:, c * 128 : (c + 1) * 128] = b2[c * 16 : (c + 1) * 16]
    order = row_order(80, 16)
    spread(gate, exact(order, b0[...]), 0, 16)
    spread(up, exact(order, b1[...]), 0, 16)
    vectors[...] = a0[GAIN_ROW : GAIN_ROW + 8]


def vmem_specs(count):
    return [pl.BlockSpec(memory_space=pltpu.VMEM)] * count


def body(
    tokens,
    w_query,
    w_key,
    w_value,
    w_out,
    w_gate,
    w_up,
    w_down,
    attn_gain,
    ffn_gain,
    head_gains,
    lengths,
    cotangent,
):
    gains = jnp.concatenate([attn_gain, ffn_gain, head_gains]).astype(F32)
    gains = jnp.pad(gains[None, :], ((0, 7), (0, 114)))

    def low(*shape):
        return pltpu.VMEM(shape, BF16)

    def full(*shape):
        return pltpu.VMEM(shape, F32)

    phases = [[low(2, 64, rows, 128) for rows in phase] for phase in ROWS]
    inboxes = [
        [low(count, rows, 128) for rows in phase] for count in (64, 48, 12, 3) for phase in ROWS
    ]
    scratch = sum(phases, []) + sum(inboxes, [])
    scratch += [low(D, 1024), low(D, 512), low(1024, D), low(D, FF), low(D, FF), low(FF, D)]
    scratch += [low(256, 256), low(256, 256), low(D, D), full(128, 128), full(8, D)]
    scratch += [full(TOK, 128), full(TOK, 128), full(TOK, KEYS)]
    scratch += [low(TOK, D), low(TOK, D), full(TOK, D)]
    scratch += [full(TOK, 1024), full(TOK, 512), low(H * TOK, HD), low(KEYS, 2 * HD)]
    scratch += [low(H * TOK, KEYS), full(H * TOK, HD), low(TOK, 1024), low(H * TOK, HD)]
    scratch += [low(H * TOK, KEYS), low(TOK, FF), low(TOK, FF), low(TOK, FF), full(TOK, D)]
    scratch += [low(KEYS, 2 * HD), low(GROUP - 1, TOK, 2 * HD), low(TOK, 1024), low(TOK, 512)]
    dma = pltpu.SemaphoreType.DMA
    scratch += [dma((2, 3, 16)), dma((2, 3, 16)), dma((2, 3, 15)), dma((2, 3, 15))]
    scratch += [dma((7,)), dma((7,)), dma((7,)), dma((7,))]
    out, grad, *sums = pl.pallas_call(
        block_kernel,
        out_shape=[jax.ShapeDtypeStruct((TOK, D), F32)] * 2
        + [jax.ShapeDtypeStruct((rows, 128), F32) for phase in ROWS for rows in phase],
        in_specs=vmem_specs(2) + [pl.BlockSpec(memory_space=pltpu.SMEM)] + vmem_specs(8),
        out_specs=vmem_specs(8),
        scratch_shapes=scratch,
        compiler_params=pltpu.CompilerParams(
            collective_id=0, has_side_effects=True, vmem_limit_bytes=VMEM_BYTES
        ),
        name="block",
    )(
        tokens,
        cotangent,
        lengths,
        w_query,
        w_key,
        w_value,
        w_out,
        w_gate,
        w_up,
        w_down,
        gains,
    )
    shards = [
        jax.ShapeDtypeStruct(shape, F32)
        for shape in ((5, 1024), (5, 256), (5, 256), (8, D), (5, FF), (5, FF), (16, D), (8, 128))
    ]
    *results, vectors = pl.pallas_call(
        finish_kernel,
        out_shape=[jax.ShapeDtypeStruct((TOK, D), BF16), jax.ShapeDtypeStruct((TOK, D), F32)]
        + shards,
        in_specs=vmem_specs(8),
        out_specs=vmem_specs(10),
        name="finish",
    )(*sums, out, grad)
    flat = vectors[0]
    return (*results, flat[0:5], flat[5:10], flat[10:14])


def solution(mesh):
    rows = P(("dp", "fsdp"), None)
    vector = P(("dp", "fsdp"))
    return jax.shard_map(
        body,
        mesh=mesh,
        in_specs=(rows,) * 8 + (vector,) * 3 + (P("dp", None), rows),
        out_specs=(rows,) * 9 + (vector,) * 3,
        check_vma=False,
    )
```

```python
import math

import jax
import jax.numpy as jnp
from jax import lax
from jax.experimental import pallas as pl
from jax.experimental.pallas import tpu as pltpu
from jax.sharding import PartitionSpec as P

H = 4
HD = 256
D = 640
FF = 2048
TOK = 128
GROUP = 8
KEYS = TOK * GROUP
EPS = 1e-05
ROPE_BASE = 1000000.0
NEG = -1e30
SCORE_SCALE = 1.0 / math.sqrt(HD)
F32 = jnp.float32
BF16 = jnp.bfloat16

MESH = pl.DeviceIdType.MESH
VMEM_BYTES = 60 * 1024 * 1024

ORDERS = ((0, 1, 2), (1, 2, 0), (2, 0, 1))
ROWS = ((32, 32, 48), (80, 80, 80))
GAIN_ROW = 28


def coords():
    dp = lax.axis_index("dp")
    fsdp = lax.axis_index("fsdp")
    return (fsdp // 2, (dp // 2) % 4, (dp // 8) * 2 + fsdp % 2, dp % 2)


def device(place):
    x, y, z, core = place
    return ((z // 2) * 8 + y * 2 + core, x * 2 + z % 2)


def shifted(place, axis, step):
    moved = list(place)
    moved[axis] = (place[axis] + step) % 4
    return tuple(moved)


def sibling(place):
    return place[:3] + (1 - place[3],)


def group_partner(step):
    return (lax.axis_index("dp"), (lax.axis_index("fsdp") + step) % GROUP)


def greet(place):
    partners = [device(shifted(place, axis, step)) for axis in range(3) for step in (1, 2, 3)]
    partners.append(device(sibling(place)))
    x, y, z, core = place
    flipped = (x, y, (z // 2) * 2 + (1 - z % 2), core)
    partners += [device(shifted(flipped, 0, step)) for step in (1, 2, 3)]
    barrier = pltpu.get_barrier_semaphore()
    for partner in partners:
        pl.semaphore_signal(barrier, inc=1, device_id=partner, device_id_type=MESH)
    return lambda: pl.semaphore_wait(barrier, len(partners))


def remote(src, dst, send, recv, to):
    copy = pltpu.make_async_remote_copy(
        src_ref=src, dst_ref=dst, send_sem=send, recv_sem=recv, device_id=to, device_id_type=MESH
    )
    copy.start()
    return copy


class Gather:
    def __init__(self, place, s, buf, send, recv):
        self.place, self.buf, self.send, self.recv = place, buf, send, recv
        self.axes = ORDERS[s]
        self.at = tuple(place[axis] for axis in self.axes)
        self.sent, self.pair, self.kept = [], [], []

    def copy(self, slot, first, count, to, keep):
        ref = self.buf.at[self.place[3], pl.ds(first, count)]
        copy = remote(ref, ref, self.send.at[slot], self.recv.at[slot], device(to))
        keep.append(copy)

    def to_line(self, level, first, count):
        self.kept = []
        for step in (2, 1, 3):
            to = shifted(self.place, self.axes[level], step)
            self.copy(3 * level + step - 1, first, count, to, self.kept)
        self.sent += self.kept

    def arrive(self):
        for copy in self.kept:
            copy.wait_recv()

    def first(self):
        ka, kb, kc = self.at
        self.to_line(0, kc * 16 + kb * 4 + ka, 1)

    def second(self):
        self.arrive()
        ka, kb, kc = self.at
        self.to_line(1, kc * 16 + kb * 4, 4)

    def third(self):
        self.arrive()
        kc = self.at[2]
        self.to_line(2, kc * 16, 16)
        self.copy(9, kc * 16, 16, sibling(self.place), self.pair)

    def to_pair(self):
        kc = self.at[2]
        for step, copy in zip((2, 1, 3), self.kept):
            copy.wait_recv()
        for step in (1, 2, 3):
            self.copy(9 + step, (kc - step + 4) % 4 * 16, 16, sibling(self.place), self.pair)

    def finish(self):
        for copy in self.pair:
            copy.wait()
        for copy in self.sent:
            copy.wait_send()


def add_blocks(total, count, first, *others):
    def step(i, carry):
        value = total[first + i].astype(F32)
        for other in others:
            value = value + other(i).astype(F32)
        total[first + i] = value.astype(BF16)
        return carry

    lax.fori_loop(0, count, step, 0, unroll=4)


class Scatter:
    def __init__(self, place, s, buf, pair, far, mid, near, out, send, recv):
        self.place, self.buf, self.pair_in = place, buf, pair
        self.inbox, self.out = (near, mid, far), out
        self.send, self.recv = send, recv
        self.axes = ORDERS[s]
        self.at = tuple(place[axis] for axis in self.axes)
        self.own = buf.at[place[3]]
        self.sent, self.pairs, self.kept = [], {}, []

    def copy(self, slot, src, dst, to):
        copy = remote(src, dst, self.send.at[slot], self.recv.at[slot], device(to))
        self.sent.append(copy)
        return copy

    def to_pair(self):
        other = self.buf.at[1 - self.place[3]]
        for offset in (2, 1, 3, 0):
            rows = pl.ds((self.at[2] + offset) % 4 * 16, 16)
            self.pairs[offset] = self.copy(
                offset, other.at[rows], self.pair_in.at[rows], sibling(self.place)
            )

    def add_pair(self, offset):
        self.pairs[offset].wait_recv()
        start = (self.at[2] + offset) % 4 * 16
        add_blocks(self.own, 16, start, lambda i: self.pair_in[start + i])

    def to_line(self, level, base, size, prepare=None):
        inbox = self.inbox[level]
        self.kept = []
        for step in (2, 1, 3):
            if prepare is not None:
                prepare(step)
            first = base + (self.at[level] + step) % 4 * size
            copy = self.copy(
                4 + 3 * level + step - 1,
                self.own.at[pl.ds(first, size)],
                inbox.at[pl.ds((step - 1) * size, size)],
                shifted(self.place, self.axes[level], step),
            )
            self.kept.append(copy)

    def total(self, level, base, size):
        for copy in self.kept:
            copy.wait_recv()
        inbox = self.inbox[level]
        add_blocks(
            self.own,
            size,
            base + self.at[level] * size,
            *[lambda i, n=n: inbox[n * size + i] for n in range(3)],
        )

    def far(self):
        self.to_line(2, 0, 16, self.add_pair)

    def mid(self):
        self.add_pair(0)
        self.total(2, 0, 16)
        self.to_line(1, self.at[2] * 16, 4)

    def near(self):
        self.total(1, self.at[2] * 16, 4)
        self.to_line(0, self.at[2] * 16 + self.at[1] * 4, 1)

    def finish(self):
        for copy in self.kept:
            copy.wait_recv()
        ka, kb, kc = self.at
        value = self.own[kc * 16 + kb * 4 + ka].astype(F32)
        for step in range(3):
            value = value + self.inbox[0][step].astype(F32)
        self.out[...] = value
        for copy in self.sent:
            copy.wait_send()


def one_hot(rows, columns, pick):
    i = lax.broadcasted_iota(jnp.int32, (rows, columns), 0)
    j = lax.broadcasted_iota(jnp.int32, (rows, columns), 1)
    return jnp.where(pick(i) == j, 1.0, 0.0)


def dot(left, right):
    return jnp.dot(left, right, preferred_element_type=F32)


def dot_nt(left, right):
    return lax.dot_general(left, right, (((1,), (1,)), ((), ())), preferred_element_type=F32)


def dot_tn(left, right):
    return lax.dot_general(left, right, (((0,), (0,)), ((), ())), preferred_element_type=F32)


def stack_columns(shard):
    r, columns = shard.shape
    value = shard.astype(F32)
    pad = [jnp.zeros((8 - r, 128), F32)] if r < 8 else []
    pieces = []
    for c in range(columns // 128):
        pieces += [value[:, c * 128 : (c + 1) * 128]] + pad
    return jnp.concatenate(pieces, axis=0)


def query_order():
    return one_hot(32, 64, lambda i: (i & 7) * 8 + (i >> 3))


def mixed_order():
    def pick(i):
        rest = jnp.where(i < 28, 32 + (i - 20) * 8 + 4, -1)
        return jnp.where(i < 20, (i & 3) * 8 + (i >> 2), rest)

    return one_hot(32, 96, pick)


def wide_order():
    return one_hot(80, 128, lambda i: (i & 15) * 8 + (i >> 4))


def block_index(s, g, d):
    z_hi, y = g // 4, g % 4
    core, x, z_lo = d // 8, (d // 2) % 4, d % 2
    place = (x, y, z_hi * 2 + z_lo)
    a, b, c = (place[axis] for axis in ORDERS[s])
    return core, c * 16 + b * 4 + a


def rms(value):
    return lax.rsqrt(jnp.mean(value * value, axis=-1, keepdims=True) + EPS)


def rotate(value, cosines, sines):
    half = HD // 2
    u, w = value[:, :half], value[:, half:]
    return jnp.concatenate([u * cosines - w * sines, w * cosines + u * sines], axis=1)


def norm_back(grad, value, scale, gain):
    scaled = grad * gain
    back = scale * scaled - value * scale**3 * jnp.mean(scaled * value, axis=-1, keepdims=True)
    return back, jnp.sum(grad * value * scale, axis=0, keepdims=True)


def split_dot_nt(value, matrix):
    high = value.astype(BF16)
    low = (value - high.astype(F32)).astype(BF16)
    return dot_nt(high, matrix) + dot_nt(low, matrix)


def block_kernel(
    tokens,
    cotangent,
    lengths,
    w_query,
    w_key,
    w_value,
    w_out,
    w_gate,
    w_up,
    w_down,
    gains,
    block_out,
    input_grad,
    sum_a0,
    sum_a1,
    sum_a2,
    sum_b0,
    sum_b1,
    sum_b2,
    a0,
    a1,
    a2,
    b0,
    b1,
    b2,
    *scratch,
):
    it = iter(scratch)

    def take(count):
        return [next(it) for _ in range(count)]

    pair_in, far_in, mid_in, near_in = take(6), take(6), take(6), take(6)
    q_mat, kv_mat, o_mat, g_mat, u_mat, d_mat, q_grad, kv_grad = take(8)
    perm, flip, pick, head_pick, gain_cols, gain_rows = take(6)
    cos_ref, sin_ref, allowed_ref = take(3)
    tok_all, scaled, normed, ffn_in, middle = take(5)
    q_raw, kv_raw, queries, kv_all = take(4)
    probs, attended, attended_low, d_attended, d_scores = take(5)
    hidden, d_gate, d_up, d_acc = take(4)
    d_kv_low, kv_in, d_q_low = take(3)
    gather_send, gather_recv, scatter_send, scatter_recv = take(4)
    tok_send, tok_recv, dkv_send, dkv_recv = take(4)

    place = coords()
    core = place[3]
    met = greet(place)
    me = lax.axis_index("fsdp")
    mine = pl.ds(pl.multiple_of(me * TOK, TOK), TOK)
    bufs = (a0, a1, a2, b0, b1, b2)
    outs = (sum_a0, sum_a1, sum_a2, sum_b0, sum_b1, sum_b2)

    def own_ref(n):
        ka, kb, kc = (place[axis] for axis in ORDERS[n % 3])
        return bufs[n].at[core, kc * 16 + kb * 4 + ka]

    query_stack = stack_columns(w_query[...]).astype(BF16)
    own_ref(0)[...] = dot(query_order().astype(BF16), query_stack).astype(BF16)
    mixed = jnp.concatenate(
        [
            stack_columns(w_key[...]).astype(BF16),
            stack_columns(w_value[...]).astype(BF16),
            query_stack,
        ],
        axis=0,
    )
    packed = dot(mixed_order().astype(BF16), mixed)
    own_ref(1)[...] = jnp.concatenate([packed[:24], packed[24:] + gains[...]], axis=0).astype(BF16)
    packed = jnp.concatenate([stack_columns(w_out[...]), jnp.zeros((8, 128), F32)], axis=0)
    own_ref(2)[...] = packed.astype(BF16)
    order = wide_order().astype(BF16)
    own_ref(3)[...] = dot(order, stack_columns(w_gate[...]).astype(BF16)).astype(BF16)
    own_ref(4)[...] = dot(order, stack_columns(w_up[...]).astype(BF16)).astype(BF16)
    down = w_down[...]
    own_ref(5)[...] = jnp.concatenate(
        [down[:, c * 128 : (c + 1) * 128] for c in range(5)], axis=0
    )
    tok_all[mine, :] = tokens[...]

    ga = [
        Gather(place, n % 3, bufs[n], gather_send.at[n], gather_recv.at[n]) for n in range(6)
    ]
    sc = [
        Scatter(
            place,
            n % 3,
            bufs[n],
            pair_in[n],
            far_in[n],
            mid_in[n],
            near_in[n],
            outs[n],
            scatter_send.at[n],
            scatter_recv.at[n],
        )
        for n in range(6)
    ]
    met()
    for n in (1, 0, 2, 3, 4, 5):
        ga[n].first()

    perm[...] = one_hot(256, 256, lambda i: (i & 15) * 16 + (i >> 4)).astype(BF16)
    flip[...] = one_hot(
        256, 256, lambda i: ((i & 127) >> 3) * 16 + (i >> 7) * 8 + (i & 7)
    ).astype(BF16)
    row = lax.broadcasted_iota(jnp.int32, (D, D), 0)
    column = lax.broadcasted_iota(jnp.int32, (D, D), 1)
    pick[...] = jnp.where(row == 5 * (column & 127) + (column >> 7), 1.0, 0.0).astype(BF16)
    row = lax.broadcasted_iota(jnp.int32, (2 * HD, 2 * HD), 0)
    column = lax.broadcasted_iota(jnp.int32, (2 * HD, 2 * HD), 1)
    head_pick[...] = jnp.where(row == 4 * (column & 127) + (column >> 7), 1.0, 0.0).astype(BF16)
    for n in (1, 0, 2):
        ga[n].second()
    tok_copies = [
        remote(
            tok_all.at[mine],
            tok_all.at[mine],
            tok_send.at[step - 1],
            tok_recv.at[step - 1],
            group_partner(step),
        )
        for step in range(1, GROUP)
    ]
    first_len, second_len = lengths[0, 0], lengths[0, 1]
    first_end, second_end = first_len, first_len + second_len

    def segment(ids):
        past_one = jnp.where(ids >= first_end, 1, 0)
        past_two = jnp.where(ids >= second_end, 1, 0)
        return past_one + past_two, ids - past_one * first_len - past_two * second_len

    lane = lax.broadcasted_iota(jnp.int32, (TOK, HD // 2), 1).astype(F32)
    frequencies = jnp.exp(lane * (2.0 / HD) * (-math.log(ROPE_BASE)))

    def tables(m, carry):
        ids = m * TOK + lax.broadcasted_iota(jnp.int32, (TOK, HD // 2), 0)
        angles = segment(ids)[1].astype(F32) * frequencies
        rows = pl.ds(pl.multiple_of(m * TOK, TOK), TOK)
        cos_ref[rows, :] = jnp.cos(angles)
        sin_ref[rows, :] = jnp.sin(angles)
        return carry

    lax.fori_loop(0, GROUP, tables, 0)
    for n in (1, 0, 2):
        ga[n].third()
    row_ids = me * TOK + lax.broadcasted_iota(jnp.int32, (TOK, KEYS), 0)
    key_ids = lax.broadcasted_iota(jnp.int32, (TOK, KEYS), 1)
    same = segment(row_ids)[0] == segment(key_ids)[0]
    allowed_ref[...] = jnp.where(same & (key_ids <= row_ids), 1.0, 0.0)
    for n in (3, 4, 5):
        ga[n].second()
    inputs = tokens[...].astype(F32)
    scale_one = rms(inputs)
    for n in (1, 0):
        ga[n].to_pair()
    for copy in tok_copies:
        copy.wait()

    def scale_tokens(m, carry):
        rows = pl.ds(pl.multiple_of(m * TOK, TOK), TOK)
        value = tok_all[rows, :]
        scaled[rows, :] = dot(value, pick[...]) * rms(value.astype(F32))
        return carry

    lax.fori_loop(0, GROUP, scale_tokens, 0)
    for n in (3, 4, 5):
        ga[n].third()
    ga[1].finish()
    ga[0].finish()

    def slab(n, g, j):
        tiles = []
        for d in range(16):
            c, index = block_index(n % 3, g, d)
            tiles.append(bufs[n][c, index, pl.ds(j * 16, 16), :])
        return jnp.concatenate(tiles, axis=0)

    def turn(matrix, parts):
        out = dot(matrix, jnp.concatenate(parts, axis=1)).astype(BF16)
        return [out[:, i * 128 : (i + 1) * 128] for i in range(len(parts))]

    def tiles_wide(block, first, count):
        return jnp.concatenate(
            [block[(first + i) * 16 : (first + i + 1) * 16] for i in range(count)], axis=1
        )

    def unpack_a(g, carry):
        at = pl.ds(pl.multiple_of(g * 16, 16), 16)

        def rows(r):
            return pl.ds(pl.multiple_of(r * 128 + g * 16, 16), 16)

        kv0, kv1 = turn(perm[...], [slab(1, g, 0), slab(1, g, 1)])
        q0, q1 = turn(perm[...], [slab(0, g, 0), slab(0, g, 1)])
        for r, (block, first) in enumerate(((q0, 0), (q0, 8), (q1, 0), (q1, 8), (kv1, 4))):
            q_mat[rows(r), :] = tiles_wide(block, first, 8)
        gain_cols[at, :] = kv1[12 * 16 : 13 * 16].astype(F32)
        for r in range(4):
            kv_mat[rows(r), :] = tiles_wide(kv0, 4 * r, 4)
        kv_mat[rows(4), :] = tiles_wide(kv1, 0, 4)
        return carry

    lax.fori_loop(0, 8, unpack_a, 0)

    def unpack_out(g, carry):
        o0, o1 = turn(flip[...], [slab(2, g, 0), slab(2, g, 1)])
        (o2,) = turn(flip[...], [slab(2, g, 2)])
        o_mat[pl.ds(pl.multiple_of(g * 128, 128), 128), :] = jnp.concatenate(
            [o0[:128], o0[128:], o1[:128], o1[128:], o2[:128]], axis=1
        )
        return carry

    turned = gain_cols[...].T

    def by_column(first, count):
        return jnp.concatenate([turned[first + i : first + i + 1] for i in range(count)], axis=1)

    gain_rows[2:3, 0 : 2 * HD] = dot_nt(by_column(10, 4).astype(BF16), head_pick[...])

    key_gain = gain_rows[2:3, HD : 2 * HD]
    query_gain = gain_rows[2:3, 0:HD]
    turned_gain = by_column(0, 5)

    def keys_forward(m, carry):
        rows = pl.ds(pl.multiple_of(m * 256, 256), 256)
        normed_rows = (scaled[rows, :] * turned_gain).astype(BF16)
        normed[rows, :] = normed_rows
        raw = dot(normed_rows, kv_mat[...])
        kv_raw[rows, :] = raw
        key_raw = raw[:, 0:HD]
        key_rot = rotate(key_raw * rms(key_raw) * key_gain, cos_ref[rows, :], sin_ref[rows, :])
        kv_all[rows, :] = jnp.concatenate([key_rot, raw[:, HD:]], axis=1).astype(BF16)
        return carry

    lax.fori_loop(0, KEYS // 256, keys_forward, 0)
    cosines, sines = cos_ref[mine, :], sin_ref[mine, :]
    q_raw[...] = dot(normed[mine, :], q_mat[...])
    for h in range(H):
        raw = q_raw[:, h * HD : (h + 1) * HD]
        rot = rotate(raw * rms(raw) * query_gain, cosines, sines)
        queries[h * TOK : (h + 1) * TOK, :] = rot.astype(BF16)
    ga[2].to_pair()

    def attend(h, carry):
        rows = pl.ds(pl.multiple_of(h * TOK, TOK), TOK)
        allowed = allowed_ref[...]
        scores = dot_nt(queries[rows, :], kv_all[:, 0:HD]) * SCORE_SCALE
        scores = jnp.where(allowed > 0.0, scores, NEG)
        peak = jnp.max(scores, axis=-1, keepdims=True)
        expd = jnp.exp(scores - peak) * allowed
        low = (expd * (1.0 / jnp.sum(expd, axis=-1, keepdims=True))).astype(BF16)
        probs[rows, :] = low
        value = dot(low, kv_all[:, HD : 2 * HD])
        attended[rows, :] = value
        attended_low[:, pl.ds(pl.multiple_of(h * HD, HD), HD)] = value.astype(BF16)
        return carry

    lax.fori_loop(0, H, attend, 0)
    for n in (3, 4, 5):
        ga[n].to_pair()
    ga[2].finish()
    lax.fori_loop(0, 8, unpack_out, 0)
    gain_rows[0:1, :] = dot_nt(by_column(0, 5).astype(BF16), pick[...])
    gain_rows[1:2, :] = dot_nt(by_column(5, 5).astype(BF16), pick[...])
    middle[...] = inputs + dot(attended_low[...], o_mat[...])
    scale_two = rms(middle[...])
    ffn_nat = (middle[...] * scale_two * gain_rows[1:2, :]).astype(BF16)
    ffn_in[...] = dot(ffn_nat, pick[...]).astype(BF16)
    for n in (3, 4, 5):
        ga[n].finish()

    def unpack_b(g, carry):
        for mat, n in ((g_mat, 3), (u_mat, 4)):
            slabs = [slab(n, g, j) for j in range(5)]
            turned_slabs = turn(perm[...], slabs[0:2])
            turned_slabs += turn(perm[...], slabs[2:4])
            turned_slabs += turn(perm[...], slabs[4:5])
            for r in range(5):
                mat[pl.ds(pl.multiple_of(r * 128 + g * 16, 16), 16), :] = tiles_wide(
                    turned_slabs[r], 0, 16
                )
        for d in range(16):
            c, index = block_index(2, g, d)
            block = bufs[5][c, index]
            d_mat[pl.ds(pl.multiple_of(g * 256 + d * 16, 16), 16), :] = tiles_wide(block, 0, 5)
        return carry

    lax.fori_loop(0, 8, unpack_b, 0)

    block_out[...] = middle[...]
    d_acc[...] = jnp.zeros_like(d_acc)
    root = math.sqrt(2.0 / math.pi)

    def feed(n, carry):
        at = pl.ds(pl.multiple_of(n * 512, 512), 512)
        gate = dot(ffn_in[...], g_mat[:, at])
        up = dot(ffn_in[...], u_mat[:, at])
        d_hidden = dot_nt(cotangent[...], d_mat[at, :])
        square = gate * gate
        tanh = jnp.tanh(root * gate * (1.0 + 0.044715 * square))
        lift = 0.5 * (1.0 + tanh)
        act = gate * lift
        slope = lift + 0.5 * gate * (1.0 - tanh * tanh) * root * (1.0 + 3 * 0.044715 * square)
        hid = (act * up).astype(BF16)
        dg = (d_hidden * up * slope).astype(BF16)
        du = (d_hidden * act).astype(BF16)
        hidden[:, at] = hid
        d_gate[:, at] = dg
        d_up[:, at] = du
        block_out[...] += dot(hid, d_mat[at, :])
        d_acc[...] += dot_nt(dg, g_mat[:, at]) + dot_nt(du, u_mat[:, at])
        return carry

    lax.fori_loop(0, 4, feed, 0)

    def put(n, g, j, block):
        for d in range(16):
            c, index = block_index(n % 3, g, d)
            bufs[n][c, index, pl.ds(j * 16, 16), :] = block[d * 16 : (d + 1) * 16]

    def down_grads(g, carry):
        at = pl.ds(pl.multiple_of(g * 256, 256), 256)
        grad = dot_tn(hidden[:, at], cotangent[...]).astype(BF16)
        for d in range(16):
            c, index = block_index(2, g, d)
            rows = grad[d * 16 : (d + 1) * 16]
            bufs[5][c, index] = jnp.concatenate(
                [rows[:, i * 128 : (i + 1) * 128] for i in range(5)], axis=0
            )
        return carry

    def stack(grad, g, count):
        rows = grad[g * 16 : (g + 1) * 16]
        return [rows[:, i * 128 : (i + 1) * 128] for i in range(count)]

    def wide_grads(n, source):
        def step(r, carry):
            at = pl.ds(pl.multiple_of(r * 128, 128), 128)
            grad = dot_tn(ffn_in[:, at], source[...]).astype(BF16)
            for g in range(0, 8, 2):
                one, two = turn(
                    perm[...],
                    [jnp.concatenate(stack(grad, g + i, 16), axis=0) for i in range(2)],
                )
                put(n, g, r, one)
                put(n, g + 1, r, two)
            return carry

        lax.fori_loop(0, 5, step, 0)

    lax.fori_loop(0, 8, down_grads, 0)
    sc[5].to_pair()
    wide_grads(3, d_gate)
    sc[3].to_pair()
    sc[5].far()
    wide_grads(4, d_up)
    sc[4].to_pair()
    sc[3].far()

    d_ffn = split_dot_nt(d_acc[...], pick[...])
    d_norm, grad_two = norm_back(d_ffn, middle[...], scale_two, gain_rows[1:2, :])
    d_middle = cotangent[...].astype(F32) + d_norm
    input_grad[...] = d_middle
    d_branch = d_middle.astype(BF16)
    d_attended_flat = dot_nt(d_branch, o_mat[...]).astype(BF16)
    for h in range(H):
        d_attended[h * TOK : (h + 1) * TOK, :] = d_attended_flat[:, h * HD : (h + 1) * HD]
    sc[4].far()

    def out_grads(g, carry):
        at = pl.ds(pl.multiple_of(g * 128, 128), 128)
        grad = dot_tn(attended_low[:, at], d_branch).astype(BF16)
        cols = [grad[:, i * 128 : (i + 1) * 128] for i in range(5)]
        slabs = [
            jnp.concatenate(cols[0:2], axis=0),
            jnp.concatenate(cols[2:4], axis=0),
            jnp.concatenate([cols[4], jnp.zeros((128, 128), BF16)], axis=0),
        ]
        turned_back = dot_tn(flip[...], jnp.concatenate(slabs, axis=1)).astype(BF16)
        for j in range(3):
            put(2, g, j, turned_back[:, j * 128 : (j + 1) * 128])
        return carry

    lax.fori_loop(0, 8, out_grads, 0)
    sc[2].to_pair()

    def scores_back(h, carry):
        rows = pl.ds(pl.multiple_of(h * TOK, TOK), TOK)
        upstream = d_attended[rows, :]
        delta = jnp.sum(upstream.astype(F32) * attended[rows, :], axis=-1, keepdims=True)
        d_probs = dot_nt(upstream, kv_all[:, HD : 2 * HD])
        d_scores[rows, :] = (probs[rows, :].astype(F32) * (d_probs - delta)).astype(BF16)
        return carry

    lax.fori_loop(0, H, scores_back, 0)
    sc[5].mid()

    def keys_back(n, key_gain_grad):
        at = pl.ds(pl.multiple_of(n * 256, 256), 256)
        d_keys = dot_tn(d_scores[:, at], queries[...]) * SCORE_SCALE
        d_values = dot_tn(probs[:, at], d_attended[...])
        d_rot = rotate(d_keys, cos_ref[at, :], -sin_ref[at, :])
        raw = kv_raw[at, 0:HD]
        d_raw, gain_grad = norm_back(d_rot, raw, rms(raw), key_gain)
        d_kv_low[at, :] = jnp.concatenate([d_raw, d_values], axis=1).astype(BF16)
        return key_gain_grad + gain_grad

    key_gain_grad = lax.fori_loop(0, KEYS // 256, keys_back, jnp.zeros((1, HD), F32))
    sc[2].far()
    sc[3].mid()

    query_gain_grad = jnp.zeros((1, HD), F32)
    for h in range(H):
        rows = slice(h * TOK, (h + 1) * TOK)
        d_rot = dot(d_scores[rows, :], kv_all[:, 0:HD]) * SCORE_SCALE
        raw = q_raw[:, h * HD : (h + 1) * HD]
        d_raw, gain_grad = norm_back(
            rotate(d_rot, cosines, -sines), raw, rms(raw), query_gain
        )
        query_gain_grad = query_gain_grad + gain_grad
        d_q_low[:, h * HD : (h + 1) * HD] = d_raw.astype(BF16)
    kv_grad[...] = dot_tn(normed[...], d_kv_low[...]).astype(BF16)
    q_grad[...] = dot_tn(normed[mine, :], d_q_low[...]).astype(BF16)
    sc[4].mid()

    d_key_total = jnp.zeros((1, D), F32)
    d_normed_q = dot_nt(d_q_low[...], q_mat[...])

    def norm_one_grad(n, total):
        at = pl.ds(pl.multiple_of(n * 256, 256), 256)
        return total + jnp.sum(
            dot_nt(d_kv_low[at, :], kv_mat[...]) * scaled[at, :], axis=0, keepdims=True
        )

    grad_one = lax.fori_loop(0, KEYS // 256, norm_one_grad, d_key_total)
    grad_one = grad_one + jnp.sum(d_normed_q * scaled[mine, :], axis=0, keepdims=True)

    def by_device(row, count, matrix):
        turned_row = dot(row.astype(BF16), matrix)
        return [turned_row[:, i * 128 : (i + 1) * 128] for i in range(count)]

    heads = jnp.concatenate([query_gain_grad, key_gain_grad], axis=1)
    gain_parts = [grad_one[:, i * 128 : (i + 1) * 128] for i in range(5)]
    gain_parts += by_device(grad_two, 5, pick[...]) + by_device(heads, 4, head_pick[...])
    gain_parts.append(jnp.zeros((114, 128), F32))
    gain_cols[...] = jnp.concatenate(gain_parts, axis=0).T

    def grads_a(g, carry):
        at = pl.ds(pl.multiple_of(g * 16, 16), 16)
        q_tiles, kv_tiles = [], []
        for r in range(5):
            rows = pl.ds(pl.multiple_of(r * 128 + g * 16, 16), 16)
            q_row, kv_row = q_grad[rows, :], kv_grad[rows, :]
            q_tiles += [q_row[:, i * 128 : (i + 1) * 128] for i in range(8)]
            kv_tiles += [kv_row[:, i * 128 : (i + 1) * 128] for i in range(4)]
        kv_tiles += q_tiles[32:40] + [gain_cols[at, :].astype(BF16)]
        kv_tiles += [jnp.zeros((16, 128), BF16)] * 3
        slabs = [
            jnp.concatenate(tiles[i : i + 16], axis=0)
            for tiles in (q_tiles, kv_tiles)
            for i in (0, 16)
        ]
        out = turn(perm[...], slabs[0:2]) + turn(perm[...], slabs[2:4])
        for n in range(2):
            for j in range(2):
                put(n, g, j, out[2 * n + j])
        return carry

    lax.fori_loop(0, 8, grads_a, 0)
    sc[1].to_pair()
    sc[0].to_pair()
    sc[1].far()
    sc[0].far()
    dkv_copies = [
        remote(
            d_kv_low.at[pl.ds(pl.multiple_of((me + step) % GROUP * TOK, TOK), TOK)],
            kv_in.at[step - 1],
            dkv_send.at[step - 1],
            dkv_recv.at[step - 1],
            group_partner(step),
        )
        for step in range(1, GROUP)
    ]
    sc[5].near()
    sc[3].near()
    sc[4].near()
    sc[2].mid()
    sc[1].mid()
    sc[0].mid()
    sc[5].finish()
    sc[3].finish()
    sc[4].finish()
    sc[2].near()
    sc[1].near()
    sc[0].near()

    total = d_kv_low[mine, :].astype(F32)
    for step in range(GROUP - 1):
        dkv_copies[step].wait()
        total = total + kv_in[step].astype(F32)
    d_normed = d_normed_q + dot_nt(total.astype(BF16), kv_mat[...])
    d_normed = split_dot_nt(d_normed, pick[...])
    d_norm, _ = norm_back(d_normed, inputs, scale_one, gain_rows[0:1, :])
    input_grad[...] += d_norm
    sc[2].finish()
    sc[1].finish()
    sc[0].finish()


def finish_kernel(a0, a1, a2, b0, b1, b2, out, grad, block_out, input_grad, *outs):
    query, key, value, output, gate, up, down, norm_one, norm_two, heads = outs
    block_out[...] = out[...].astype(BF16)
    input_grad[...] = grad[...]

    def exact(order, block):
        return lax.dot_general(
            order,
            block,
            (((0,), (0,)), ((), ())),
            precision=lax.Precision.HIGHEST,
            preferred_element_type=F32,
        )

    def spread(ref, stacked, first, count):
        for c in range(count):
            ref[:, c * 128 : (c + 1) * 128] = stacked[(first + c) * 8 : (first + c) * 8 + 5]

    stacked = exact(mixed_order(), a1[...])
    spread(query, exact(query_order(), a0[...]) + stacked[32:], 0, 8)
    spread(key, stacked, 0, 2)
    spread(value, stacked, 2, 2)
    for c in range(5):
        output[:, c * 128 : (c + 1) * 128] = a2[c * 8 : (c + 1) * 8]
        down[:, c * 128 : (c + 1) * 128] = b2[c * 16 : (c + 1) * 16]
    order = wide_order()
    spread(gate, exact(order, b0[...]), 0, 16)
    spread(up, exact(order, b1[...]), 0, 16)
    row = a1[GAIN_ROW]
    norm_one[...] = row[0:5]
    norm_two[...] = row[5:10]
    heads[...] = row[10:14]


def vmem_specs(count):
    return [pl.BlockSpec(memory_space=pltpu.VMEM)] * count


def body(
    tokens,
    w_query,
    w_key,
    w_value,
    w_out,
    w_gate,
    w_up,
    w_down,
    attn_gain,
    ffn_gain,
    head_gains,
    lengths,
    cotangent,
):
    gains = jnp.concatenate([attn_gain, ffn_gain, head_gains]).astype(F32)
    gains = jnp.pad(gains[None, :], ((GAIN_ROW - 24, 31 - GAIN_ROW), (0, 114)))

    def low(*shape):
        return pltpu.VMEM(shape, BF16)

    def full(*shape):
        return pltpu.VMEM(shape, F32)

    streams = [rows for phase in ROWS for rows in phase]
    scratch = [low(2, 64, rows, 128) for rows in streams]
    scratch += [low(count, rows, 128) for count in (64, 48, 12, 3) for rows in streams]
    scratch += [low(D, 1024), low(D, 512), low(1024, D), low(D, FF), low(D, FF), low(FF, D)]
    scratch += [low(D, 1024), low(D, 512)]
    scratch += [low(256, 256), low(256, 256), low(D, D), low(512, 512)]
    scratch += [full(128, 128), full(8, D)]
    scratch += [full(KEYS, 128), full(KEYS, 128), full(TOK, KEYS)]
    scratch += [low(KEYS, D), full(KEYS, D), low(KEYS, D), low(TOK, D), full(TOK, D)]
    scratch += [full(TOK, 1024), full(KEYS, 512), low(H * TOK, HD), low(KEYS, 2 * HD)]
    scratch += [low(H * TOK, KEYS), full(H * TOK, HD), low(TOK, 1024), low(H * TOK, HD)]
    scratch += [low(H * TOK, KEYS), low(TOK, FF), low(TOK, FF), low(TOK, FF), full(TOK, D)]
    scratch += [low(KEYS, 2 * HD), low(GROUP - 1, TOK, 2 * HD), low(TOK, 1024)]
    dma = pltpu.SemaphoreType.DMA
    scratch += [dma((6, 13)), dma((6, 13)), dma((6, 13)), dma((6, 13))]
    scratch += [dma((7,)), dma((7,)), dma((7,)), dma((7,))]
    out, grad, *sums = pl.pallas_call(
        block_kernel,
        out_shape=[jax.ShapeDtypeStruct((TOK, D), F32)] * 2
        + [jax.ShapeDtypeStruct((rows, 128), F32) for phase in ROWS for rows in phase],
        in_specs=vmem_specs(2) + [pl.BlockSpec(memory_space=pltpu.SMEM)] + vmem_specs(8),
        out_specs=vmem_specs(8),
        scratch_shapes=scratch,
        compiler_params=pltpu.CompilerParams(
            collective_id=0, has_side_effects=True, vmem_limit_bytes=VMEM_BYTES
        ),
        name="block",
    )(
        tokens,
        cotangent,
        lengths,
        w_query,
        w_key,
        w_value,
        w_out,
        w_gate,
        w_up,
        w_down,
        gains,
    )
    shards = [
        jax.ShapeDtypeStruct(shape, F32)
        for shape in ((5, 1024), (5, 256), (5, 256), (8, D), (5, FF), (5, FF), (16, D))
    ]
    shards += [jax.ShapeDtypeStruct((count,), F32) for count in (5, 5, 4)]
    return pl.pallas_call(
        finish_kernel,
        out_shape=[jax.ShapeDtypeStruct((TOK, D), BF16), jax.ShapeDtypeStruct((TOK, D), F32)]
        + shards,
        in_specs=vmem_specs(8),
        out_specs=vmem_specs(12),
        name="finish",
    )(*sums, out, grad)


def solution(mesh):
    rows = P(("dp", "fsdp"), None)
    vector = P(("dp", "fsdp"))
    return jax.shard_map(
        body,
        mesh=mesh,
        in_specs=(rows,) * 8 + (vector,) * 3 + (P("dp", None), rows),
        out_specs=(rows,) * 9 + (vector,) * 3,
        check_vma=False,
    )
```

```python
import math

import jax
import jax.numpy as jnp
from jax import lax
from jax.experimental import pallas as pl
from jax.experimental.pallas import tpu as pltpu
from jax.sharding import PartitionSpec as P

H = 4
HD = 256
D = 640
FF = 2048
TOK = 128
GROUP = 8
KEYS = TOK * GROUP
EPS = 1e-05
ROPE_BASE = 1000000.0
NEG = -1e30
SCORE_SCALE = 1.0 / math.sqrt(HD)
F32 = jnp.float32
BF16 = jnp.bfloat16

MESH = pl.DeviceIdType.MESH
VMEM_BYTES = 60 * 1024 * 1024

ORDERS = ((0, 1, 2), (1, 2, 0), (2, 0, 1))
ROWS = ((32, 32, 48), (80, 80, 80))
GAIN_ROW = 28


def coords():
    dp = lax.axis_index("dp")
    fsdp = lax.axis_index("fsdp")
    return (fsdp // 2, (dp // 2) % 4, (dp // 8) * 2 + fsdp % 2, dp % 2)


def device(place):
    x, y, z, core = place
    return ((z // 2) * 8 + y * 2 + core, x * 2 + z % 2)


def shifted(place, axis, step):
    moved = list(place)
    moved[axis] = (place[axis] + step) % 4
    return tuple(moved)


def sibling(place):
    return place[:3] + (1 - place[3],)


def beside(place):
    x, y, z, core = place
    return (x, y, (z // 2) * 2 + (1 - z % 2), core)


def greet(place):
    partners = [device(shifted(place, axis, step)) for axis in range(3) for step in (1, 2, 3)]
    partners.append(device(sibling(place)))
    barrier = pltpu.get_barrier_semaphore()
    for partner in partners:
        pl.semaphore_signal(barrier, inc=1, device_id=partner, device_id_type=MESH)
    return lambda: pl.semaphore_wait(barrier, len(partners))


def remote(src, dst, send, recv, to):
    copy = pltpu.make_async_remote_copy(
        src_ref=src, dst_ref=dst, send_sem=send, recv_sem=recv, device_id=to, device_id_type=MESH
    )
    copy.start()
    return copy


class Gather:
    def __init__(self, place, s, buf, send, recv):
        self.place, self.buf, self.send, self.recv = place, buf, send, recv
        self.axes = ORDERS[s]
        self.at = tuple(place[axis] for axis in self.axes)
        self.sent, self.pair, self.kept = [], [], []

    def copy(self, slot, first, count, to, keep):
        ref = self.buf.at[self.place[3], pl.ds(first, count)]
        copy = remote(ref, ref, self.send.at[slot], self.recv.at[slot], device(to))
        keep.append(copy)

    def to_line(self, level, first, count):
        self.kept = []
        for step in (2, 1, 3):
            to = shifted(self.place, self.axes[level], step)
            self.copy(3 * level + step - 1, first, count, to, self.kept)
        self.sent += self.kept

    def arrive(self):
        for copy in self.kept:
            copy.wait_recv()

    def first(self):
        ka, kb, kc = self.at
        self.to_line(0, kc * 16 + kb * 4 + ka, 1)

    def second(self):
        self.arrive()
        ka, kb, kc = self.at
        self.to_line(1, kc * 16 + kb * 4, 4)

    def third(self):
        self.arrive()
        kc = self.at[2]
        self.to_line(2, kc * 16, 16)
        self.copy(9, kc * 16, 16, sibling(self.place), self.pair)

    def to_pair(self):
        kc = self.at[2]
        for step, copy in zip((2, 1, 3), self.kept):
            copy.wait_recv()
        for step in (1, 2, 3):
            self.copy(9 + step, (kc - step + 4) % 4 * 16, 16, sibling(self.place), self.pair)

    def finish(self):
        for copy in self.pair:
            copy.wait()
        for copy in self.sent:
            copy.wait_send()


def add_blocks(total, count, first, *others):
    def step(i, carry):
        value = total[first + i].astype(F32)
        for other in others:
            value = value + other(i).astype(F32)
        total[first + i] = value.astype(BF16)
        return carry

    lax.fori_loop(0, count, step, 0, unroll=4)


class Scatter:
    def __init__(self, place, s, buf, pair, far, mid, near, out, send, recv):
        self.place, self.buf, self.pair_in = place, buf, pair
        self.inbox, self.out = (near, mid, far), out
        self.send, self.recv = send, recv
        self.axes = ORDERS[s]
        self.at = tuple(place[axis] for axis in self.axes)
        self.own = buf.at[place[3]]
        self.sent, self.pairs, self.kept = [], {}, []

    def copy(self, slot, src, dst, to):
        copy = remote(src, dst, self.send.at[slot], self.recv.at[slot], device(to))
        self.sent.append(copy)
        return copy

    def to_pair(self):
        other = self.buf.at[1 - self.place[3]]
        for offset in (2, 1, 3, 0):
            rows = pl.ds((self.at[2] + offset) % 4 * 16, 16)
            self.pairs[offset] = self.copy(
                offset, other.at[rows], self.pair_in.at[rows], sibling(self.place)
            )

    def add_pair(self, offset):
        self.pairs[offset].wait_recv()
        start = (self.at[2] + offset) % 4 * 16
        add_blocks(self.own, 16, start, lambda i: self.pair_in[start + i])

    def to_line(self, level, base, size, prepare=None):
        inbox = self.inbox[level]
        self.kept = []
        for step in (2, 1, 3):
            if prepare is not None:
                prepare(step)
            first = base + (self.at[level] + step) % 4 * size
            copy = self.copy(
                4 + 3 * level + step - 1,
                self.own.at[pl.ds(first, size)],
                inbox.at[pl.ds((step - 1) * size, size)],
                shifted(self.place, self.axes[level], step),
            )
            self.kept.append(copy)

    def total(self, level, base, size):
        for copy in self.kept:
            copy.wait_recv()
        inbox = self.inbox[level]
        add_blocks(
            self.own,
            size,
            base + self.at[level] * size,
            *[lambda i, n=n: inbox[n * size + i] for n in range(3)],
        )

    def far(self):
        self.to_line(2, 0, 16, self.add_pair)

    def mid(self):
        self.add_pair(0)
        self.total(2, 0, 16)
        self.to_line(1, self.at[2] * 16, 4)

    def near(self):
        self.total(1, self.at[2] * 16, 4)
        self.to_line(0, self.at[2] * 16 + self.at[1] * 4, 1)

    def finish(self):
        for copy in self.kept:
            copy.wait_recv()
        ka, kb, kc = self.at
        value = self.own[kc * 16 + kb * 4 + ka].astype(F32)
        for step in range(3):
            value = value + self.inbox[0][step].astype(F32)
        self.out[...] = value
        for copy in self.sent:
            copy.wait_send()


class GroupGather:
    def __init__(self, place, me, buf, send, recv):
        self.place, self.me, self.buf, self.send, self.recv = place, me, buf, send, recv
        self.sent, self.along, self.across = [], [], []

    def copy(self, slot, ref, to, keep):
        copy = remote(ref, ref, self.send.at[slot], self.recv.at[slot], device(to))
        keep.append(copy)
        self.sent.append(copy)

    def half(self, member, bottom, count=1):
        rows = TOK // 2
        return self.buf.at[pl.ds(member, count), pl.ds(bottom * rows, rows)]

    def first(self):
        for step in (2, 1, 3):
            to = shifted(self.place, 0, step)
            self.copy(step - 1, self.half(self.me, 0), to, self.along)
        self.copy(3, self.half(self.me, 1), beside(self.place), self.across)
        self.copy(4, self.half(self.me, 0), beside(self.place), self.across)

    def second(self):
        x = self.place[0]
        self.across[0].wait_recv()
        for step in (2, 1, 3):
            to = shifted(self.place, 0, step)
            self.copy(7 + step, self.half(2 * x, 1, 2), to, self.across)
        for step, copy in zip((2, 1, 3), list(self.along)):
            copy.wait_recv()
            member = (x - step + 4) % 4 * 2 + self.me % 2
            self.copy(4 + step, self.half(member, 0), beside(self.place), self.across)

    def finish(self):
        for copy in self.across[1:]:
            copy.wait_recv()
        for copy in self.sent:
            copy.wait_send()


class GroupScatter:
    def __init__(self, place, buf, inbox, send, recv):
        self.place, self.buf, self.inbox, self.send, self.recv = place, buf, inbox, send, recv
        self.sent = []

    def copy(self, slot, src, dst, to):
        copy = remote(src, dst, self.send.at[slot], self.recv.at[slot], device(to))
        self.sent.append(copy)
        return copy

    def first(self):
        x, z = self.place[0], self.place[2] % 2
        by_x, by_z = self.inbox[0], self.inbox[1]
        half = TOK // 2
        self.along = [
            self.copy(
                step - 1,
                self.buf.at[pl.ds(0, 2), (x + step) % 4, pl.ds(0, half)],
                by_x.at[step - 1],
                shifted(self.place, 0, step),
            )
            for step in (2, 1, 3)
        ]
        self.across = self.copy(
            3, self.buf.at[1 - z, pl.ds(0, 4), pl.ds(half, half)], by_z, beside(self.place)
        )

    def second(self):
        x, z = self.place[0], self.place[2] % 2
        by_x, by_z, last_x, last_z = self.inbox
        half = TOK // 2
        top, bottom = pl.ds(0, half), pl.ds(half, half)
        self.across.wait_recv()
        for k in range(4):
            value = self.buf[z, k, bottom, :].astype(F32) + by_z[k].astype(F32)
            self.buf[z, k, bottom, :] = value.astype(BF16)
        self.last = [
            self.copy(
                3 + step,
                self.buf.at[z, (x + step) % 4, bottom],
                last_x.at[step - 1],
                shifted(self.place, 0, step),
            )
            for step in (2, 1, 3)
        ]
        for copy in self.along:
            copy.wait_recv()
        for k in range(2):
            value = self.buf[k, x, top, :].astype(F32)
            for step in range(3):
                value = value + by_x[step, k].astype(F32)
            self.buf[k, x, top, :] = value.astype(BF16)
        self.last.append(self.copy(7, self.buf.at[1 - z, x, top], last_z, beside(self.place)))

    def finish(self):
        x, z = self.place[0], self.place[2] % 2
        last_x, last_z = self.inbox[2:]
        half = TOK // 2
        for copy in self.last:
            copy.wait_recv()
        value = self.buf[z, x].astype(F32)
        upper = value[:half] + last_z[...].astype(F32)
        lower = value[half:]
        for step in range(3):
            lower = lower + last_x[step].astype(F32)
        for copy in self.sent:
            copy.wait_send()
        return jnp.concatenate([upper, lower], axis=0)


def one_hot(rows, columns, pick):
    i = lax.broadcasted_iota(jnp.int32, (rows, columns), 0)
    j = lax.broadcasted_iota(jnp.int32, (rows, columns), 1)
    return jnp.where(pick(i) == j, 1.0, 0.0)


def dot(left, right):
    return jnp.dot(left, right, preferred_element_type=F32)


def dot_nt(left, right):
    return lax.dot_general(left, right, (((1,), (1,)), ((), ())), preferred_element_type=F32)


def dot_tn(left, right):
    return lax.dot_general(left, right, (((0,), (0,)), ((), ())), preferred_element_type=F32)


def stack_columns(shard):
    r, columns = shard.shape
    value = shard.astype(F32)
    pad = [jnp.zeros((8 - r, 128), F32)] if r < 8 else []
    pieces = []
    for c in range(columns // 128):
        pieces += [value[:, c * 128 : (c + 1) * 128]] + pad
    return jnp.concatenate(pieces, axis=0)


def query_order():
    return one_hot(32, 64, lambda i: (i & 7) * 8 + (i >> 3))


def mixed_order():
    def pick(i):
        rest = jnp.where(i < 28, 32 + (i - 20) * 8 + 4, -1)
        return jnp.where(i < 20, (i & 3) * 8 + (i >> 2), rest)

    return one_hot(32, 96, pick)


def wide_order():
    return one_hot(80, 128, lambda i: (i & 15) * 8 + (i >> 4))


def block_index(s, g, d):
    z_hi, y = g // 4, g % 4
    core, x, z_lo = d // 8, (d // 2) % 4, d % 2
    place = (x, y, z_hi * 2 + z_lo)
    a, b, c = (place[axis] for axis in ORDERS[s])
    return core, c * 16 + b * 4 + a


def rms(value):
    return lax.rsqrt(jnp.mean(value * value, axis=-1, keepdims=True) + EPS)


def rotate(value, cosines, sines):
    half = HD // 2
    u, w = value[:, :half], value[:, half:]
    return jnp.concatenate([u * cosines - w * sines, w * cosines + u * sines], axis=1)


def norm_back(grad, value, scale, gain):
    scaled = grad * gain
    back = scale * scaled - value * scale**3 * jnp.mean(scaled * value, axis=-1, keepdims=True)
    return back, jnp.sum(grad * value * scale, axis=0, keepdims=True)


def split_dot_nt(value, matrix):
    high = value.astype(BF16)
    low = (value - high.astype(F32)).astype(BF16)
    return dot_nt(high, matrix) + dot_nt(low, matrix)


def block_kernel(
    tokens,
    cotangent,
    lengths,
    w_query,
    w_key,
    w_value,
    w_out,
    w_gate,
    w_up,
    w_down,
    gains,
    block_out,
    input_grad,
    sum_a0,
    sum_a1,
    sum_a2,
    sum_b0,
    sum_b1,
    sum_b2,
    a0,
    a1,
    a2,
    b0,
    b1,
    b2,
    *scratch,
):
    it = iter(scratch)

    def take(count):
        return [next(it) for _ in range(count)]

    pair_in, far_in, mid_in, near_in = take(6), take(6), take(6), take(6)
    q_mat, kv_mat, o_mat, g_mat, u_mat, d_mat, q_grad, kv_grad = take(8)
    perm, flip, pick, head_pick, gain_cols, gain_rows = take(6)
    cos_ref, sin_ref, allowed_ref = take(3)
    tok_all, scaled, normed, ffn_in, middle = take(5)
    q_raw, kv_raw, queries, kv_all = take(4)
    probs, attended, attended_low, d_attended, d_scores = take(5)
    hidden, d_gate, d_up, d_acc = take(4)
    d_kv_low, d_kv, d_q_low, *d_kv_in = take(7)
    gather_send, gather_recv, scatter_send, scatter_recv = take(4)
    tok_send, tok_recv, dkv_send, dkv_recv = take(4)

    place = coords()
    core = place[3]
    met = greet(place)
    me = lax.axis_index("fsdp")
    mine = pl.ds(pl.multiple_of(me * TOK, TOK), TOK)
    bufs = (a0, a1, a2, b0, b1, b2)
    outs = (sum_a0, sum_a1, sum_a2, sum_b0, sum_b1, sum_b2)

    def own_ref(n):
        ka, kb, kc = (place[axis] for axis in ORDERS[n % 3])
        return bufs[n].at[core, kc * 16 + kb * 4 + ka]

    query_stack = stack_columns(w_query[...]).astype(BF16)
    own_ref(0)[...] = dot(query_order().astype(BF16), query_stack).astype(BF16)
    mixed = jnp.concatenate(
        [
            stack_columns(w_key[...]).astype(BF16),
            stack_columns(w_value[...]).astype(BF16),
            query_stack,
        ],
        axis=0,
    )
    packed = dot(mixed_order().astype(BF16), mixed)
    own_ref(1)[...] = jnp.concatenate([packed[:24], packed[24:] + gains[...]], axis=0).astype(BF16)
    packed = jnp.concatenate([stack_columns(w_out[...]), jnp.zeros((8, 128), F32)], axis=0)
    own_ref(2)[...] = packed.astype(BF16)
    order = wide_order().astype(BF16)
    own_ref(3)[...] = dot(order, stack_columns(w_gate[...]).astype(BF16)).astype(BF16)
    own_ref(4)[...] = dot(order, stack_columns(w_up[...]).astype(BF16)).astype(BF16)
    down = w_down[...]
    own_ref(5)[...] = jnp.concatenate(
        [down[:, c * 128 : (c + 1) * 128] for c in range(5)], axis=0
    )
    tok_all[me] = tokens[...]

    ga = [
        Gather(place, n % 3, bufs[n], gather_send.at[n], gather_recv.at[n]) for n in range(6)
    ]
    sc = [
        Scatter(
            place,
            n % 3,
            bufs[n],
            pair_in[n],
            far_in[n],
            mid_in[n],
            near_in[n],
            outs[n],
            scatter_send.at[n],
            scatter_recv.at[n],
        )
        for n in range(6)
    ]
    tg = GroupGather(place, me, tok_all, tok_send, tok_recv)
    ds = GroupScatter(place, d_kv, d_kv_in, dkv_send, dkv_recv)
    met()
    for n in (1, 0, 2, 3, 4, 5):
        ga[n].first()
    tg.first()

    perm[...] = one_hot(256, 256, lambda i: (i & 15) * 16 + (i >> 4)).astype(BF16)
    flip[...] = one_hot(
        256, 256, lambda i: ((i & 127) >> 3) * 16 + (i >> 7) * 8 + (i & 7)
    ).astype(BF16)
    row = lax.broadcasted_iota(jnp.int32, (D, D), 0)
    column = lax.broadcasted_iota(jnp.int32, (D, D), 1)
    pick[...] = jnp.where(row == 5 * (column & 127) + (column >> 7), 1.0, 0.0).astype(BF16)
    row = lax.broadcasted_iota(jnp.int32, (2 * HD, 2 * HD), 0)
    column = lax.broadcasted_iota(jnp.int32, (2 * HD, 2 * HD), 1)
    head_pick[...] = jnp.where(row == 4 * (column & 127) + (column >> 7), 1.0, 0.0).astype(BF16)
    for n in (1, 0, 2, 3, 4, 5):
        ga[n].second()
    tg.second()
    first_len, second_len = lengths[0, 0], lengths[0, 1]
    first_end, second_end = first_len, first_len + second_len

    def segment(ids):
        past_one = jnp.where(ids >= first_end, 1, 0)
        past_two = jnp.where(ids >= second_end, 1, 0)
        return past_one + past_two, ids - past_one * first_len - past_two * second_len

    lane = lax.broadcasted_iota(jnp.int32, (TOK, HD // 2), 1).astype(F32)
    frequencies = jnp.exp(lane * (2.0 / HD) * (-math.log(ROPE_BASE)))

    def tables(m, carry):
        ids = m * TOK + lax.broadcasted_iota(jnp.int32, (TOK, HD // 2), 0)
        angles = segment(ids)[1].astype(F32) * frequencies
        rows = pl.ds(pl.multiple_of(m * TOK, TOK), TOK)
        cos_ref[rows, :] = jnp.cos(angles)
        sin_ref[rows, :] = jnp.sin(angles)
        return carry

    lax.fori_loop(0, GROUP, tables, 0)
    for n in (1, 0, 2, 3, 4, 5):
        ga[n].third()
    row_ids = me * TOK + lax.broadcasted_iota(jnp.int32, (TOK, KEYS), 0)
    key_ids = lax.broadcasted_iota(jnp.int32, (TOK, KEYS), 1)
    same = segment(row_ids)[0] == segment(key_ids)[0]
    allowed_ref[...] = jnp.where(same & (key_ids <= row_ids), 1.0, 0.0)
    inputs = tokens[...].astype(F32)
    scale_one = rms(inputs)
    tg.finish()

    def scale_tokens(m, carry):
        rows = pl.ds(pl.multiple_of(m * TOK, TOK), TOK)
        value = tok_all[m]
        scaled[rows, :] = dot(value, pick[...]) * rms(value.astype(F32))
        return carry

    lax.fori_loop(0, GROUP, scale_tokens, 0)
    for n in (1, 0):
        ga[n].to_pair()
    ga[1].finish()
    ga[0].finish()

    def slab(n, g, j):
        tiles = []
        for d in range(16):
            c, index = block_index(n % 3, g, d)
            tiles.append(bufs[n][c, index, pl.ds(j * 16, 16), :])
        return jnp.concatenate(tiles, axis=0)

    def turn(matrix, parts):
        out = dot(matrix, jnp.concatenate(parts, axis=1)).astype(BF16)
        return [out[:, i * 128 : (i + 1) * 128] for i in range(len(parts))]

    def tiles_wide(block, first, count):
        return jnp.concatenate(
            [block[(first + i) * 16 : (first + i + 1) * 16] for i in range(count)], axis=1
        )

    def unpack_a(g, carry):
        at = pl.ds(pl.multiple_of(g * 16, 16), 16)

        def rows(r):
            return pl.ds(pl.multiple_of(r * 128 + g * 16, 16), 16)

        kv0, kv1 = turn(perm[...], [slab(1, g, 0), slab(1, g, 1)])
        q0, q1 = turn(perm[...], [slab(0, g, 0), slab(0, g, 1)])
        for r, (block, first) in enumerate(((q0, 0), (q0, 8), (q1, 0), (q1, 8), (kv1, 4))):
            q_mat[rows(r), :] = tiles_wide(block, first, 8)
        gain_cols[at, :] = kv1[12 * 16 : 13 * 16].astype(F32)
        for r in range(4):
            kv_mat[rows(r), :] = tiles_wide(kv0, 4 * r, 4)
        kv_mat[rows(4), :] = tiles_wide(kv1, 0, 4)
        return carry

    lax.fori_loop(0, 8, unpack_a, 0)

    def unpack_out(g, carry):
        o0, o1 = turn(flip[...], [slab(2, g, 0), slab(2, g, 1)])
        (o2,) = turn(flip[...], [slab(2, g, 2)])
        o_mat[pl.ds(pl.multiple_of(g * 128, 128), 128), :] = jnp.concatenate(
            [o0[:128], o0[128:], o1[:128], o1[128:], o2[:128]], axis=1
        )
        return carry

    turned = gain_cols[...].T

    def by_column(first, count):
        return jnp.concatenate([turned[first + i : first + i + 1] for i in range(count)], axis=1)

    gain_rows[2:3, 0 : 2 * HD] = dot_nt(by_column(10, 4).astype(BF16), head_pick[...])

    key_gain = gain_rows[2:3, HD : 2 * HD]
    query_gain = gain_rows[2:3, 0:HD]
    turned_gain = by_column(0, 5)

    def keys_forward(m, carry):
        rows = pl.ds(pl.multiple_of(m * 256, 256), 256)
        normed_rows = (scaled[rows, :] * turned_gain).astype(BF16)
        normed[rows, :] = normed_rows
        raw = dot(normed_rows, kv_mat[...])
        kv_raw[rows, :] = raw
        key_raw = raw[:, 0:HD]
        key_rot = rotate(key_raw * rms(key_raw) * key_gain, cos_ref[rows, :], sin_ref[rows, :])
        kv_all[rows, :] = jnp.concatenate([key_rot, raw[:, HD:]], axis=1).astype(BF16)
        return carry

    lax.fori_loop(0, KEYS // 256, keys_forward, 0)
    cosines, sines = cos_ref[mine, :], sin_ref[mine, :]
    q_raw[...] = dot(normed[mine, :], q_mat[...])
    for h in range(H):
        raw = q_raw[:, h * HD : (h + 1) * HD]
        rot = rotate(raw * rms(raw) * query_gain, cosines, sines)
        queries[h * TOK : (h + 1) * TOK, :] = rot.astype(BF16)
    ga[2].to_pair()

    def attend(h, carry):
        rows = pl.ds(pl.multiple_of(h * TOK, TOK), TOK)
        allowed = allowed_ref[...]
        scores = dot_nt(queries[rows, :], kv_all[:, 0:HD]) * SCORE_SCALE
        scores = jnp.where(allowed > 0.0, scores, NEG)
        peak = jnp.max(scores, axis=-1, keepdims=True)
        expd = jnp.exp(scores - peak) * allowed
        low = (expd * (1.0 / jnp.sum(expd, axis=-1, keepdims=True))).astype(BF16)
        probs[rows, :] = low
        value = dot(low, kv_all[:, HD : 2 * HD])
        attended[rows, :] = value
        attended_low[:, pl.ds(pl.multiple_of(h * HD, HD), HD)] = value.astype(BF16)
        return carry

    lax.fori_loop(0, H, attend, 0)
    for n in (3, 4, 5):
        ga[n].to_pair()
    ga[2].finish()
    lax.fori_loop(0, 8, unpack_out, 0)
    gain_rows[0:1, :] = dot_nt(by_column(0, 5).astype(BF16), pick[...])
    gain_rows[1:2, :] = dot_nt(by_column(5, 5).astype(BF16), pick[...])
    middle[...] = inputs + dot(attended_low[...], o_mat[...])
    scale_two = rms(middle[...])
    ffn_nat = (middle[...] * scale_two * gain_rows[1:2, :]).astype(BF16)
    ffn_in[...] = dot(ffn_nat, pick[...]).astype(BF16)
    for n in (3, 4, 5):
        ga[n].finish()

    def unpack_b(g, carry):
        for mat, n in ((g_mat, 3), (u_mat, 4)):
            slabs = [slab(n, g, j) for j in range(5)]
            turned_slabs = turn(perm[...], slabs[0:2])
            turned_slabs += turn(perm[...], slabs[2:4])
            turned_slabs += turn(perm[...], slabs[4:5])
            for r in range(5):
                mat[pl.ds(pl.multiple_of(r * 128 + g * 16, 16), 16), :] = tiles_wide(
                    turned_slabs[r], 0, 16
                )
        for d in range(16):
            c, index = block_index(2, g, d)
            block = bufs[5][c, index]
            d_mat[pl.ds(pl.multiple_of(g * 256 + d * 16, 16), 16), :] = tiles_wide(block, 0, 5)
        return carry

    lax.fori_loop(0, 8, unpack_b, 0)

    block_out[...] = middle[...]
    d_acc[...] = jnp.zeros_like(d_acc)
    root = math.sqrt(2.0 / math.pi)

    def feed(n, carry):
        at = pl.ds(pl.multiple_of(n * 512, 512), 512)
        gate = dot(ffn_in[...], g_mat[:, at])
        up = dot(ffn_in[...], u_mat[:, at])
        d_hidden = dot_nt(cotangent[...], d_mat[at, :])
        square = gate * gate
        tanh = jnp.tanh(root * gate * (1.0 + 0.044715 * square))
        lift = 0.5 * (1.0 + tanh)
        act = gate * lift
        slope = lift + 0.5 * gate * (1.0 - tanh * tanh) * root * (1.0 + 3 * 0.044715 * square)
        hid = (act * up).astype(BF16)
        dg = (d_hidden * up * slope).astype(BF16)
        du = (d_hidden * act).astype(BF16)
        hidden[:, at] = hid
        d_gate[:, at] = dg
        d_up[:, at] = du
        block_out[...] += dot(hid, d_mat[at, :])
        d_acc[...] += dot_nt(dg, g_mat[:, at]) + dot_nt(du, u_mat[:, at])
        return carry

    lax.fori_loop(0, 4, feed, 0)

    def put(n, g, j, block):
        for d in range(16):
            c, index = block_index(n % 3, g, d)
            bufs[n][c, index, pl.ds(j * 16, 16), :] = block[d * 16 : (d + 1) * 16]

    def down_grads(g, carry):
        at = pl.ds(pl.multiple_of(g * 256, 256), 256)
        grad = dot_tn(hidden[:, at], cotangent[...]).astype(BF16)
        for d in range(16):
            c, index = block_index(2, g, d)
            rows = grad[d * 16 : (d + 1) * 16]
            bufs[5][c, index] = jnp.concatenate(
                [rows[:, i * 128 : (i + 1) * 128] for i in range(5)], axis=0
            )
        return carry

    def stack(grad, g, count):
        rows = grad[g * 16 : (g + 1) * 16]
        return [rows[:, i * 128 : (i + 1) * 128] for i in range(count)]

    def wide_grads(n, source):
        def step(r, carry):
            at = pl.ds(pl.multiple_of(r * 128, 128), 128)
            grad = dot_tn(ffn_in[:, at], source[...]).astype(BF16)
            for g in range(0, 8, 2):
                one, two = turn(
                    perm[...],
                    [jnp.concatenate(stack(grad, g + i, 16), axis=0) for i in range(2)],
                )
                put(n, g, r, one)
                put(n, g + 1, r, two)
            return carry

        lax.fori_loop(0, 5, step, 0)

    lax.fori_loop(0, 8, down_grads, 0)
    sc[5].to_pair()
    wide_grads(3, d_gate)
    sc[3].to_pair()
    sc[5].far()
    wide_grads(4, d_up)
    sc[4].to_pair()
    sc[3].far()

    d_ffn = split_dot_nt(d_acc[...], pick[...])
    d_norm, grad_two = norm_back(d_ffn, middle[...], scale_two, gain_rows[1:2, :])
    d_middle = cotangent[...].astype(F32) + d_norm
    input_grad[...] = d_middle
    d_branch = d_middle.astype(BF16)
    d_attended_flat = dot_nt(d_branch, o_mat[...]).astype(BF16)
    for h in range(H):
        d_attended[h * TOK : (h + 1) * TOK, :] = d_attended_flat[:, h * HD : (h + 1) * HD]
    sc[4].far()

    def out_grads(g, carry):
        at = pl.ds(pl.multiple_of(g * 128, 128), 128)
        grad = dot_tn(attended_low[:, at], d_branch).astype(BF16)
        cols = [grad[:, i * 128 : (i + 1) * 128] for i in range(5)]
        slabs = [
            jnp.concatenate(cols[0:2], axis=0),
            jnp.concatenate(cols[2:4], axis=0),
            jnp.concatenate([cols[4], jnp.zeros((128, 128), BF16)], axis=0),
        ]
        turned_back = dot_tn(flip[...], jnp.concatenate(slabs, axis=1)).astype(BF16)
        for j in range(3):
            put(2, g, j, turned_back[:, j * 128 : (j + 1) * 128])
        return carry

    lax.fori_loop(0, 8, out_grads, 0)
    sc[2].to_pair()

    def scores_back(h, carry):
        rows = pl.ds(pl.multiple_of(h * TOK, TOK), TOK)
        upstream = d_attended[rows, :]
        delta = jnp.sum(upstream.astype(F32) * attended[rows, :], axis=-1, keepdims=True)
        d_probs = dot_nt(upstream, kv_all[:, HD : 2 * HD])
        d_scores[rows, :] = (probs[rows, :].astype(F32) * (d_probs - delta)).astype(BF16)
        return carry

    lax.fori_loop(0, H, scores_back, 0)

    def keys_back(n, key_gain_grad):
        at = pl.ds(pl.multiple_of(n * 256, 256), 256)
        d_keys = dot_tn(d_scores[:, at], queries[...]) * SCORE_SCALE
        d_values = dot_tn(probs[:, at], d_attended[...])
        d_rot = rotate(d_keys, cos_ref[at, :], -sin_ref[at, :])
        raw = kv_raw[at, 0:HD]
        d_raw, gain_grad = norm_back(d_rot, raw, rms(raw), key_gain)
        low = jnp.concatenate([d_raw, d_values], axis=1).astype(BF16)
        d_kv_low[at, :] = low
        d_kv[0, n] = low[:TOK]
        d_kv[1, n] = low[TOK:]
        return key_gain_grad + gain_grad

    key_gain_grad = lax.fori_loop(0, KEYS // 256, keys_back, jnp.zeros((1, HD), F32))
    ds.first()
    sc[2].far()

    query_gain_grad = jnp.zeros((1, HD), F32)
    for h in range(H):
        rows = slice(h * TOK, (h + 1) * TOK)
        d_rot = dot(d_scores[rows, :], kv_all[:, 0:HD]) * SCORE_SCALE
        raw = q_raw[:, h * HD : (h + 1) * HD]
        d_raw, gain_grad = norm_back(
            rotate(d_rot, cosines, -sines), raw, rms(raw), query_gain
        )
        query_gain_grad = query_gain_grad + gain_grad
        d_q_low[:, h * HD : (h + 1) * HD] = d_raw.astype(BF16)
    kv_grad[...] = dot_tn(normed[...], d_kv_low[...]).astype(BF16)
    q_grad[...] = dot_tn(normed[mine, :], d_q_low[...]).astype(BF16)

    d_key_total = jnp.zeros((1, D), F32)
    d_normed_q = dot_nt(d_q_low[...], q_mat[...])

    def norm_one_grad(n, total):
        at = pl.ds(pl.multiple_of(n * 256, 256), 256)
        return total + jnp.sum(
            dot_nt(d_kv_low[at, :], kv_mat[...]) * scaled[at, :], axis=0, keepdims=True
        )

    grad_one = lax.fori_loop(0, KEYS // 256, norm_one_grad, d_key_total)
    grad_one = grad_one + jnp.sum(d_normed_q * scaled[mine, :], axis=0, keepdims=True)

    def by_device(row, count, matrix):
        turned_row = dot(row.astype(BF16), matrix)
        return [turned_row[:, i * 128 : (i + 1) * 128] for i in range(count)]

    heads = jnp.concatenate([query_gain_grad, key_gain_grad], axis=1)
    gain_parts = [grad_one[:, i * 128 : (i + 1) * 128] for i in range(5)]
    gain_parts += by_device(grad_two, 5, pick[...]) + by_device(heads, 4, head_pick[...])
    gain_parts.append(jnp.zeros((114, 128), F32))
    gain_cols[...] = jnp.concatenate(gain_parts, axis=0).T

    def grads_a(g, carry):
        at = pl.ds(pl.multiple_of(g * 16, 16), 16)
        q_tiles, kv_tiles = [], []
        for r in range(5):
            rows = pl.ds(pl.multiple_of(r * 128 + g * 16, 16), 16)
            q_row, kv_row = q_grad[rows, :], kv_grad[rows, :]
            q_tiles += [q_row[:, i * 128 : (i + 1) * 128] for i in range(8)]
            kv_tiles += [kv_row[:, i * 128 : (i + 1) * 128] for i in range(4)]
        kv_tiles += q_tiles[32:40] + [gain_cols[at, :].astype(BF16)]
        kv_tiles += [jnp.zeros((16, 128), BF16)] * 3
        slabs = [
            jnp.concatenate(tiles[i : i + 16], axis=0)
            for tiles in (q_tiles, kv_tiles)
            for i in (0, 16)
        ]
        out = turn(perm[...], slabs[0:2]) + turn(perm[...], slabs[2:4])
        for n in range(2):
            for j in range(2):
                put(n, g, j, out[2 * n + j])
        return carry

    lax.fori_loop(0, 8, grads_a, 0)
    sc[1].to_pair()
    sc[0].to_pair()
    sc[1].far()
    sc[0].far()
    ds.second()
    for n in (5, 3, 4, 2, 1, 0):
        sc[n].mid()
    for n in (5, 3, 4, 2, 1, 0):
        sc[n].near()

    total = ds.finish()
    d_normed = d_normed_q + dot_nt(total.astype(BF16), kv_mat[...])
    d_normed = split_dot_nt(d_normed, pick[...])
    d_norm, _ = norm_back(d_normed, inputs, scale_one, gain_rows[0:1, :])
    input_grad[...] += d_norm
    for n in (5, 3, 4, 2, 1, 0):
        sc[n].finish()


def finish_kernel(a0, a1, a2, b0, b1, b2, out, grad, block_out, input_grad, *outs):
    query, key, value, output, gate, up, down, norm_one, norm_two, heads = outs
    block_out[...] = out[...].astype(BF16)
    input_grad[...] = grad[...]

    def exact(order, block):
        return lax.dot_general(
            order,
            block,
            (((0,), (0,)), ((), ())),
            precision=lax.Precision.HIGHEST,
            preferred_element_type=F32,
        )

    def spread(ref, stacked, first, count):
        for c in range(count):
            ref[:, c * 128 : (c + 1) * 128] = stacked[(first + c) * 8 : (first + c) * 8 + 5]

    stacked = exact(mixed_order(), a1[...])
    spread(query, exact(query_order(), a0[...]) + stacked[32:], 0, 8)
    spread(key, stacked, 0, 2)
    spread(value, stacked, 2, 2)
    for c in range(5):
        output[:, c * 128 : (c + 1) * 128] = a2[c * 8 : (c + 1) * 8]
        down[:, c * 128 : (c + 1) * 128] = b2[c * 16 : (c + 1) * 16]
    order = wide_order()
    spread(gate, exact(order, b0[...]), 0, 16)
    spread(up, exact(order, b1[...]), 0, 16)
    row = a1[GAIN_ROW]
    norm_one[...] = row[0:5]
    norm_two[...] = row[5:10]
    heads[...] = row[10:14]


def vmem_specs(count):
    return [pl.BlockSpec(memory_space=pltpu.VMEM)] * count


def body(
    tokens,
    w_query,
    w_key,
    w_value,
    w_out,
    w_gate,
    w_up,
    w_down,
    attn_gain,
    ffn_gain,
    head_gains,
    lengths,
    cotangent,
):
    gains = jnp.concatenate([attn_gain, ffn_gain, head_gains]).astype(F32)
    gains = jnp.pad(gains[None, :], ((GAIN_ROW - 24, 31 - GAIN_ROW), (0, 114)))

    def low(*shape):
        return pltpu.VMEM(shape, BF16)

    def full(*shape):
        return pltpu.VMEM(shape, F32)

    streams = [rows for phase in ROWS for rows in phase]
    scratch = [low(2, 64, rows, 128) for rows in streams]
    scratch += [low(count, rows, 128) for count in (64, 48, 12, 3) for rows in streams]
    scratch += [low(D, 1024), low(D, 512), low(1024, D), low(D, FF), low(D, FF), low(FF, D)]
    scratch += [low(D, 1024), low(D, 512)]
    scratch += [low(256, 256), low(256, 256), low(D, D), low(512, 512)]
    scratch += [full(128, 128), full(8, D)]
    scratch += [full(KEYS, 128), full(KEYS, 128), full(TOK, KEYS)]
    scratch += [low(GROUP, TOK, D), full(KEYS, D), low(KEYS, D)]
    scratch += [low(TOK, D), full(TOK, D)]
    scratch += [full(TOK, 1024), full(KEYS, 512), low(H * TOK, HD), low(KEYS, 2 * HD)]
    scratch += [low(H * TOK, KEYS), full(H * TOK, HD), low(TOK, 1024), low(H * TOK, HD)]
    scratch += [low(H * TOK, KEYS), low(TOK, FF), low(TOK, FF), low(TOK, FF), full(TOK, D)]
    scratch += [low(KEYS, 2 * HD), low(2, 4, TOK, 2 * HD), low(TOK, 1024)]
    half = TOK // 2
    scratch += [low(3, 2, half, 2 * HD), low(4, half, 2 * HD)]
    scratch += [low(3, half, 2 * HD), low(half, 2 * HD)]
    dma = pltpu.SemaphoreType.DMA
    scratch += [dma((6, 13)), dma((6, 13)), dma((6, 13)), dma((6, 13))]
    scratch += [dma((11,)), dma((11,)), dma((8,)), dma((8,))]
    out, grad, *sums = pl.pallas_call(
        block_kernel,
        out_shape=[jax.ShapeDtypeStruct((TOK, D), F32)] * 2
        + [jax.ShapeDtypeStruct((rows, 128), F32) for phase in ROWS for rows in phase],
        in_specs=vmem_specs(2) + [pl.BlockSpec(memory_space=pltpu.SMEM)] + vmem_specs(8),
        out_specs=vmem_specs(8),
        scratch_shapes=scratch,
        compiler_params=pltpu.CompilerParams(
            collective_id=0, has_side_effects=True, vmem_limit_bytes=VMEM_BYTES
        ),
        name="block",
    )(
        tokens,
        cotangent,
        lengths,
        w_query,
        w_key,
        w_value,
        w_out,
        w_gate,
        w_up,
        w_down,
        gains,
    )
    shards = [
        jax.ShapeDtypeStruct(shape, F32)
        for shape in ((5, 1024), (5, 256), (5, 256), (8, D), (5, FF), (5, FF), (16, D))
    ]
    shards += [jax.ShapeDtypeStruct((count,), F32) for count in (5, 5, 4)]
    return pl.pallas_call(
        finish_kernel,
        out_shape=[jax.ShapeDtypeStruct((TOK, D), BF16), jax.ShapeDtypeStruct((TOK, D), F32)]
        + shards,
        in_specs=vmem_specs(8),
        out_specs=vmem_specs(12),
        name="finish",
    )(*sums, out, grad)


def solution(mesh):
    rows = P(("dp", "fsdp"), None)
    vector = P(("dp", "fsdp"))
    return jax.shard_map(
        body,
        mesh=mesh,
        in_specs=(rows,) * 8 + (vector,) * 3 + (P("dp", None), rows),
        out_specs=(rows,) * 9 + (vector,) * 3,
        check_vma=False,
    )
```

```python
import math

import jax
import jax.numpy as jnp
from jax import lax
from jax.experimental import pallas as pl
from jax.experimental.pallas import tpu as pltpu
from jax.sharding import PartitionSpec as P

H = 4
HD = 256
D = 640
FF = 2048
TOK = 128
GROUP = 8
KEYS = TOK * GROUP
EPS = 1e-05
ROPE_BASE = 1000000.0
NEG = -1e30
SCORE_SCALE = 1.0 / math.sqrt(HD)
F32 = jnp.float32
BF16 = jnp.bfloat16

MESH = pl.DeviceIdType.MESH
VMEM_BYTES = 60 * 1024 * 1024

ORDERS = ((0, 1, 2), (1, 2, 0), (2, 0, 1))
ROWS = ((32, 32, 48), (80, 80, 80))
GAIN_ROW = 28


def coords():
    dp = lax.axis_index("dp")
    fsdp = lax.axis_index("fsdp")
    return (fsdp // 2, (dp // 2) % 4, (dp // 8) * 2 + fsdp % 2, dp % 2)


def device(place):
    x, y, z, core = place
    return ((z // 2) * 8 + y * 2 + core, x * 2 + z % 2)


def shifted(place, axis, step):
    moved = list(place)
    moved[axis] = (place[axis] + step) % 4
    return tuple(moved)


def sibling(place):
    return place[:3] + (1 - place[3],)


def beside(place):
    x, y, z, core = place
    return (x, y, (z // 2) * 2 + (1 - z % 2), core)


def greet(place):
    partners = [device(shifted(place, axis, step)) for axis in range(3) for step in (1, 2, 3)]
    partners.append(device(sibling(place)))
    barrier = pltpu.get_barrier_semaphore()
    for partner in partners:
        pl.semaphore_signal(barrier, inc=1, device_id=partner, device_id_type=MESH)
    return lambda: pl.semaphore_wait(barrier, len(partners))


def remote(src, dst, send, recv, to):
    copy = pltpu.make_async_remote_copy(
        src_ref=src, dst_ref=dst, send_sem=send, recv_sem=recv, device_id=to, device_id_type=MESH
    )
    copy.start()
    return copy


class Gather:
    def __init__(self, place, s, buf, send, recv):
        self.place, self.buf, self.send, self.recv = place, buf, send, recv
        self.axes = ORDERS[s]
        self.at = tuple(place[axis] for axis in self.axes)
        self.sent, self.pair, self.kept = [], [], []

    def copy(self, slot, first, count, to, keep):
        ref = self.buf.at[self.place[3], pl.ds(first, count)]
        copy = remote(ref, ref, self.send.at[slot], self.recv.at[slot], device(to))
        keep.append(copy)

    def to_line(self, level, first, count):
        self.kept = []
        for step in (2, 1, 3):
            to = shifted(self.place, self.axes[level], step)
            self.copy(3 * level + step - 1, first, count, to, self.kept)
        self.sent += self.kept

    def arrive(self):
        for copy in self.kept:
            copy.wait_recv()

    def first(self):
        ka, kb, kc = self.at
        self.to_line(0, kc * 16 + kb * 4 + ka, 1)

    def second(self):
        self.arrive()
        ka, kb, kc = self.at
        self.to_line(1, kc * 16 + kb * 4, 4)

    def third(self):
        self.arrive()
        kc = self.at[2]
        self.to_line(2, kc * 16, 16)
        self.copy(9, kc * 16, 16, sibling(self.place), self.pair)

    def to_pair(self):
        kc = self.at[2]
        for step, copy in zip((2, 1, 3), self.kept):
            copy.wait_recv()
        for step in (1, 2, 3):
            self.copy(9 + step, (kc - step + 4) % 4 * 16, 16, sibling(self.place), self.pair)

    def finish(self):
        for copy in self.pair:
            copy.wait()
        for copy in self.sent:
            copy.wait_send()


def add_blocks(total, count, first, *others):
    def step(i, carry):
        value = total[first + i].astype(F32)
        for other in others:
            value = value + other(i).astype(F32)
        total[first + i] = value.astype(BF16)
        return carry

    lax.fori_loop(0, count, step, 0, unroll=4)


class Scatter:
    def __init__(self, place, s, buf, pair, far, mid, near, out, send, recv):
        self.place, self.buf, self.pair_in = place, buf, pair
        self.inbox, self.out = (near, mid, far), out
        self.send, self.recv = send, recv
        self.axes = ORDERS[s]
        self.at = tuple(place[axis] for axis in self.axes)
        self.own = buf.at[place[3]]
        self.sent, self.pairs, self.kept = [], {}, []

    def copy(self, slot, src, dst, to):
        copy = remote(src, dst, self.send.at[slot], self.recv.at[slot], device(to))
        self.sent.append(copy)
        return copy

    def to_pair(self):
        other = self.buf.at[1 - self.place[3]]
        for offset in (2, 1, 3, 0):
            rows = pl.ds((self.at[2] + offset) % 4 * 16, 16)
            self.pairs[offset] = self.copy(
                offset, other.at[rows], self.pair_in.at[rows], sibling(self.place)
            )

    def add_pair(self, offset):
        self.pairs[offset].wait_recv()
        start = (self.at[2] + offset) % 4 * 16
        add_blocks(self.own, 16, start, lambda i: self.pair_in[start + i])

    def to_line(self, level, base, size, prepare=None):
        inbox = self.inbox[level]
        self.kept = []
        for step in (2, 1, 3):
            if prepare is not None:
                prepare(step)
            first = base + (self.at[level] + step) % 4 * size
            copy = self.copy(
                4 + 3 * level + step - 1,
                self.own.at[pl.ds(first, size)],
                inbox.at[pl.ds((step - 1) * size, size)],
                shifted(self.place, self.axes[level], step),
            )
            self.kept.append(copy)

    def total(self, level, base, size):
        for copy in self.kept:
            copy.wait_recv()
        inbox = self.inbox[level]
        add_blocks(
            self.own,
            size,
            base + self.at[level] * size,
            *[lambda i, n=n: inbox[n * size + i] for n in range(3)],
        )

    def far(self):
        self.to_line(2, 0, 16, self.add_pair)

    def mid(self):
        self.add_pair(0)
        self.total(2, 0, 16)
        self.to_line(1, self.at[2] * 16, 4)

    def near(self):
        self.total(1, self.at[2] * 16, 4)
        self.to_line(0, self.at[2] * 16 + self.at[1] * 4, 1)

    def finish(self):
        for copy in self.kept:
            copy.wait_recv()
        ka, kb, kc = self.at
        value = self.own[kc * 16 + kb * 4 + ka].astype(F32)
        for step in range(3):
            value = value + self.inbox[0][step].astype(F32)
        self.out[...] = value
        for copy in self.sent:
            copy.wait_send()


class GroupGather:
    def __init__(self, place, me, buf, send, recv):
        self.place, self.me, self.buf, self.send, self.recv = place, me, buf, send, recv
        self.sent, self.along, self.across = [], [], []

    def copy(self, slot, ref, to, keep):
        copy = remote(ref, ref, self.send.at[slot], self.recv.at[slot], device(to))
        keep.append(copy)
        self.sent.append(copy)

    def half(self, member, bottom, count=1):
        rows = TOK // 2
        return self.buf.at[pl.ds(member, count), pl.ds(bottom * rows, rows)]

    def first(self):
        for step in (2, 1, 3):
            to = shifted(self.place, 0, step)
            self.copy(step - 1, self.half(self.me, 0), to, self.along)
        self.copy(3, self.half(self.me, 1), beside(self.place), self.across)
        self.copy(4, self.half(self.me, 0), beside(self.place), self.across)

    def second(self):
        x = self.place[0]
        self.across[0].wait_recv()
        for step in (2, 1, 3):
            to = shifted(self.place, 0, step)
            self.copy(7 + step, self.half(2 * x, 1, 2), to, self.across)
        for step, copy in zip((2, 1, 3), list(self.along)):
            copy.wait_recv()
            member = (x - step + 4) % 4 * 2 + self.me % 2
            self.copy(4 + step, self.half(member, 0), beside(self.place), self.across)

    def finish(self):
        for copy in self.across[1:]:
            copy.wait_recv()
        for copy in self.sent:
            copy.wait_send()


class GroupScatter:
    def __init__(self, place, buf, inbox, send, recv):
        self.place, self.buf, self.inbox, self.send, self.recv = place, buf, inbox, send, recv
        self.sent = []

    def copy(self, slot, src, dst, to):
        copy = remote(src, dst, self.send.at[slot], self.recv.at[slot], device(to))
        self.sent.append(copy)
        return copy

    def first(self):
        x, z = self.place[0], self.place[2] % 2
        by_x, by_z = self.inbox[0], self.inbox[1]
        half = TOK // 2
        self.along = [
            self.copy(
                step - 1,
                self.buf.at[pl.ds(0, 2), (x + step) % 4, pl.ds(0, half)],
                by_x.at[step - 1],
                shifted(self.place, 0, step),
            )
            for step in (2, 1, 3)
        ]
        self.across = self.copy(
            3, self.buf.at[1 - z, pl.ds(0, 4), pl.ds(half, half)], by_z, beside(self.place)
        )

    def second(self):
        x, z = self.place[0], self.place[2] % 2
        by_x, by_z, last_x, last_z = self.inbox
        half = TOK // 2
        top, bottom = pl.ds(0, half), pl.ds(half, half)
        self.across.wait_recv()
        for k in range(4):
            value = self.buf[z, k, bottom, :].astype(F32) + by_z[k].astype(F32)
            self.buf[z, k, bottom, :] = value.astype(BF16)
        self.last = [
            self.copy(
                3 + step,
                self.buf.at[z, (x + step) % 4, bottom],
                last_x.at[step - 1],
                shifted(self.place, 0, step),
            )
            for step in (2, 1, 3)
        ]
        for copy in self.along:
            copy.wait_recv()
        for k in range(2):
            value = self.buf[k, x, top, :].astype(F32)
            for step in range(3):
                value = value + by_x[step, k].astype(F32)
            self.buf[k, x, top, :] = value.astype(BF16)
        self.last.append(self.copy(7, self.buf.at[1 - z, x, top], last_z, beside(self.place)))

    def finish(self):
        x, z = self.place[0], self.place[2] % 2
        last_x, last_z = self.inbox[2:]
        half = TOK // 2
        for copy in self.last:
            copy.wait_recv()
        value = self.buf[z, x].astype(F32)
        upper = value[:half] + last_z[...].astype(F32)
        lower = value[half:]
        for step in range(3):
            lower = lower + last_x[step].astype(F32)
        for copy in self.sent:
            copy.wait_send()
        return jnp.concatenate([upper, lower], axis=0)


def one_hot(rows, columns, pick):
    i = lax.broadcasted_iota(jnp.int32, (rows, columns), 0)
    j = lax.broadcasted_iota(jnp.int32, (rows, columns), 1)
    return jnp.where(pick(i) == j, 1.0, 0.0)


def dot(left, right):
    return jnp.dot(left, right, preferred_element_type=F32)


def dot_nt(left, right):
    return lax.dot_general(left, right, (((1,), (1,)), ((), ())), preferred_element_type=F32)


def dot_tn(left, right):
    return lax.dot_general(left, right, (((0,), (0,)), ((), ())), preferred_element_type=F32)


def stack_columns(shard):
    r, columns = shard.shape
    value = shard.astype(F32)
    pad = [jnp.zeros((8 - r, 128), F32)] if r < 8 else []
    pieces = []
    for c in range(columns // 128):
        pieces += [value[:, c * 128 : (c + 1) * 128]] + pad
    return jnp.concatenate(pieces, axis=0)


def query_order():
    return one_hot(32, 64, lambda i: (i & 7) * 8 + (i >> 3))


def mixed_order():
    def pick(i):
        rest = jnp.where(i < 28, 32 + (i - 20) * 8 + 4, -1)
        return jnp.where(i < 20, (i & 3) * 8 + (i >> 2), rest)

    return one_hot(32, 96, pick)


def wide_order():
    return one_hot(80, 128, lambda i: (i & 15) * 8 + (i >> 4))


def block_index(s, g, d):
    z_hi, y = g // 4, g % 4
    core, x, z_lo = d // 8, (d // 2) % 4, d % 2
    place = (x, y, z_hi * 2 + z_lo)
    a, b, c = (place[axis] for axis in ORDERS[s])
    return core, c * 16 + b * 4 + a


def rms(value):
    return lax.rsqrt(jnp.mean(value * value, axis=-1, keepdims=True) + EPS)


def rotate(value, cosines, sines):
    half = HD // 2
    u, w = value[:, :half], value[:, half:]
    return jnp.concatenate([u * cosines - w * sines, w * cosines + u * sines], axis=1)


def norm_back(grad, value, scale, gain):
    scaled = grad * gain
    back = scale * scaled - value * scale**3 * jnp.mean(scaled * value, axis=-1, keepdims=True)
    return back, jnp.sum(grad * value * scale, axis=0, keepdims=True)


def split_dot_nt(value, matrix):
    high = value.astype(BF16)
    low = (value - high.astype(F32)).astype(BF16)
    return dot_nt(high, matrix) + dot_nt(low, matrix)


def block_kernel(
    tokens,
    cotangent,
    lengths,
    w_query,
    w_key,
    w_value,
    w_out,
    w_gate,
    w_up,
    w_down,
    gains,
    block_out,
    input_grad,
    sum_a0,
    sum_a1,
    sum_a2,
    sum_b0,
    sum_b1,
    sum_b2,
    a0,
    a1,
    a2,
    b0,
    b1,
    b2,
    *scratch,
):
    it = iter(scratch)

    def take(count):
        return [next(it) for _ in range(count)]

    pair_in, far_in, mid_in, near_in = take(6), take(6), take(6), take(6)
    q_mat, kv_mat, o_mat, g_mat, u_mat, d_mat, q_grad, kv_grad = take(8)
    perm, flip, pick, head_pick, gain_cols, gain_rows = take(6)
    cos_ref, sin_ref, allowed_ref = take(3)
    tok_all, scaled, normed, ffn_in, middle = take(5)
    q_raw, kv_raw, queries, kv_all = take(4)
    probs, attended, attended_low, d_attended, d_scores = take(5)
    hidden, d_gate, d_up, d_acc = take(4)
    d_kv_low, d_kv, d_q_low, *d_kv_in = take(7)
    gather_send, gather_recv, scatter_send, scatter_recv = take(4)
    tok_send, tok_recv, dkv_send, dkv_recv = take(4)

    place = coords()
    core = place[3]
    met = greet(place)
    me = lax.axis_index("fsdp")
    mine = pl.ds(pl.multiple_of(me * TOK, TOK), TOK)
    bufs = (a0, a1, a2, b0, b1, b2)
    outs = (sum_a0, sum_a1, sum_a2, sum_b0, sum_b1, sum_b2)

    def own_ref(n):
        ka, kb, kc = (place[axis] for axis in ORDERS[n % 3])
        return bufs[n].at[core, kc * 16 + kb * 4 + ka]

    query_stack = stack_columns(w_query[...]).astype(BF16)
    own_ref(0)[...] = dot(query_order().astype(BF16), query_stack).astype(BF16)
    mixed = jnp.concatenate(
        [
            stack_columns(w_key[...]).astype(BF16),
            stack_columns(w_value[...]).astype(BF16),
            query_stack,
        ],
        axis=0,
    )
    packed = dot(mixed_order().astype(BF16), mixed)
    own_ref(1)[...] = jnp.concatenate([packed[:24], packed[24:] + gains[...]], axis=0).astype(BF16)
    packed = jnp.concatenate([stack_columns(w_out[...]), jnp.zeros((8, 128), F32)], axis=0)
    own_ref(2)[...] = packed.astype(BF16)
    order = wide_order().astype(BF16)
    own_ref(3)[...] = dot(order, stack_columns(w_gate[...]).astype(BF16)).astype(BF16)
    own_ref(4)[...] = dot(order, stack_columns(w_up[...]).astype(BF16)).astype(BF16)
    down = w_down[...]
    own_ref(5)[...] = jnp.concatenate(
        [down[:, c * 128 : (c + 1) * 128] for c in range(5)], axis=0
    )
    tok_all[me] = tokens[...]

    ga = [
        Gather(place, n % 3, bufs[n], gather_send.at[n], gather_recv.at[n]) for n in range(6)
    ]
    sc = [
        Scatter(
            place,
            n % 3,
            bufs[n],
            pair_in[n],
            far_in[n],
            mid_in[n],
            near_in[n],
            outs[n],
            scatter_send.at[n],
            scatter_recv.at[n],
        )
        for n in range(6)
    ]
    tg = GroupGather(place, me, tok_all, tok_send, tok_recv)
    ds = GroupScatter(place, d_kv, d_kv_in, dkv_send, dkv_recv)
    met()
    for n in (1, 0, 2, 3, 4, 5):
        ga[n].first()
    tg.first()

    perm[...] = one_hot(256, 256, lambda i: (i & 15) * 16 + (i >> 4)).astype(BF16)
    flip[...] = one_hot(
        256, 256, lambda i: ((i & 127) >> 3) * 16 + (i >> 7) * 8 + (i & 7)
    ).astype(BF16)
    row = lax.broadcasted_iota(jnp.int32, (D, D), 0)
    column = lax.broadcasted_iota(jnp.int32, (D, D), 1)
    pick[...] = jnp.where(row == 5 * (column & 127) + (column >> 7), 1.0, 0.0).astype(BF16)
    row = lax.broadcasted_iota(jnp.int32, (2 * HD, 2 * HD), 0)
    column = lax.broadcasted_iota(jnp.int32, (2 * HD, 2 * HD), 1)
    head_pick[...] = jnp.where(row == 4 * (column & 127) + (column >> 7), 1.0, 0.0).astype(BF16)
    for n in (1, 0, 2, 3, 4, 5):
        ga[n].second()
    tg.second()
    first_len, second_len = lengths[0, 0], lengths[0, 1]
    first_end, second_end = first_len, first_len + second_len

    def segment(ids):
        past_one = jnp.where(ids >= first_end, 1, 0)
        past_two = jnp.where(ids >= second_end, 1, 0)
        return past_one + past_two, ids - past_one * first_len - past_two * second_len

    lane = lax.broadcasted_iota(jnp.int32, (TOK, HD // 2), 1).astype(F32)
    frequencies = jnp.exp(lane * (2.0 / HD) * (-math.log(ROPE_BASE)))

    def tables(m, carry):
        ids = m * TOK + lax.broadcasted_iota(jnp.int32, (TOK, HD // 2), 0)
        angles = segment(ids)[1].astype(F32) * frequencies
        rows = pl.ds(pl.multiple_of(m * TOK, TOK), TOK)
        cos_ref[rows, :] = jnp.cos(angles)
        sin_ref[rows, :] = jnp.sin(angles)
        return carry

    lax.fori_loop(0, GROUP, tables, 0, unroll=2)
    for n in (1, 0, 2, 3, 4, 5):
        ga[n].third()
    row_ids = me * TOK + lax.broadcasted_iota(jnp.int32, (TOK, KEYS), 0)
    key_ids = lax.broadcasted_iota(jnp.int32, (TOK, KEYS), 1)
    same = segment(row_ids)[0] == segment(key_ids)[0]
    allowed_ref[...] = jnp.where(same & (key_ids <= row_ids), 1.0, 0.0)
    inputs = tokens[...].astype(F32)
    scale_one = rms(inputs)
    tg.finish()

    def scale_tokens(m, carry):
        rows = pl.ds(pl.multiple_of(m * TOK, TOK), TOK)
        value = tok_all[m]
        scaled[rows, :] = dot(value, pick[...]) * rms(value.astype(F32))
        return carry

    lax.fori_loop(0, GROUP, scale_tokens, 0, unroll=2)
    for n in (1, 0):
        ga[n].to_pair()
    ga[1].finish()
    ga[0].finish()

    def slab(n, g, j):
        tiles = []
        for d in range(16):
            c, index = block_index(n % 3, g, d)
            tiles.append(bufs[n][c, index, pl.ds(j * 16, 16), :])
        return jnp.concatenate(tiles, axis=0)

    def turn(matrix, parts):
        out = dot(matrix, jnp.concatenate(parts, axis=1)).astype(BF16)
        return [out[:, i * 128 : (i + 1) * 128] for i in range(len(parts))]

    def tiles_wide(block, first, count):
        return jnp.concatenate(
            [block[(first + i) * 16 : (first + i + 1) * 16] for i in range(count)], axis=1
        )

    def unpack_a(g, carry):
        at = pl.ds(pl.multiple_of(g * 16, 16), 16)

        def rows(r):
            return pl.ds(pl.multiple_of(r * 128 + g * 16, 16), 16)

        kv0, kv1 = turn(perm[...], [slab(1, g, 0), slab(1, g, 1)])
        q0, q1 = turn(perm[...], [slab(0, g, 0), slab(0, g, 1)])
        for r, (block, first) in enumerate(((q0, 0), (q0, 8), (q1, 0), (q1, 8), (kv1, 4))):
            q_mat[rows(r), :] = tiles_wide(block, first, 8)
        gain_cols[at, :] = kv1[12 * 16 : 13 * 16].astype(F32)
        for r in range(4):
            kv_mat[rows(r), :] = tiles_wide(kv0, 4 * r, 4)
        kv_mat[rows(4), :] = tiles_wide(kv1, 0, 4)
        return carry

    lax.fori_loop(0, 8, unpack_a, 0, unroll=8)

    def unpack_out(g, carry):
        o0, o1 = turn(flip[...], [slab(2, g, 0), slab(2, g, 1)])
        (o2,) = turn(flip[...], [slab(2, g, 2)])
        o_mat[pl.ds(pl.multiple_of(g * 128, 128), 128), :] = jnp.concatenate(
            [o0[:128], o0[128:], o1[:128], o1[128:], o2[:128]], axis=1
        )
        return carry

    turned = gain_cols[...].T

    def by_column(first, count):
        return jnp.concatenate([turned[first + i : first + i + 1] for i in range(count)], axis=1)

    gain_rows[2:3, 0 : 2 * HD] = dot_nt(by_column(10, 4).astype(BF16), head_pick[...])

    key_gain = gain_rows[2:3, HD : 2 * HD]
    query_gain = gain_rows[2:3, 0:HD]
    turned_gain = by_column(0, 5)

    def keys_forward(m, carry):
        rows = pl.ds(pl.multiple_of(m * 256, 256), 256)
        normed_rows = (scaled[rows, :] * turned_gain).astype(BF16)
        normed[rows, :] = normed_rows
        raw = dot(normed_rows, kv_mat[...])
        kv_raw[rows, :] = raw
        key_raw = raw[:, 0:HD]
        key_rot = rotate(key_raw * rms(key_raw) * key_gain, cos_ref[rows, :], sin_ref[rows, :])
        kv_all[rows, :] = jnp.concatenate([key_rot, raw[:, HD:]], axis=1).astype(BF16)
        return carry

    lax.fori_loop(0, KEYS // 256, keys_forward, 0, unroll=4)
    cosines, sines = cos_ref[mine, :], sin_ref[mine, :]
    q_raw[...] = dot(normed[mine, :], q_mat[...])
    for h in range(H):
        raw = q_raw[:, h * HD : (h + 1) * HD]
        rot = rotate(raw * rms(raw) * query_gain, cosines, sines)
        queries[h * TOK : (h + 1) * TOK, :] = rot.astype(BF16)
    for n in (2, 3, 4, 5):
        ga[n].to_pair()

    def attend(h, carry):
        rows = pl.ds(pl.multiple_of(h * TOK, TOK), TOK)
        allowed = allowed_ref[...]
        scores = dot_nt(queries[rows, :], kv_all[:, 0:HD]) * SCORE_SCALE
        scores = jnp.where(allowed > 0.0, scores, NEG)
        peak = jnp.max(scores, axis=-1, keepdims=True)
        expd = jnp.exp(scores - peak) * allowed
        low = (expd * (1.0 / jnp.sum(expd, axis=-1, keepdims=True))).astype(BF16)
        probs[rows, :] = low
        value = dot(low, kv_all[:, HD : 2 * HD])
        attended[rows, :] = value
        attended_low[:, pl.ds(pl.multiple_of(h * HD, HD), HD)] = value.astype(BF16)
        return carry

    lax.fori_loop(0, H, attend, 0, unroll=4)
    ga[2].finish()
    lax.fori_loop(0, 8, unpack_out, 0, unroll=8)
    gain_rows[0:1, :] = dot_nt(by_column(0, 5).astype(BF16), pick[...])
    gain_rows[1:2, :] = dot_nt(by_column(5, 5).astype(BF16), pick[...])
    middle[...] = inputs + dot(attended_low[...], o_mat[...])
    scale_two = rms(middle[...])
    ffn_nat = (middle[...] * scale_two * gain_rows[1:2, :]).astype(BF16)
    ffn_in[...] = dot(ffn_nat, pick[...]).astype(BF16)
    for n in (3, 4, 5):
        ga[n].finish()

    def unpack_b(g, carry):
        for mat, n in ((g_mat, 3), (u_mat, 4)):
            slabs = [slab(n, g, j) for j in range(5)]
            turned_slabs = turn(perm[...], slabs[0:2])
            turned_slabs += turn(perm[...], slabs[2:4])
            turned_slabs += turn(perm[...], slabs[4:5])
            for r in range(5):
                mat[pl.ds(pl.multiple_of(r * 128 + g * 16, 16), 16), :] = tiles_wide(
                    turned_slabs[r], 0, 16
                )
        for d in range(16):
            c, index = block_index(2, g, d)
            block = bufs[5][c, index]
            d_mat[pl.ds(pl.multiple_of(g * 256 + d * 16, 16), 16), :] = tiles_wide(block, 0, 5)
        return carry

    lax.fori_loop(0, 8, unpack_b, 0, unroll=8)

    block_out[...] = middle[...]
    d_acc[...] = jnp.zeros_like(d_acc)
    root = math.sqrt(2.0 / math.pi)

    def feed(n, carry):
        at = pl.ds(pl.multiple_of(n * 512, 512), 512)
        gate = dot(ffn_in[...], g_mat[:, at])
        up = dot(ffn_in[...], u_mat[:, at])
        d_hidden = dot_nt(cotangent[...], d_mat[at, :])
        square = gate * gate
        tanh = jnp.tanh(root * gate * (1.0 + 0.044715 * square))
        lift = 0.5 * (1.0 + tanh)
        act = gate * lift
        slope = lift + 0.5 * gate * (1.0 - tanh * tanh) * root * (1.0 + 3 * 0.044715 * square)
        hid = (act * up).astype(BF16)
        dg = (d_hidden * up * slope).astype(BF16)
        du = (d_hidden * act).astype(BF16)
        hidden[:, at] = hid
        d_gate[:, at] = dg
        d_up[:, at] = du
        block_out[...] += dot(hid, d_mat[at, :])
        d_acc[...] += dot_nt(dg, g_mat[:, at]) + dot_nt(du, u_mat[:, at])
        return carry

    lax.fori_loop(0, 4, feed, 0, unroll=2)

    def put(n, g, j, block):
        for d in range(16):
            c, index = block_index(n % 3, g, d)
            bufs[n][c, index, pl.ds(j * 16, 16), :] = block[d * 16 : (d + 1) * 16]

    def down_grads(g, carry):
        at = pl.ds(pl.multiple_of(g * 256, 256), 256)
        grad = dot_tn(hidden[:, at], cotangent[...]).astype(BF16)
        for d in range(16):
            c, index = block_index(2, g, d)
            rows = grad[d * 16 : (d + 1) * 16]
            bufs[5][c, index] = jnp.concatenate(
                [rows[:, i * 128 : (i + 1) * 128] for i in range(5)], axis=0
            )
        return carry

    def stack(grad, g, count):
        rows = grad[g * 16 : (g + 1) * 16]
        return [rows[:, i * 128 : (i + 1) * 128] for i in range(count)]

    def wide_grads(n, source):
        def loop_r(r, carry):
            at = pl.ds(pl.multiple_of(r * 128, 128), 128)
            grad = dot_tn(ffn_in[:, at], source[...]).astype(BF16)
            for g in range(0, 8, 2):
                one, two = turn(
                    perm[...],
                    [jnp.concatenate(stack(grad, g + i, 16), axis=0) for i in range(2)],
                )
                put(n, g, r, one)
                put(n, g + 1, r, two)
            return carry

        lax.fori_loop(0, 5, loop_r, 0, unroll=5)

    lax.fori_loop(0, 8, down_grads, 0, unroll=8)
    sc[5].to_pair()
    wide_grads(3, d_gate)
    sc[3].to_pair()
    sc[5].far()
    wide_grads(4, d_up)
    sc[4].to_pair()
    sc[3].far()

    d_ffn = split_dot_nt(d_acc[...], pick[...])
    d_norm, grad_two = norm_back(d_ffn, middle[...], scale_two, gain_rows[1:2, :])
    d_middle = cotangent[...].astype(F32) + d_norm
    input_grad[...] = d_middle
    d_branch = d_middle.astype(BF16)
    d_attended_flat = dot_nt(d_branch, o_mat[...]).astype(BF16)
    for h in range(H):
        d_attended[h * TOK : (h + 1) * TOK, :] = d_attended_flat[:, h * HD : (h + 1) * HD]
    sc[4].far()

    def out_grads(g, carry):
        at = pl.ds(pl.multiple_of(g * 128, 128), 128)
        grad = dot_tn(attended_low[:, at], d_branch).astype(BF16)
        cols = [grad[:, i * 128 : (i + 1) * 128] for i in range(5)]
        slabs = [
            jnp.concatenate(cols[0:2], axis=0),
            jnp.concatenate(cols[2:4], axis=0),
            jnp.concatenate([cols[4], jnp.zeros((128, 128), BF16)], axis=0),
        ]
        turned_back = dot_tn(flip[...], jnp.concatenate(slabs, axis=1)).astype(BF16)
        for j in range(3):
            put(2, g, j, turned_back[:, j * 128 : (j + 1) * 128])
        return carry

    lax.fori_loop(0, 8, out_grads, 0, unroll=8)
    sc[2].to_pair()

    def scores_back(h, carry):
        rows = pl.ds(pl.multiple_of(h * TOK, TOK), TOK)
        upstream = d_attended[rows, :]
        delta = jnp.sum(upstream.astype(F32) * attended[rows, :], axis=-1, keepdims=True)
        d_probs = dot_nt(upstream, kv_all[:, HD : 2 * HD])
        d_scores[rows, :] = (probs[rows, :].astype(F32) * (d_probs - delta)).astype(BF16)
        return carry

    lax.fori_loop(0, H, scores_back, 0, unroll=4)

    def keys_back(n, key_gain_grad):
        at = pl.ds(pl.multiple_of(n * 256, 256), 256)
        d_keys = dot_tn(d_scores[:, at], queries[...]) * SCORE_SCALE
        d_values = dot_tn(probs[:, at], d_attended[...])
        d_rot = rotate(d_keys, cos_ref[at, :], -sin_ref[at, :])
        raw = kv_raw[at, 0:HD]
        d_raw, gain_grad = norm_back(d_rot, raw, rms(raw), key_gain)
        low = jnp.concatenate([d_raw, d_values], axis=1).astype(BF16)
        d_kv_low[at, :] = low
        d_kv[0, n] = low[:TOK]
        d_kv[1, n] = low[TOK:]
        return key_gain_grad + gain_grad

    key_gain_grad = lax.fori_loop(0, KEYS // 256, keys_back, jnp.zeros((1, HD), F32), unroll=4)
    ds.first()
    sc[2].far()

    query_gain_grad = jnp.zeros((1, HD), F32)
    for h in range(H):
        rows = slice(h * TOK, (h + 1) * TOK)
        d_rot = dot(d_scores[rows, :], kv_all[:, 0:HD]) * SCORE_SCALE
        raw = q_raw[:, h * HD : (h + 1) * HD]
        d_raw, gain_grad = norm_back(
            rotate(d_rot, cosines, -sines), raw, rms(raw), query_gain
        )
        query_gain_grad = query_gain_grad + gain_grad
        d_q_low[:, h * HD : (h + 1) * HD] = d_raw.astype(BF16)
    kv_grad[...] = dot_tn(normed[...], d_kv_low[...]).astype(BF16)
    q_grad[...] = dot_tn(normed[mine, :], d_q_low[...]).astype(BF16)

    d_key_total = jnp.zeros((1, D), F32)
    d_normed_q = dot_nt(d_q_low[...], q_mat[...])

    def norm_one_grad(n, total):
        at = pl.ds(pl.multiple_of(n * 256, 256), 256)
        return total + jnp.sum(
            dot_nt(d_kv_low[at, :], kv_mat[...]) * scaled[at, :], axis=0, keepdims=True
        )

    grad_one = lax.fori_loop(0, KEYS // 256, norm_one_grad, d_key_total, unroll=4)
    grad_one = grad_one + jnp.sum(d_normed_q * scaled[mine, :], axis=0, keepdims=True)

    def by_device(row, count, matrix):
        turned_row = dot(row.astype(BF16), matrix)
        return [turned_row[:, i * 128 : (i + 1) * 128] for i in range(count)]

    heads = jnp.concatenate([query_gain_grad, key_gain_grad], axis=1)
    gain_parts = [grad_one[:, i * 128 : (i + 1) * 128] for i in range(5)]
    gain_parts += by_device(grad_two, 5, pick[...]) + by_device(heads, 4, head_pick[...])
    gain_parts.append(jnp.zeros((114, 128), F32))
    gain_cols[...] = jnp.concatenate(gain_parts, axis=0).T

    def grads_a(g, carry):
        at = pl.ds(pl.multiple_of(g * 16, 16), 16)
        q_tiles, kv_tiles = [], []
        for r in range(5):
            rows = pl.ds(pl.multiple_of(r * 128 + g * 16, 16), 16)
            q_row, kv_row = q_grad[rows, :], kv_grad[rows, :]
            q_tiles += [q_row[:, i * 128 : (i + 1) * 128] for i in range(8)]
            kv_tiles += [kv_row[:, i * 128 : (i + 1) * 128] for i in range(4)]
        kv_tiles += q_tiles[32:40] + [gain_cols[at, :].astype(BF16)]
        kv_tiles += [jnp.zeros((16, 128), BF16)] * 3
        slabs = [
            jnp.concatenate(tiles[i : i + 16], axis=0)
            for tiles in (q_tiles, kv_tiles)
            for i in (0, 16)
        ]
        out = turn(perm[...], slabs[0:2]) + turn(perm[...], slabs[2:4])
        for n in range(2):
            for j in range(2):
                put(n, g, j, out[2 * n + j])
        return carry

    lax.fori_loop(0, 8, grads_a, 0, unroll=8)
    sc[1].to_pair()
    sc[0].to_pair()
    sc[1].far()
    sc[0].far()
    ds.second()
    for n in (5, 3, 4, 2, 1, 0):
        sc[n].mid()
    for n in (5, 3, 4, 2, 1, 0):
        sc[n].near()

    total = ds.finish()
    d_normed = d_normed_q + dot_nt(total.astype(BF16), kv_mat[...])
    d_normed = split_dot_nt(d_normed, pick[...])
    d_norm, _ = norm_back(d_normed, inputs, scale_one, gain_rows[0:1, :])
    input_grad[...] += d_norm
    for n in (5, 3, 4, 2, 1, 0):
        sc[n].finish()


def finish_kernel(a0, a1, a2, b0, b1, b2, out, grad, block_out, input_grad, *outs):
    query, key, value, output, gate, up, down, norm_one, norm_two, heads = outs
    block_out[...] = out[...].astype(BF16)
    input_grad[...] = grad[...]

    def exact(order, block):
        return lax.dot_general(
            order,
            block,
            (((0,), (0,)), ((), ())),
            precision=lax.Precision.HIGHEST,
            preferred_element_type=F32,
        )

    def spread(ref, stacked, first, count):
        for c in range(count):
            ref[:, c * 128 : (c + 1) * 128] = stacked[(first + c) * 8 : (first + c) * 8 + 5]

    stacked = exact(mixed_order(), a1[...])
    spread(query, exact(query_order(), a0[...]) + stacked[32:], 0, 8)
    spread(key, stacked, 0, 2)
    spread(value, stacked, 2, 2)
    for c in range(5):
        output[:, c * 128 : (c + 1) * 128] = a2[c * 8 : (c + 1) * 8]
        down[:, c * 128 : (c + 1) * 128] = b2[c * 16 : (c + 1) * 16]
    order = wide_order()
    spread(gate, exact(order, b0[...]), 0, 16)
    spread(up, exact(order, b1[...]), 0, 16)
    row = a1[GAIN_ROW]
    norm_one[...] = row[0:5]
    norm_two[...] = row[5:10]
    heads[...] = row[10:14]


def vmem_specs(count):
    return [pl.BlockSpec(memory_space=pltpu.VMEM)] * count


def body(
    tokens,
    w_query,
    w_key,
    w_value,
    w_out,
    w_gate,
    w_up,
    w_down,
    attn_gain,
    ffn_gain,
    head_gains,
    lengths,
    cotangent,
):
    gains = jnp.concatenate([attn_gain, ffn_gain, head_gains]).astype(F32)
    gains = jnp.pad(gains[None, :], ((GAIN_ROW - 24, 31 - GAIN_ROW), (0, 114)))

    def low(*shape):
        return pltpu.VMEM(shape, BF16)

    def full(*shape):
        return pltpu.VMEM(shape, F32)

    streams = [rows for phase in ROWS for rows in phase]
    scratch = [low(2, 64, rows, 128) for rows in streams]
    scratch += [low(count, rows, 128) for count in (64, 48, 12, 3) for rows in streams]
    scratch += [low(D, 1024), low(D, 512), low(1024, D), low(D, FF), low(D, FF), low(FF, D)]
    scratch += [low(D, 1024), low(D, 512)]
    scratch += [low(256, 256), low(256, 256), low(D, D), low(512, 512)]
    scratch += [full(128, 128), full(8, D)]
    scratch += [full(KEYS, 128), full(KEYS, 128), full(TOK, KEYS)]
    scratch += [low(GROUP, TOK, D), full(KEYS, D), low(KEYS, D)]
    scratch += [low(TOK, D), full(TOK, D)]
    scratch += [full(TOK, 1024), full(KEYS, 512), low(H * TOK, HD), low(KEYS, 2 * HD)]
    scratch += [low(H * TOK, KEYS), full(H * TOK, HD), low(TOK, 1024), low(H * TOK, HD)]
    scratch += [low(H * TOK, KEYS), low(TOK, FF), low(TOK, FF), low(TOK, FF), full(TOK, D)]
    scratch += [low(KEYS, 2 * HD), low(2, 4, TOK, 2 * HD), low(TOK, 1024)]
    half = TOK // 2
    scratch += [low(3, 2, half, 2 * HD), low(4, half, 2 * HD)]
    scratch += [low(3, half, 2 * HD), low(half, 2 * HD)]
    dma = pltpu.SemaphoreType.DMA
    scratch += [dma((6, 13)), dma((6, 13)), dma((6, 13)), dma((6, 13))]
    scratch += [dma((11,)), dma((11,)), dma((8,)), dma((8,))]
    out, grad, *sums = pl.pallas_call(
        block_kernel,
        out_shape=[jax.ShapeDtypeStruct((TOK, D), F32)] * 2
        + [jax.ShapeDtypeStruct((rows, 128), F32) for phase in ROWS for rows in phase],
        in_specs=vmem_specs(2) + [pl.BlockSpec(memory_space=pltpu.SMEM)] + vmem_specs(8),
        out_specs=vmem_specs(8),
        scratch_shapes=scratch,
        compiler_params=pltpu.CompilerParams(
            collective_id=0, has_side_effects=True, vmem_limit_bytes=VMEM_BYTES
        ),
        name="block",
    )(
        tokens,
        cotangent,
        lengths,
        w_query,
        w_key,
        w_value,
        w_out,
        w_gate,
        w_up,
        w_down,
        gains,
    )
    shards = [
        jax.ShapeDtypeStruct(shape, F32)
        for shape in ((5, 1024), (5, 256), (5, 256), (8, D), (5, FF), (5, FF), (16, D))
    ]
    shards += [jax.ShapeDtypeStruct((count,), F32) for count in (5, 5, 4)]
    return pl.pallas_call(
        finish_kernel,
        out_shape=[jax.ShapeDtypeStruct((TOK, D), BF16), jax.ShapeDtypeStruct((TOK, D), F32)]
        + shards,
        in_specs=vmem_specs(8),
        out_specs=vmem_specs(12),
        name="finish",
    )(*sums, out, grad)


def solution(mesh):
    rows = P(("dp", "fsdp"), None)
    vector = P(("dp", "fsdp"))
    return jax.shard_map(
        body,
        mesh=mesh,
        in_specs=(rows,) * 8 + (vector,) * 3 + (P("dp", None), rows),
        out_specs=(rows,) * 9 + (vector,) * 3,
        check_vma=False,
    )
```

```python
import math

import jax
import jax.numpy as jnp
from jax import lax
from jax.experimental import pallas as pl
from jax.experimental.pallas import tpu as pltpu
from jax.sharding import PartitionSpec as P

H = 4
HD = 256
D = 640
FF = 2048
TOK = 128
GROUP = 8
KEYS = TOK * GROUP
EPS = 1e-05
ROPE_BASE = 1000000.0
NEG = -1e30
SCORE_SCALE = 1.0 / math.sqrt(HD)
F32 = jnp.float32
BF16 = jnp.bfloat16

MESH = pl.DeviceIdType.MESH
VMEM_BYTES = 60 * 1024 * 1024

ORDERS = ((0, 1, 2), (1, 2, 0), (2, 0, 1))
ROWS = ((32, 32, 48), (80, 80, 80))
GAIN_ROW = 28


def coords():
    dp = lax.axis_index("dp")
    fsdp = lax.axis_index("fsdp")
    return (fsdp // 2, (dp // 2) % 4, (dp // 8) * 2 + fsdp % 2, dp % 2)


def device(place):
    x, y, z, core = place
    return ((z // 2) * 8 + y * 2 + core, x * 2 + z % 2)


def shifted(place, axis, step):
    moved = list(place)
    moved[axis] = (place[axis] + step) % 4
    return tuple(moved)


def sibling(place):
    return place[:3] + (1 - place[3],)


def beside(place):
    x, y, z, core = place
    return (x, y, (z // 2) * 2 + (1 - z % 2), core)


def greet(place):
    partners = [device(shifted(place, axis, step)) for axis in range(3) for step in (1, 2, 3)]
    partners.append(device(sibling(place)))
    barrier = pltpu.get_barrier_semaphore()
    for partner in partners:
        pl.semaphore_signal(barrier, inc=1, device_id=partner, device_id_type=MESH)
    return lambda: pl.semaphore_wait(barrier, len(partners))


def remote(src, dst, send, recv, to):
    copy = pltpu.make_async_remote_copy(
        src_ref=src, dst_ref=dst, send_sem=send, recv_sem=recv, device_id=to, device_id_type=MESH
    )
    copy.start()
    return copy


class Gather:
    def __init__(self, place, s, buf, send, recv):
        self.place, self.buf, self.send, self.recv = place, buf, send, recv
        self.axes = ORDERS[s]
        self.at = tuple(place[axis] for axis in self.axes)
        self.sent, self.pair, self.kept = [], [], []

    def copy(self, slot, first, count, to, keep):
        ref = self.buf.at[self.place[3], pl.ds(first, count)]
        copy = remote(ref, ref, self.send.at[slot], self.recv.at[slot], device(to))
        keep.append(copy)

    def to_line(self, level, first, count):
        self.kept = []
        for step in (2, 1, 3):
            to = shifted(self.place, self.axes[level], step)
            self.copy(3 * level + step - 1, first, count, to, self.kept)
        self.sent += self.kept

    def arrive(self):
        for copy in self.kept:
            copy.wait_recv()

    def first(self):
        ka, kb, kc = self.at
        self.to_line(0, kc * 16 + kb * 4 + ka, 1)

    def second(self):
        self.arrive()
        ka, kb, kc = self.at
        self.to_line(1, kc * 16 + kb * 4, 4)

    def third(self):
        self.arrive()
        kc = self.at[2]
        self.to_line(2, kc * 16, 16)
        self.copy(9, kc * 16, 16, sibling(self.place), self.pair)

    def to_pair(self):
        kc = self.at[2]
        for step, copy in zip((2, 1, 3), self.kept):
            copy.wait_recv()
        for step in (1, 2, 3):
            self.copy(9 + step, (kc - step + 4) % 4 * 16, 16, sibling(self.place), self.pair)

    def finish(self):
        for copy in self.pair:
            copy.wait()
        for copy in self.sent:
            copy.wait_send()


def add_blocks(total, count, first, *others):
    def step(i, carry):
        value = total[first + i].astype(F32)
        for other in others:
            value = value + other(i).astype(F32)
        total[first + i] = value.astype(BF16)
        return carry

    lax.fori_loop(0, count, step, 0, unroll=min(count, 8))


class Scatter:
    def __init__(self, place, s, buf, pair, far, mid, near, out, send, recv):
        self.place, self.buf, self.pair_in = place, buf, pair
        self.inbox, self.out = (near, mid, far), out
        self.send, self.recv = send, recv
        self.axes = ORDERS[s]
        self.at = tuple(place[axis] for axis in self.axes)
        self.own = buf.at[place[3]]
        self.sent, self.pairs, self.kept = [], {}, []

    def copy(self, slot, src, dst, to):
        copy = remote(src, dst, self.send.at[slot], self.recv.at[slot], device(to))
        self.sent.append(copy)
        return copy

    def to_pair(self):
        other = self.buf.at[1 - self.place[3]]
        for offset in (2, 1, 3, 0):
            rows = pl.ds((self.at[2] + offset) % 4 * 16, 16)
            self.pairs[offset] = self.copy(
                offset, other.at[rows], self.pair_in.at[rows], sibling(self.place)
            )

    def add_pair(self, offset):
        self.pairs[offset].wait_recv()
        start = (self.at[2] + offset) % 4 * 16
        add_blocks(self.own, 16, start, lambda i: self.pair_in[start + i])

    def to_line(self, level, base, size, prepare=None):
        inbox = self.inbox[level]
        self.kept = []
        for step in (2, 1, 3):
            if prepare is not None:
                prepare(step)
            first = base + (self.at[level] + step) % 4 * size
            copy = self.copy(
                4 + 3 * level + step - 1,
                self.own.at[pl.ds(first, size)],
                inbox.at[pl.ds((step - 1) * size, size)],
                shifted(self.place, self.axes[level], step),
            )
            self.kept.append(copy)

    def total(self, level, base, size):
        for copy in self.kept:
            copy.wait_recv()
        inbox = self.inbox[level]
        add_blocks(
            self.own,
            size,
            base + self.at[level] * size,
            *[lambda i, n=n: inbox[n * size + i] for n in range(3)],
        )

    def far(self):
        self.to_line(2, 0, 16, self.add_pair)

    def mid(self):
        self.add_pair(0)
        self.total(2, 0, 16)
        self.to_line(1, self.at[2] * 16, 4)

    def near(self):
        self.total(1, self.at[2] * 16, 4)
        self.to_line(0, self.at[2] * 16 + self.at[1] * 4, 1)

    def finish(self):
        for copy in self.kept:
            copy.wait_recv()
        ka, kb, kc = self.at
        value = self.own[kc * 16 + kb * 4 + ka].astype(F32)
        for step in range(3):
            value = value + self.inbox[0][step].astype(F32)
        self.out[...] = value
        for copy in self.sent:
            copy.wait_send()


class GroupGather:
    def __init__(self, place, me, buf, send, recv):
        self.place, self.me, self.buf, self.send, self.recv = place, me, buf, send, recv
        self.sent, self.along, self.across = [], [], []

    def copy(self, slot, ref, to, keep):
        copy = remote(ref, ref, self.send.at[slot], self.recv.at[slot], device(to))
        keep.append(copy)
        self.sent.append(copy)

    def half(self, member, bottom, count=1):
        rows = TOK // 2
        return self.buf.at[pl.ds(member, count), pl.ds(bottom * rows, rows)]

    def first(self):
        for step in (2, 1, 3):
            to = shifted(self.place, 0, step)
            self.copy(step - 1, self.half(self.me, 0), to, self.along)
        self.copy(3, self.half(self.me, 1), beside(self.place), self.across)
        self.copy(4, self.half(self.me, 0), beside(self.place), self.across)

    def second(self):
        x = self.place[0]
        self.across[0].wait_recv()
        for step in (2, 1, 3):
            to = shifted(self.place, 0, step)
            self.copy(7 + step, self.half(2 * x, 1, 2), to, self.across)
        for step, copy in zip((2, 1, 3), list(self.along)):
            copy.wait_recv()
            member = (x - step + 4) % 4 * 2 + self.me % 2
            self.copy(4 + step, self.half(member, 0), beside(self.place), self.across)

    def finish(self):
        for copy in self.across[1:]:
            copy.wait_recv()
        for copy in self.sent:
            copy.wait_send()


class GroupScatter:
    def __init__(self, place, buf, inbox, send, recv):
        self.place, self.buf, self.inbox, self.send, self.recv = place, buf, inbox, send, recv
        self.sent = []

    def copy(self, slot, src, dst, to):
        copy = remote(src, dst, self.send.at[slot], self.recv.at[slot], device(to))
        self.sent.append(copy)
        return copy

    def first(self):
        x, z = self.place[0], self.place[2] % 2
        by_x, by_z = self.inbox[0], self.inbox[1]
        half = TOK // 2
        self.along = [
            self.copy(
                step - 1,
                self.buf.at[pl.ds(0, 2), (x + step) % 4, pl.ds(0, half)],
                by_x.at[step - 1],
                shifted(self.place, 0, step),
            )
            for step in (2, 1, 3)
        ]
        self.across = self.copy(
            3, self.buf.at[1 - z, pl.ds(0, 4), pl.ds(half, half)], by_z, beside(self.place)
        )

    def second(self):
        x, z = self.place[0], self.place[2] % 2
        by_x, by_z, last_x, last_z = self.inbox
        half = TOK // 2
        top, bottom = pl.ds(0, half), pl.ds(half, half)
        self.across.wait_recv()
        for k in range(4):
            value = self.buf[z, k, bottom, :].astype(F32) + by_z[k].astype(F32)
            self.buf[z, k, bottom, :] = value.astype(BF16)
        self.last = [
            self.copy(
                3 + step,
                self.buf.at[z, (x + step) % 4, bottom],
                last_x.at[step - 1],
                shifted(self.place, 0, step),
            )
            for step in (2, 1, 3)
        ]
        for copy in self.along:
            copy.wait_recv()
        for k in range(2):
            value = self.buf[k, x, top, :].astype(F32)
            for step in range(3):
                value = value + by_x[step, k].astype(F32)
            self.buf[k, x, top, :] = value.astype(BF16)
        self.last.append(self.copy(7, self.buf.at[1 - z, x, top], last_z, beside(self.place)))

    def finish(self):
        x, z = self.place[0], self.place[2] % 2
        last_x, last_z = self.inbox[2:]
        half = TOK // 2
        for copy in self.last:
            copy.wait_recv()
        value = self.buf[z, x].astype(F32)
        upper = value[:half] + last_z[...].astype(F32)
        lower = value[half:]
        for step in range(3):
            lower = lower + last_x[step].astype(F32)
        for copy in self.sent:
            copy.wait_send()
        return jnp.concatenate([upper, lower], axis=0)


def one_hot(rows, columns, pick):
    i = lax.broadcasted_iota(jnp.int32, (rows, columns), 0)
    j = lax.broadcasted_iota(jnp.int32, (rows, columns), 1)
    return jnp.where(pick(i) == j, 1.0, 0.0)


def dot(left, right):
    return jnp.dot(left, right, preferred_element_type=F32)


def dot_nt(left, right):
    return lax.dot_general(left, right, (((1,), (1,)), ((), ())), preferred_element_type=F32)


def dot_tn(left, right):
    return lax.dot_general(left, right, (((0,), (0,)), ((), ())), preferred_element_type=F32)


def stack_columns(shard):
    r, columns = shard.shape
    value = shard.astype(F32)
    pad = [jnp.zeros((8 - r, 128), F32)] if r < 8 else []
    pieces = []
    for c in range(columns // 128):
        pieces += [value[:, c * 128 : (c + 1) * 128]] + pad
    return jnp.concatenate(pieces, axis=0)


def query_order():
    return one_hot(32, 64, lambda i: (i & 7) * 8 + (i >> 3))


def mixed_order():
    def pick(i):
        rest = jnp.where(i < 28, 32 + (i - 20) * 8 + 4, -1)
        return jnp.where(i < 20, (i & 3) * 8 + (i >> 2), rest)

    return one_hot(32, 96, pick)


def wide_order():
    return one_hot(80, 128, lambda i: (i & 15) * 8 + (i >> 4))


def block_index(s, g, d):
    z_hi, y = g // 4, g % 4
    core, x, z_lo = d // 8, (d // 2) % 4, d % 2
    place = (x, y, z_hi * 2 + z_lo)
    a, b, c = (place[axis] for axis in ORDERS[s])
    return core, c * 16 + b * 4 + a


def rms(value):
    return lax.rsqrt(jnp.mean(value * value, axis=-1, keepdims=True) + EPS)


def rotate(value, cosines, sines):
    half = HD // 2
    u, w = value[:, :half], value[:, half:]
    return jnp.concatenate([u * cosines - w * sines, w * cosines + u * sines], axis=1)


def norm_back(grad, value, scale, gain):
    scaled = grad * gain
    back = scale * scaled - value * scale**3 * jnp.mean(scaled * value, axis=-1, keepdims=True)
    return back, jnp.sum(grad * value * scale, axis=0, keepdims=True)


def split_dot_nt(value, matrix):
    high = value.astype(BF16)
    low = (value - high.astype(F32)).astype(BF16)
    return dot_nt(high, matrix) + dot_nt(low, matrix)


def block_kernel(
    tokens,
    cotangent,
    lengths,
    w_query,
    w_key,
    w_value,
    w_out,
    w_gate,
    w_up,
    w_down,
    attn_gain,
    ffn_gain,
    head_gains,
    block_out,
    input_grad,
    sum_a0,
    sum_a1,
    sum_a2,
    sum_b0,
    sum_b1,
    sum_b2,
    a0,
    a1,
    a2,
    b0,
    b1,
    b2,
    *scratch,
):
    it = iter(scratch)

    def take(count):
        return [next(it) for _ in range(count)]

    pair_in, far_in, mid_in, near_in = take(6), take(6), take(6), take(6)
    q_mat, kv_mat, o_mat, g_mat, u_mat, d_mat, q_grad, kv_grad = take(8)
    perm, flip, pick, head_pick, gain_cols, gain_rows = take(6)
    cos_ref, sin_ref, allowed_ref = take(3)
    tok_all, scaled, normed, ffn_in, middle = take(5)
    q_raw, kv_raw, queries, kv_all = take(4)
    probs, attended, attended_low, d_attended, d_scores = take(5)
    hidden, d_gate, d_up, d_acc = take(4)
    d_kv_low, d_kv, d_q_low, *d_kv_in = take(7)
    gather_send, gather_recv, scatter_send, scatter_recv = take(4)
    tok_send, tok_recv, dkv_send, dkv_recv = take(4)

    place = coords()
    core = place[3]
    met = greet(place)
    me = lax.axis_index("fsdp")
    mine = pl.ds(pl.multiple_of(me * TOK, TOK), TOK)
    bufs = (a0, a1, a2, b0, b1, b2)
    outs = (sum_a0, sum_a1, sum_a2, sum_b0, sum_b1, sum_b2)

    def own_ref(n):
        ka, kb, kc = (place[axis] for axis in ORDERS[n % 3])
        return bufs[n].at[core, kc * 16 + kb * 4 + ka]

    query_stack = stack_columns(w_query[...]).astype(BF16)
    own_ref(0)[...] = dot(query_order().astype(BF16), query_stack).astype(BF16)
    mixed = jnp.concatenate(
        [
            stack_columns(w_key[...]).astype(BF16),
            stack_columns(w_value[...]).astype(BF16),
            query_stack,
        ],
        axis=0,
    )
    packed = dot(mixed_order().astype(BF16), mixed)
    gains = jnp.concatenate(
        [ref[...].astype(F32) for ref in (attn_gain, ffn_gain, head_gains)]
        + [jnp.zeros((1, 114), F32)],
        axis=1,
    )
    gain_place = lax.broadcasted_iota(jnp.int32, (8, 128), 0) == GAIN_ROW - 24
    own_ref(1)[...] = jnp.concatenate([packed[:24], packed[24:] + jnp.where(gain_place, gains, 0.0)], axis=0).astype(BF16)
    packed = jnp.concatenate([stack_columns(w_out[...]), jnp.zeros((8, 128), F32)], axis=0)
    own_ref(2)[...] = packed.astype(BF16)
    order = wide_order().astype(BF16)
    own_ref(3)[...] = dot(order, stack_columns(w_gate[...]).astype(BF16)).astype(BF16)
    own_ref(4)[...] = dot(order, stack_columns(w_up[...]).astype(BF16)).astype(BF16)
    down = w_down[...]
    own_ref(5)[...] = jnp.concatenate(
        [down[:, c * 128 : (c + 1) * 128] for c in range(5)], axis=0
    )
    tok_all[me] = tokens[...]

    ga = [
        Gather(place, n % 3, bufs[n], gather_send.at[n], gather_recv.at[n]) for n in range(6)
    ]
    sc = [
        Scatter(
            place,
            n % 3,
            bufs[n],
            pair_in[n],
            far_in[n],
            mid_in[n],
            near_in[n],
            outs[n],
            scatter_send.at[n],
            scatter_recv.at[n],
        )
        for n in range(6)
    ]
    tg = GroupGather(place, me, tok_all, tok_send, tok_recv)
    ds = GroupScatter(place, d_kv, d_kv_in, dkv_send, dkv_recv)
    met()
    for n in (1, 0, 2, 3, 4, 5):
        ga[n].first()
    tg.first()

    perm[...] = one_hot(256, 256, lambda i: (i & 15) * 16 + (i >> 4)).astype(BF16)
    flip[...] = one_hot(
        256, 256, lambda i: ((i & 127) >> 3) * 16 + (i >> 7) * 8 + (i & 7)
    ).astype(BF16)
    row = lax.broadcasted_iota(jnp.int32, (D, D), 0)
    column = lax.broadcasted_iota(jnp.int32, (D, D), 1)
    pick[...] = jnp.where(row == 5 * (column & 127) + (column >> 7), 1.0, 0.0).astype(BF16)
    row = lax.broadcasted_iota(jnp.int32, (2 * HD, 2 * HD), 0)
    column = lax.broadcasted_iota(jnp.int32, (2 * HD, 2 * HD), 1)
    head_pick[...] = jnp.where(row == 4 * (column & 127) + (column >> 7), 1.0, 0.0).astype(BF16)
    for n in (1, 0, 2, 3, 4, 5):
        ga[n].second()
    tg.second()
    first_len, second_len = lengths[0, 0], lengths[0, 1]
    first_end, second_end = first_len, first_len + second_len

    def segment(ids):
        past_one = jnp.where(ids >= first_end, 1, 0)
        past_two = jnp.where(ids >= second_end, 1, 0)
        return past_one + past_two, ids - past_one * first_len - past_two * second_len

    lane = lax.broadcasted_iota(jnp.int32, (TOK, HD // 2), 1).astype(F32)
    frequencies = jnp.exp(lane * (2.0 / HD) * (-math.log(ROPE_BASE)))

    def tables(m, carry):
        ids = m * TOK + lax.broadcasted_iota(jnp.int32, (TOK, HD // 2), 0)
        angles = segment(ids)[1].astype(F32) * frequencies
        rows = pl.ds(pl.multiple_of(m * TOK, TOK), TOK)
        cos_ref[rows, :] = jnp.cos(angles)
        sin_ref[rows, :] = jnp.sin(angles)
        return carry

    lax.fori_loop(0, GROUP, tables, 0, unroll=2)
    for n in (1, 0, 2):
        ga[n].third()
    row_ids = me * TOK + lax.broadcasted_iota(jnp.int32, (TOK, KEYS), 0)
    key_ids = lax.broadcasted_iota(jnp.int32, (TOK, KEYS), 1)
    same = segment(row_ids)[0] == segment(key_ids)[0]
    allowed_ref[...] = jnp.where(same & (key_ids <= row_ids), 1.0, 0.0)
    for n in (3, 4, 5):
        ga[n].third()
    inputs = tokens[...].astype(F32)
    scale_one = rms(inputs)
    for n in (1, 0):
        ga[n].to_pair()
    tg.finish()

    def scale_tokens(m, carry):
        rows = pl.ds(pl.multiple_of(m * TOK, TOK), TOK)
        value = tok_all[m]
        scaled[rows, :] = dot(value, pick[...]) * rms(value.astype(F32))
        return carry

    lax.fori_loop(0, GROUP, scale_tokens, 0, unroll=2)
    ga[1].finish()
    ga[0].finish()

    def slab(n, g, j):
        tiles = []
        for d in range(16):
            c, index = block_index(n % 3, g, d)
            tiles.append(bufs[n][c, index, pl.ds(j * 16, 16), :])
        return jnp.concatenate(tiles, axis=0)

    def turn(matrix, parts):
        out = dot(matrix, jnp.concatenate(parts, axis=1)).astype(BF16)
        return [out[:, i * 128 : (i + 1) * 128] for i in range(len(parts))]

    def tiles_wide(block, first, count):
        return jnp.concatenate(
            [block[(first + i) * 16 : (first + i + 1) * 16] for i in range(count)], axis=1
        )

    def unpack_a(g, carry):
        at = pl.ds(pl.multiple_of(g * 16, 16), 16)

        def rows(r):
            return pl.ds(pl.multiple_of(r * 128 + g * 16, 16), 16)

        kv0, kv1 = turn(perm[...], [slab(1, g, 0), slab(1, g, 1)])
        q0, q1 = turn(perm[...], [slab(0, g, 0), slab(0, g, 1)])
        for r, (block, first) in enumerate(((q0, 0), (q0, 8), (q1, 0), (q1, 8), (kv1, 4))):
            q_mat[rows(r), :] = tiles_wide(block, first, 8)
        gain_cols[at, :] = kv1[12 * 16 : 13 * 16].astype(F32)
        for r in range(4):
            kv_mat[rows(r), :] = tiles_wide(kv0, 4 * r, 4)
        kv_mat[rows(4), :] = tiles_wide(kv1, 0, 4)
        return carry

    lax.fori_loop(0, 8, unpack_a, 0, unroll=8)

    def unpack_out(g, carry):
        o0, o1 = turn(flip[...], [slab(2, g, 0), slab(2, g, 1)])
        (o2,) = turn(flip[...], [slab(2, g, 2)])
        o_mat[pl.ds(pl.multiple_of(g * 128, 128), 128), :] = jnp.concatenate(
            [o0[:128], o0[128:], o1[:128], o1[128:], o2[:128]], axis=1
        )
        return carry

    turned = gain_cols[...].T

    def by_column(first, count):
        return jnp.concatenate([turned[first + i : first + i + 1] for i in range(count)], axis=1)

    gain_rows[2:3, 0 : 2 * HD] = dot_nt(by_column(10, 4).astype(BF16), head_pick[...])

    key_gain = gain_rows[2:3, HD : 2 * HD]
    query_gain = gain_rows[2:3, 0:HD]
    turned_gain = by_column(0, 5)

    def keys_forward(m, carry):
        rows = pl.ds(pl.multiple_of(m * 256, 256), 256)
        normed_rows = (scaled[rows, :] * turned_gain).astype(BF16)
        normed[rows, :] = normed_rows
        raw = dot(normed_rows, kv_mat[...])
        kv_raw[rows, :] = raw
        key_raw = raw[:, 0:HD]
        key_rot = rotate(key_raw * rms(key_raw) * key_gain, cos_ref[rows, :], sin_ref[rows, :])
        kv_all[rows, :] = jnp.concatenate([key_rot, raw[:, HD:]], axis=1).astype(BF16)
        return carry

    lax.fori_loop(0, KEYS // 256, keys_forward, 0, unroll=4)
    cosines, sines = cos_ref[mine, :], sin_ref[mine, :]
    q_raw[...] = dot(normed[mine, :], q_mat[...])
    for h in range(H):
        raw = q_raw[:, h * HD : (h + 1) * HD]
        rot = rotate(raw * rms(raw) * query_gain, cosines, sines)
        queries[h * TOK : (h + 1) * TOK, :] = rot.astype(BF16)
    for n in (2, 3, 4, 5):
        ga[n].to_pair()

    def attend(h, carry):
        rows = pl.ds(pl.multiple_of(h * TOK, TOK), TOK)
        allowed = allowed_ref[...]
        scores = dot_nt(queries[rows, :], kv_all[:, 0:HD]) * SCORE_SCALE
        scores = jnp.where(allowed > 0.0, scores, NEG)
        peak = jnp.max(scores, axis=-1, keepdims=True)
        expd = jnp.exp(scores - peak) * allowed
        low = (expd * (1.0 / jnp.sum(expd, axis=-1, keepdims=True))).astype(BF16)
        probs[rows, :] = low
        value = dot(low, kv_all[:, HD : 2 * HD])
        attended[rows, :] = value
        attended_low[:, pl.ds(pl.multiple_of(h * HD, HD), HD)] = value.astype(BF16)
        return carry

    lax.fori_loop(0, H, attend, 0, unroll=4)
    ga[2].finish()
    lax.fori_loop(0, 8, unpack_out, 0, unroll=8)
    gain_rows[0:1, :] = dot_nt(by_column(0, 5).astype(BF16), pick[...])
    gain_rows[1:2, :] = dot_nt(by_column(5, 5).astype(BF16), pick[...])
    middle[...] = inputs + dot(attended_low[...], o_mat[...])
    scale_two = rms(middle[...])
    ffn_nat = (middle[...] * scale_two * gain_rows[1:2, :]).astype(BF16)
    ffn_in[...] = dot(ffn_nat, pick[...]).astype(BF16)
    for n in (3, 4, 5):
        ga[n].finish()

    def unpack_b(g, carry):
        for mat, n in ((g_mat, 3), (u_mat, 4)):
            slabs = [slab(n, g, j) for j in range(5)]
            turned_slabs = turn(perm[...], slabs[0:2])
            turned_slabs += turn(perm[...], slabs[2:4])
            turned_slabs += turn(perm[...], slabs[4:5])
            for r in range(5):
                mat[pl.ds(pl.multiple_of(r * 128 + g * 16, 16), 16), :] = tiles_wide(
                    turned_slabs[r], 0, 16
                )
        for d in range(16):
            c, index = block_index(2, g, d)
            block = bufs[5][c, index]
            d_mat[pl.ds(pl.multiple_of(g * 256 + d * 16, 16), 16), :] = tiles_wide(block, 0, 5)
        return carry

    lax.fori_loop(0, 8, unpack_b, 0, unroll=8)

    block_out[...] = middle[...]
    d_acc[...] = jnp.zeros_like(d_acc)
    root = math.sqrt(2.0 / math.pi)

    def feed(n, carry):
        at = pl.ds(pl.multiple_of(n * 512, 512), 512)
        gate = dot(ffn_in[...], g_mat[:, at])
        up = dot(ffn_in[...], u_mat[:, at])
        d_hidden = dot_nt(cotangent[...], d_mat[at, :])
        square = gate * gate
        tanh = jnp.tanh(root * gate * (1.0 + 0.044715 * square))
        lift = 0.5 * (1.0 + tanh)
        act = gate * lift
        slope = lift + 0.5 * gate * (1.0 - tanh * tanh) * root * (1.0 + 3 * 0.044715 * square)
        hid = (act * up).astype(BF16)
        dg = (d_hidden * up * slope).astype(BF16)
        du = (d_hidden * act).astype(BF16)
        hidden[:, at] = hid
        d_gate[:, at] = dg
        d_up[:, at] = du
        block_out[...] += dot(hid, d_mat[at, :])
        d_acc[...] += dot_nt(dg, g_mat[:, at]) + dot_nt(du, u_mat[:, at])
        return carry

    lax.fori_loop(0, 4, feed, 0, unroll=2)

    def put(n, g, j, block):
        for d in range(16):
            c, index = block_index(n % 3, g, d)
            bufs[n][c, index, pl.ds(j * 16, 16), :] = block[d * 16 : (d + 1) * 16]

    def down_grads(g, carry):
        at = pl.ds(pl.multiple_of(g * 256, 256), 256)
        grad = dot_tn(hidden[:, at], cotangent[...]).astype(BF16)
        for d in range(16):
            c, index = block_index(2, g, d)
            rows = grad[d * 16 : (d + 1) * 16]
            bufs[5][c, index] = jnp.concatenate(
                [rows[:, i * 128 : (i + 1) * 128] for i in range(5)], axis=0
            )
        return carry

    def stack(grad, g, count):
        rows = grad[g * 16 : (g + 1) * 16]
        return [rows[:, i * 128 : (i + 1) * 128] for i in range(count)]

    def wide_grads(n, source):
        def loop_r(r, carry):
            at = pl.ds(pl.multiple_of(r * 128, 128), 128)
            grad = dot_tn(ffn_in[:, at], source[...]).astype(BF16)
            for g in range(0, 8, 2):
                one, two = turn(
                    perm[...],
                    [jnp.concatenate(stack(grad, g + i, 16), axis=0) for i in range(2)],
                )
                put(n, g, r, one)
                put(n, g + 1, r, two)
            return carry

        lax.fori_loop(0, 5, loop_r, 0, unroll=5)

    wide_grads(4, d_up)
    sc[4].to_pair()
    wide_grads(3, d_gate)
    sc[3].to_pair()
    sc[4].far()
    lax.fori_loop(0, 8, down_grads, 0, unroll=8)
    sc[5].to_pair()
    sc[3].far()

    d_ffn = split_dot_nt(d_acc[...], pick[...])
    d_norm, grad_two = norm_back(d_ffn, middle[...], scale_two, gain_rows[1:2, :])
    d_middle = cotangent[...].astype(F32) + d_norm
    input_grad[...] = d_middle
    d_branch = d_middle.astype(BF16)
    d_attended_flat = dot_nt(d_branch, o_mat[...]).astype(BF16)
    for h in range(H):
        d_attended[h * TOK : (h + 1) * TOK, :] = d_attended_flat[:, h * HD : (h + 1) * HD]
    sc[5].far()

    def out_grads(g, carry):
        at = pl.ds(pl.multiple_of(g * 128, 128), 128)
        grad = dot_tn(attended_low[:, at], d_branch).astype(BF16)
        cols = [grad[:, i * 128 : (i + 1) * 128] for i in range(5)]
        slabs = [
            jnp.concatenate(cols[0:2], axis=0),
            jnp.concatenate(cols[2:4], axis=0),
            jnp.concatenate([cols[4], jnp.zeros((128, 128), BF16)], axis=0),
        ]
        turned_back = dot_tn(flip[...], jnp.concatenate(slabs, axis=1)).astype(BF16)
        for j in range(3):
            put(2, g, j, turned_back[:, j * 128 : (j + 1) * 128])
        return carry

    lax.fori_loop(0, 8, out_grads, 0, unroll=8)
    sc[2].to_pair()

    def scores_back(h, carry):
        rows = pl.ds(pl.multiple_of(h * TOK, TOK), TOK)
        upstream = d_attended[rows, :]
        delta = jnp.sum(upstream.astype(F32) * attended[rows, :], axis=-1, keepdims=True)
        d_probs = dot_nt(upstream, kv_all[:, HD : 2 * HD])
        d_scores[rows, :] = (probs[rows, :].astype(F32) * (d_probs - delta)).astype(BF16)
        return carry

    lax.fori_loop(0, H, scores_back, 0, unroll=4)

    def keys_back(n, key_gain_grad):
        at = pl.ds(pl.multiple_of(n * 256, 256), 256)
        d_keys = dot_tn(d_scores[:, at], queries[...]) * SCORE_SCALE
        d_values = dot_tn(probs[:, at], d_attended[...])
        d_rot = rotate(d_keys, cos_ref[at, :], -sin_ref[at, :])
        raw = kv_raw[at, 0:HD]
        d_raw, gain_grad = norm_back(d_rot, raw, rms(raw), key_gain)
        low = jnp.concatenate([d_raw, d_values], axis=1).astype(BF16)
        d_kv_low[at, :] = low
        d_kv[0, n] = low[:TOK]
        d_kv[1, n] = low[TOK:]
        return key_gain_grad + gain_grad

    key_gain_grad = lax.fori_loop(0, KEYS // 256, keys_back, jnp.zeros((1, HD), F32), unroll=4)
    sc[2].far()

    query_gain_grad = jnp.zeros((1, HD), F32)
    for h in range(H):
        rows = slice(h * TOK, (h + 1) * TOK)
        d_rot = dot(d_scores[rows, :], kv_all[:, 0:HD]) * SCORE_SCALE
        raw = q_raw[:, h * HD : (h + 1) * HD]
        d_raw, gain_grad = norm_back(
            rotate(d_rot, cosines, -sines), raw, rms(raw), query_gain
        )
        query_gain_grad = query_gain_grad + gain_grad
        d_q_low[:, h * HD : (h + 1) * HD] = d_raw.astype(BF16)
    kv_grad[...] = dot_tn(normed[...], d_kv_low[...]).astype(BF16)
    q_grad[...] = dot_tn(normed[mine, :], d_q_low[...]).astype(BF16)

    d_key_total = jnp.zeros((1, D), F32)
    d_normed_q = dot_nt(d_q_low[...], q_mat[...])

    def norm_one_grad(n, total):
        at = pl.ds(pl.multiple_of(n * 256, 256), 256)
        return total + jnp.sum(
            dot_nt(d_kv_low[at, :], kv_mat[...]) * scaled[at, :], axis=0, keepdims=True
        )

    grad_one = lax.fori_loop(0, KEYS // 256, norm_one_grad, d_key_total, unroll=4)
    grad_one = grad_one + jnp.sum(d_normed_q * scaled[mine, :], axis=0, keepdims=True)

    def by_device(row, count, matrix):
        turned_row = dot(row.astype(BF16), matrix)
        return [turned_row[:, i * 128 : (i + 1) * 128] for i in range(count)]

    heads = jnp.concatenate([query_gain_grad, key_gain_grad], axis=1)
    gain_parts = [grad_one[:, i * 128 : (i + 1) * 128] for i in range(5)]
    gain_parts += by_device(grad_two, 5, pick[...]) + by_device(heads, 4, head_pick[...])
    gain_parts.append(jnp.zeros((114, 128), F32))
    gain_cols[...] = jnp.concatenate(gain_parts, axis=0).T

    def grads_a(g, carry):
        at = pl.ds(pl.multiple_of(g * 16, 16), 16)
        q_tiles, kv_tiles = [], []
        for r in range(5):
            rows = pl.ds(pl.multiple_of(r * 128 + g * 16, 16), 16)
            q_row, kv_row = q_grad[rows, :], kv_grad[rows, :]
            q_tiles += [q_row[:, i * 128 : (i + 1) * 128] for i in range(8)]
            kv_tiles += [kv_row[:, i * 128 : (i + 1) * 128] for i in range(4)]
        kv_tiles += q_tiles[32:40] + [gain_cols[at, :].astype(BF16)]
        kv_tiles += [jnp.zeros((16, 128), BF16)] * 3
        slabs = [
            jnp.concatenate(tiles[i : i + 16], axis=0)
            for tiles in (q_tiles, kv_tiles)
            for i in (0, 16)
        ]
        out = turn(perm[...], slabs[0:2]) + turn(perm[...], slabs[2:4])
        for n in range(2):
            for j in range(2):
                put(n, g, j, out[2 * n + j])
        return carry

    lax.fori_loop(0, 8, grads_a, 0, unroll=8)
    sc[1].to_pair()
    sc[0].to_pair()
    sc[1].far()
    sc[0].far()
    ds.first()
    for n in (4, 3, 5, 2, 1, 0):
        sc[n].mid()
    ds.second()
    for n in (4, 3, 5, 2, 1, 0):
        sc[n].near()

    total = ds.finish()
    d_normed = d_normed_q + dot_nt(total.astype(BF16), kv_mat[...])
    d_normed = split_dot_nt(d_normed, pick[...])
    d_norm, _ = norm_back(d_normed, inputs, scale_one, gain_rows[0:1, :])
    input_grad[...] += d_norm
    for n in (4, 3, 5, 2, 1, 0):
        sc[n].finish()


def finish_kernel(a0, a1, a2, b0, b1, b2, out, grad, block_out, input_grad, *outs):
    query, key, value, output, gate, up, down, norm_one, norm_two, heads = outs
    block_out[...] = out[...].astype(BF16)
    input_grad[...] = grad[...]

    def exact(order, block):
        return lax.dot_general(
            order,
            block,
            (((0,), (0,)), ((), ())),
            precision=lax.Precision.HIGHEST,
            preferred_element_type=F32,
        )

    def spread(ref, stacked, first, count):
        for c in range(count):
            ref[:, c * 128 : (c + 1) * 128] = stacked[(first + c) * 8 : (first + c) * 8 + 5]

    stacked = exact(mixed_order(), a1[...])
    spread(query, exact(query_order(), a0[...]) + stacked[32:], 0, 8)
    spread(key, stacked, 0, 2)
    spread(value, stacked, 2, 2)
    for c in range(5):
        output[:, c * 128 : (c + 1) * 128] = a2[c * 8 : (c + 1) * 8]
        down[:, c * 128 : (c + 1) * 128] = b2[c * 16 : (c + 1) * 16]
    order = wide_order()
    spread(gate, exact(order, b0[...]), 0, 16)
    spread(up, exact(order, b1[...]), 0, 16)
    row = a1[GAIN_ROW]
    norm_one[...] = row[0:5]
    norm_two[...] = row[5:10]
    heads[...] = row[10:14]


def vmem_specs(count):
    return [pl.BlockSpec(memory_space=pltpu.VMEM)] * count


def body(
    tokens,
    w_query,
    w_key,
    w_value,
    w_out,
    w_gate,
    w_up,
    w_down,
    attn_gain,
    ffn_gain,
    head_gains,
    lengths,
    cotangent,
):

    def low(*shape):
        return pltpu.VMEM(shape, BF16)

    def full(*shape):
        return pltpu.VMEM(shape, F32)

    streams = [rows for phase in ROWS for rows in phase]
    scratch = [low(2, 64, rows, 128) for rows in streams]
    scratch += [low(count, rows, 128) for count in (64, 48, 12, 3) for rows in streams]
    scratch += [low(D, 1024), low(D, 512), low(1024, D), low(D, FF), low(D, FF), low(FF, D)]
    scratch += [low(D, 1024), low(D, 512)]
    scratch += [low(256, 256), low(256, 256), low(D, D), low(512, 512)]
    scratch += [full(128, 128), full(8, D)]
    scratch += [full(KEYS, 128), full(KEYS, 128), full(TOK, KEYS)]
    scratch += [low(GROUP, TOK, D), full(KEYS, D), low(KEYS, D)]
    scratch += [low(TOK, D), full(TOK, D)]
    scratch += [full(TOK, 1024), full(KEYS, 512), low(H * TOK, HD), low(KEYS, 2 * HD)]
    scratch += [low(H * TOK, KEYS), full(H * TOK, HD), low(TOK, 1024), low(H * TOK, HD)]
    scratch += [low(H * TOK, KEYS), low(TOK, FF), low(TOK, FF), low(TOK, FF), full(TOK, D)]
    scratch += [low(KEYS, 2 * HD), low(2, 4, TOK, 2 * HD), low(TOK, 1024)]
    half = TOK // 2
    scratch += [low(3, 2, half, 2 * HD), low(4, half, 2 * HD)]
    scratch += [low(3, half, 2 * HD), low(half, 2 * HD)]
    dma = pltpu.SemaphoreType.DMA
    scratch += [dma((6, 13)), dma((6, 13)), dma((6, 13)), dma((6, 13))]
    scratch += [dma((11,)), dma((11,)), dma((8,)), dma((8,))]
    out, grad, *sums = pl.pallas_call(
        block_kernel,
        out_shape=[jax.ShapeDtypeStruct((TOK, D), F32)] * 2
        + [jax.ShapeDtypeStruct((rows, 128), F32) for phase in ROWS for rows in phase],
        in_specs=vmem_specs(2) + [pl.BlockSpec(memory_space=pltpu.SMEM)] + vmem_specs(10),
        out_specs=vmem_specs(8),
        scratch_shapes=scratch,
        compiler_params=pltpu.CompilerParams(
            collective_id=0, has_side_effects=True, vmem_limit_bytes=VMEM_BYTES
        ),
        name="block",
    )(
        tokens,
        cotangent,
        lengths,
        w_query,
        w_key,
        w_value,
        w_out,
        w_gate,
        w_up,
        w_down,
        attn_gain[None],
        ffn_gain[None],
        head_gains[None],
    )
    shards = [
        jax.ShapeDtypeStruct(shape, F32)
        for shape in ((5, 1024), (5, 256), (5, 256), (8, D), (5, FF), (5, FF), (16, D))
    ]
    shards += [jax.ShapeDtypeStruct((count,), F32) for count in (5, 5, 4)]
    return pl.pallas_call(
        finish_kernel,
        out_shape=[jax.ShapeDtypeStruct((TOK, D), BF16), jax.ShapeDtypeStruct((TOK, D), F32)]
        + shards,
        in_specs=vmem_specs(8),
        out_specs=vmem_specs(12),
        name="finish",
    )(*sums, out, grad)


def solution(mesh):
    rows = P(("dp", "fsdp"), None)
    vector = P(("dp", "fsdp"))
    return jax.shard_map(
        body,
        mesh=mesh,
        in_specs=(rows,) * 8 + (vector,) * 3 + (P("dp", None), rows),
        out_specs=(rows,) * 9 + (vector,) * 3,
        check_vma=False,
    )
```

```python
import math

import jax
import jax.numpy as jnp
from jax import lax
from jax.experimental import pallas as pl
from jax.experimental.pallas import tpu as pltpu
from jax.sharding import PartitionSpec as P

H = 4
HD = 256
D = 640
FF = 2048
TOK = 128
GROUP = 8
KEYS = TOK * GROUP
EPS = 1e-05
ROPE_BASE = 1000000.0
NEG = -1e30
SCORE_SCALE = 1.0 / math.sqrt(HD)
F32 = jnp.float32
BF16 = jnp.bfloat16

MESH = pl.DeviceIdType.MESH
VMEM_BYTES = 60 * 1024 * 1024

ORDERS = ((0, 1, 2), (1, 2, 0), (2, 0, 1))
ROWS = ((32, 32, 48), (80, 80, 80))
GAIN_ROW = 28


def coords():
    dp = lax.axis_index("dp")
    fsdp = lax.axis_index("fsdp")
    return (fsdp // 2, (dp // 2) % 4, (dp // 8) * 2 + fsdp % 2, dp % 2)


def device(place):
    x, y, z, core = place
    return ((z // 2) * 8 + y * 2 + core, x * 2 + z % 2)


def shifted(place, axis, step):
    moved = list(place)
    moved[axis] = (place[axis] + step) % 4
    return tuple(moved)


def sibling(place):
    return place[:3] + (1 - place[3],)


def beside(place):
    x, y, z, core = place
    return (x, y, (z // 2) * 2 + (1 - z % 2), core)


def greet(place):
    partners = [device(shifted(place, axis, step)) for axis in range(3) for step in (1, 2, 3)]
    partners.append(device(sibling(place)))
    barrier = pltpu.get_barrier_semaphore()
    for partner in partners:
        pl.semaphore_signal(barrier, inc=1, device_id=partner, device_id_type=MESH)
    return lambda: pl.semaphore_wait(barrier, len(partners))


def remote(src, dst, send, recv, to):
    copy = pltpu.make_async_remote_copy(
        src_ref=src, dst_ref=dst, send_sem=send, recv_sem=recv, device_id=to, device_id_type=MESH
    )
    copy.start()
    return copy


class Gather:
    def __init__(self, place, s, buf, send, recv):
        self.place, self.buf, self.send, self.recv = place, buf, send, recv
        self.axes = ORDERS[s]
        self.at = tuple(place[axis] for axis in self.axes)
        self.sent, self.pair, self.kept = [], [], []

    def copy(self, slot, first, count, to, keep):
        ref = self.buf.at[self.place[3], pl.ds(first, count)]
        copy = remote(ref, ref, self.send.at[slot], self.recv.at[slot], device(to))
        keep.append(copy)

    def to_line(self, level, first, count):
        self.kept = []
        for step in (2, 1, 3):
            to = shifted(self.place, self.axes[level], step)
            self.copy(3 * level + step - 1, first, count, to, self.kept)
        self.sent += self.kept

    def arrive(self):
        for copy in self.kept:
            copy.wait_recv()

    def first(self):
        ka, kb, kc = self.at
        self.to_line(0, kc * 16 + kb * 4 + ka, 1)

    def second(self):
        self.arrive()
        ka, kb, kc = self.at
        self.to_line(1, kc * 16 + kb * 4, 4)

    def third(self):
        self.arrive()
        kc = self.at[2]
        self.to_line(2, kc * 16, 16)
        self.copy(9, kc * 16, 16, sibling(self.place), self.pair)

    def to_pair(self):
        kc = self.at[2]
        for step, copy in ((1, self.kept[1]), (3, self.kept[2]), (2, self.kept[0])):
            copy.wait_recv()
            self.copy(9 + step, (kc - step + 4) % 4 * 16, 16, sibling(self.place), self.pair)

    def finish(self):
        for copy in self.pair:
            copy.wait()
        for copy in self.sent:
            copy.wait_send()


def add_blocks(total, count, first, *others):
    def step(i, carry):
        value = total[first + i].astype(F32)
        for other in others:
            value = value + other(i).astype(F32)
        total[first + i] = value.astype(BF16)
        return carry

    lax.fori_loop(0, count, step, 0, unroll=min(count, 8))


class Scatter:
    def __init__(self, place, s, buf, pair, far, mid, near, out, send, recv):
        self.place, self.buf, self.pair_in = place, buf, pair
        self.inbox, self.out = (near, mid, far), out
        self.send, self.recv = send, recv
        self.axes = ORDERS[s]
        self.at = tuple(place[axis] for axis in self.axes)
        self.own = buf.at[place[3]]
        self.sent, self.pairs, self.kept = [], {}, []

    def copy(self, slot, src, dst, to):
        copy = remote(src, dst, self.send.at[slot], self.recv.at[slot], device(to))
        self.sent.append(copy)
        return copy

    def to_pair(self):
        other = self.buf.at[1 - self.place[3]]
        for offset in (2, 1, 3, 0):
            rows = pl.ds((self.at[2] + offset) % 4 * 16, 16)
            self.pairs[offset] = self.copy(
                offset, other.at[rows], self.pair_in.at[rows], sibling(self.place)
            )

    def add_pair(self, offset):
        self.pairs[offset].wait_recv()
        start = (self.at[2] + offset) % 4 * 16
        add_blocks(self.own, 16, start, lambda i: self.pair_in[start + i])

    def to_line(self, level, base, size, prepare=None):
        inbox = self.inbox[level]
        self.kept = []
        for step in (2, 1, 3):
            if prepare is not None:
                prepare(step)
            first = base + (self.at[level] + step) % 4 * size
            copy = self.copy(
                4 + 3 * level + step - 1,
                self.own.at[pl.ds(first, size)],
                inbox.at[pl.ds((step - 1) * size, size)],
                shifted(self.place, self.axes[level], step),
            )
            self.kept.append(copy)

    def total(self, level, base, size):
        for copy in self.kept:
            copy.wait_recv()
        inbox = self.inbox[level]
        add_blocks(
            self.own,
            size,
            base + self.at[level] * size,
            *[lambda i, n=n: inbox[n * size + i] for n in range(3)],
        )

    def far(self):
        self.to_line(2, 0, 16, self.add_pair)

    def mid(self):
        self.add_pair(0)
        self.total(2, 0, 16)
        self.to_line(1, self.at[2] * 16, 4)

    def near(self):
        self.total(1, self.at[2] * 16, 4)
        self.to_line(0, self.at[2] * 16 + self.at[1] * 4, 1)

    def finish(self):
        for copy in self.kept:
            copy.wait_recv()
        ka, kb, kc = self.at
        value = self.own[kc * 16 + kb * 4 + ka].astype(F32)
        for step in range(3):
            value = value + self.inbox[0][step].astype(F32)
        self.out[...] = value
        for copy in self.sent:
            copy.wait_send()


class GroupGather:
    def __init__(self, place, me, buf, send, recv):
        self.place, self.me, self.buf, self.send, self.recv = place, me, buf, send, recv
        self.sent, self.along, self.across = [], [], []

    def copy(self, slot, ref, to, keep):
        copy = remote(ref, ref, self.send.at[slot], self.recv.at[slot], device(to))
        keep.append(copy)
        self.sent.append(copy)

    def half(self, member, bottom, count=1):
        rows = TOK // 2
        return self.buf.at[pl.ds(member, count), pl.ds(bottom * rows, rows)]

    def first(self):
        for step in (2, 1, 3):
            to = shifted(self.place, 0, step)
            self.copy(step - 1, self.half(self.me, 0), to, self.along)
        self.copy(3, self.half(self.me, 1), beside(self.place), self.across)
        self.copy(4, self.half(self.me, 0), beside(self.place), self.across)

    def second(self):
        x = self.place[0]
        self.across[0].wait_recv()
        for step in (2, 1, 3):
            to = shifted(self.place, 0, step)
            self.copy(7 + step, self.half(2 * x, 1, 2), to, self.across)
        for step, copy in zip((2, 1, 3), list(self.along)):
            copy.wait_recv()
            member = (x - step + 4) % 4 * 2 + self.me % 2
            self.copy(4 + step, self.half(member, 0), beside(self.place), self.across)

    def finish(self):
        for copy in self.across[1:]:
            copy.wait_recv()
        for copy in self.sent:
            copy.wait_send()


class GroupScatter:
    def __init__(self, place, buf, inbox, send, recv):
        self.place, self.buf, self.inbox, self.send, self.recv = place, buf, inbox, send, recv
        self.sent = []

    def copy(self, slot, src, dst, to):
        copy = remote(src, dst, self.send.at[slot], self.recv.at[slot], device(to))
        self.sent.append(copy)
        return copy

    def first(self):
        x, z = self.place[0], self.place[2] % 2
        by_x, by_z = self.inbox[0], self.inbox[1]
        half = TOK // 2
        self.along = [
            self.copy(
                step - 1,
                self.buf.at[pl.ds(0, 2), (x + step) % 4, pl.ds(0, half)],
                by_x.at[step - 1],
                shifted(self.place, 0, step),
            )
            for step in (2, 1, 3)
        ]
        self.across = self.copy(
            3, self.buf.at[1 - z, pl.ds(0, 4), pl.ds(half, half)], by_z, beside(self.place)
        )

    def second(self):
        x, z = self.place[0], self.place[2] % 2
        by_x, by_z, last_x, last_z = self.inbox
        half = TOK // 2
        top, bottom = pl.ds(0, half), pl.ds(half, half)
        self.across.wait_recv()
        for k in range(4):
            value = self.buf[z, k, bottom, :].astype(F32) + by_z[k].astype(F32)
            self.buf[z, k, bottom, :] = value.astype(BF16)
        self.last = [
            self.copy(
                3 + step,
                self.buf.at[z, (x + step) % 4, bottom],
                last_x.at[step - 1],
                shifted(self.place, 0, step),
            )
            for step in (2, 1, 3)
        ]
        for copy in self.along:
            copy.wait_recv()
        for k in range(2):
            value = self.buf[k, x, top, :].astype(F32)
            for step in range(3):
                value = value + by_x[step, k].astype(F32)
            self.buf[k, x, top, :] = value.astype(BF16)
        self.last.append(self.copy(7, self.buf.at[1 - z, x, top], last_z, beside(self.place)))

    def finish(self):
        x, z = self.place[0], self.place[2] % 2
        last_x, last_z = self.inbox[2:]
        half = TOK // 2
        for copy in self.last:
            copy.wait_recv()
        value = self.buf[z, x].astype(F32)
        upper = value[:half] + last_z[...].astype(F32)
        lower = value[half:]
        for step in range(3):
            lower = lower + last_x[step].astype(F32)
        for copy in self.sent:
            copy.wait_send()
        return jnp.concatenate([upper, lower], axis=0)


def one_hot(rows, columns, pick):
    i = lax.broadcasted_iota(jnp.int32, (rows, columns), 0)
    j = lax.broadcasted_iota(jnp.int32, (rows, columns), 1)
    return jnp.where(pick(i) == j, 1.0, 0.0)


def dot(left, right):
    return jnp.dot(left, right, preferred_element_type=F32)


def dot_nt(left, right):
    return lax.dot_general(left, right, (((1,), (1,)), ((), ())), preferred_element_type=F32)


def dot_tn(left, right):
    return lax.dot_general(left, right, (((0,), (0,)), ((), ())), preferred_element_type=F32)


def stack_columns(shard):
    r, columns = shard.shape
    value = shard.astype(F32)
    pad = [jnp.zeros((8 - r, 128), F32)] if r < 8 else []
    pieces = []
    for c in range(columns // 128):
        pieces += [value[:, c * 128 : (c + 1) * 128]] + pad
    return jnp.concatenate(pieces, axis=0)


def query_order():
    return one_hot(32, 64, lambda i: (i & 7) * 8 + (i >> 3))


def mixed_order():
    def pick(i):
        rest = jnp.where(i < 28, 32 + (i - 20) * 8 + 4, -1)
        return jnp.where(i < 20, (i & 3) * 8 + (i >> 2), rest)

    return one_hot(32, 96, pick)


def wide_order():
    return one_hot(80, 128, lambda i: (i & 15) * 8 + (i >> 4))


def block_index(s, g, d):
    z_hi, y = g // 4, g % 4
    core, x, z_lo = d // 8, (d // 2) % 4, d % 2
    place = (x, y, z_hi * 2 + z_lo)
    a, b, c = (place[axis] for axis in ORDERS[s])
    return core, c * 16 + b * 4 + a


def rms(value):
    return lax.rsqrt(jnp.mean(value * value, axis=-1, keepdims=True) + EPS)


def rotate(value, cosines, sines):
    half = HD // 2
    u, w = value[:, :half], value[:, half:]
    return jnp.concatenate([u * cosines - w * sines, w * cosines + u * sines], axis=1)


def norm_back(grad, value, scale, gain):
    scaled = grad * gain
    back = scale * scaled - value * scale**3 * jnp.mean(scaled * value, axis=-1, keepdims=True)
    return back, jnp.sum(grad * value * scale, axis=0, keepdims=True)


def split_dot_nt(value, matrix):
    high = value.astype(BF16)
    low = (value - high.astype(F32)).astype(BF16)
    return dot_nt(high, matrix) + dot_nt(low, matrix)


def block_kernel(
    tokens,
    cotangent,
    lengths,
    w_query,
    w_key,
    w_value,
    w_out,
    w_gate,
    w_up,
    w_down,
    attn_gain,
    ffn_gain,
    head_gains,
    block_out,
    input_grad,
    sum_a0,
    sum_a1,
    sum_a2,
    sum_b0,
    sum_b1,
    sum_b2,
    a0,
    a1,
    a2,
    b0,
    b1,
    b2,
    *scratch,
):
    it = iter(scratch)

    def take(count):
        return [next(it) for _ in range(count)]

    pair_in, far_in, mid_in, near_in = take(6), take(6), take(6), take(6)
    q_mat, kv_mat, o_mat, g_mat, u_mat, d_mat, q_grad, kv_grad = take(8)
    perm, flip, pick, head_pick, gain_cols, gain_rows = take(6)
    cos_ref, sin_ref, allowed_ref = take(3)
    tok_all, scaled, normed, ffn_in, middle = take(5)
    q_raw, kv_raw, queries, kv_all = take(4)
    probs, attended, attended_low, d_attended, d_scores = take(5)
    hidden, d_gate, d_up, d_acc = take(4)
    d_kv_low, d_kv, d_q_low, *d_kv_in = take(7)
    gather_send, gather_recv, scatter_send, scatter_recv = take(4)
    tok_send, tok_recv, dkv_send, dkv_recv = take(4)

    place = coords()
    core = place[3]
    met = greet(place)
    me = lax.axis_index("fsdp")
    mine = pl.ds(pl.multiple_of(me * TOK, TOK), TOK)
    bufs = (a0, a1, a2, b0, b1, b2)
    outs = (sum_a0, sum_a1, sum_a2, sum_b0, sum_b1, sum_b2)

    def own_ref(n):
        ka, kb, kc = (place[axis] for axis in ORDERS[n % 3])
        return bufs[n].at[core, kc * 16 + kb * 4 + ka]

    query_stack = stack_columns(w_query[...]).astype(BF16)
    own_ref(0)[...] = dot(query_order().astype(BF16), query_stack).astype(BF16)
    mixed = jnp.concatenate(
        [
            stack_columns(w_key[...]).astype(BF16),
            stack_columns(w_value[...]).astype(BF16),
            query_stack,
        ],
        axis=0,
    )
    packed = dot(mixed_order().astype(BF16), mixed)
    gains = jnp.concatenate(
        [ref[...].astype(F32) for ref in (attn_gain, ffn_gain, head_gains)]
        + [jnp.zeros((1, 114), F32)],
        axis=1,
    )
    gain_place = lax.broadcasted_iota(jnp.int32, (8, 128), 0) == GAIN_ROW - 24
    own_ref(1)[...] = jnp.concatenate([packed[:24], packed[24:] + jnp.where(gain_place, gains, 0.0)], axis=0).astype(BF16)
    packed = jnp.concatenate([stack_columns(w_out[...]), jnp.zeros((8, 128), F32)], axis=0)
    own_ref(2)[...] = packed.astype(BF16)
    order = wide_order().astype(BF16)
    own_ref(3)[...] = dot(order, stack_columns(w_gate[...]).astype(BF16)).astype(BF16)
    own_ref(4)[...] = dot(order, stack_columns(w_up[...]).astype(BF16)).astype(BF16)
    down = w_down[...]
    own_ref(5)[...] = jnp.concatenate(
        [down[:, c * 128 : (c + 1) * 128] for c in range(5)], axis=0
    )
    tok_all[me] = tokens[...]

    ga = [
        Gather(place, n % 3, bufs[n], gather_send.at[n], gather_recv.at[n]) for n in range(6)
    ]
    sc = [
        Scatter(
            place,
            n % 3,
            bufs[n],
            pair_in[n],
            far_in[n],
            mid_in[n],
            near_in[n],
            outs[n],
            scatter_send.at[n],
            scatter_recv.at[n],
        )
        for n in range(6)
    ]
    tg = GroupGather(place, me, tok_all, tok_send, tok_recv)
    ds = GroupScatter(place, d_kv, d_kv_in, dkv_send, dkv_recv)
    met()
    for n in (1, 0, 2, 3, 4, 5):
        ga[n].first()
    tg.first()

    perm[...] = one_hot(256, 256, lambda i: (i & 15) * 16 + (i >> 4)).astype(BF16)
    flip[...] = one_hot(
        256, 256, lambda i: ((i & 127) >> 3) * 16 + (i >> 7) * 8 + (i & 7)
    ).astype(BF16)
    row = lax.broadcasted_iota(jnp.int32, (D, D), 0)
    column = lax.broadcasted_iota(jnp.int32, (D, D), 1)
    pick[...] = jnp.where(row == 5 * (column & 127) + (column >> 7), 1.0, 0.0).astype(BF16)
    row = lax.broadcasted_iota(jnp.int32, (2 * HD, 2 * HD), 0)
    column = lax.broadcasted_iota(jnp.int32, (2 * HD, 2 * HD), 1)
    head_pick[...] = jnp.where(row == 4 * (column & 127) + (column >> 7), 1.0, 0.0).astype(BF16)
    for n in (1, 0, 2, 3, 4, 5):
        ga[n].second()
    tg.second()
    first_len, second_len = lengths[0, 0], lengths[0, 1]
    first_end, second_end = first_len, first_len + second_len

    def segment(ids):
        past_one = jnp.where(ids >= first_end, 1, 0)
        past_two = jnp.where(ids >= second_end, 1, 0)
        return past_one + past_two, ids - past_one * first_len - past_two * second_len

    lane = lax.broadcasted_iota(jnp.int32, (TOK, HD // 2), 1).astype(F32)
    frequencies = jnp.exp(lane * (2.0 / HD) * (-math.log(ROPE_BASE)))

    def tables(m, carry):
        ids = m * TOK + lax.broadcasted_iota(jnp.int32, (TOK, HD // 2), 0)
        angles = segment(ids)[1].astype(F32) * frequencies
        rows = pl.ds(pl.multiple_of(m * TOK, TOK), TOK)
        cos_ref[rows, :] = jnp.cos(angles)
        sin_ref[rows, :] = jnp.sin(angles)
        return carry

    lax.fori_loop(0, GROUP, tables, 0, unroll=2)
    for n in (1, 0, 2):
        ga[n].third()
    row_ids = me * TOK + lax.broadcasted_iota(jnp.int32, (TOK, KEYS), 0)
    key_ids = lax.broadcasted_iota(jnp.int32, (TOK, KEYS), 1)
    same = segment(row_ids)[0] == segment(key_ids)[0]
    allowed_ref[...] = jnp.where(same & (key_ids <= row_ids), 1.0, 0.0)
    for n in (3, 4, 5):
        ga[n].third()
    inputs = tokens[...].astype(F32)
    scale_one = rms(inputs)
    for n in (1, 0):
        ga[n].to_pair()
    tg.finish()

    def scale_tokens(m, carry):
        rows = pl.ds(pl.multiple_of(m * TOK, TOK), TOK)
        value = tok_all[m]
        scaled[rows, :] = dot(value, pick[...]) * rms(value.astype(F32))
        return carry

    lax.fori_loop(0, GROUP, scale_tokens, 0, unroll=2)
    ga[1].finish()
    ga[0].finish()

    def slab(n, g, j):
        tiles = []
        for d in range(16):
            c, index = block_index(n % 3, g, d)
            tiles.append(bufs[n][c, index, pl.ds(j * 16, 16), :])
        return jnp.concatenate(tiles, axis=0)

    def turn(matrix, parts):
        out = dot(matrix, jnp.concatenate(parts, axis=1)).astype(BF16)
        return [out[:, i * 128 : (i + 1) * 128] for i in range(len(parts))]

    def tiles_wide(block, first, count):
        return jnp.concatenate(
            [block[(first + i) * 16 : (first + i + 1) * 16] for i in range(count)], axis=1
        )

    def unpack_a(g, carry):
        at = pl.ds(pl.multiple_of(g * 16, 16), 16)

        def rows(r):
            return pl.ds(pl.multiple_of(r * 128 + g * 16, 16), 16)

        kv0, kv1 = turn(perm[...], [slab(1, g, 0), slab(1, g, 1)])
        q0, q1 = turn(perm[...], [slab(0, g, 0), slab(0, g, 1)])
        for r, (block, first) in enumerate(((q0, 0), (q0, 8), (q1, 0), (q1, 8), (kv1, 4))):
            q_mat[rows(r), :] = tiles_wide(block, first, 8)
        gain_cols[at, :] = kv1[12 * 16 : 13 * 16].astype(F32)
        for r in range(4):
            kv_mat[rows(r), :] = tiles_wide(kv0, 4 * r, 4)
        kv_mat[rows(4), :] = tiles_wide(kv1, 0, 4)
        return carry

    lax.fori_loop(0, 8, unpack_a, 0, unroll=8)

    def unpack_out(g, carry):
        o0, o1 = turn(flip[...], [slab(2, g, 0), slab(2, g, 1)])
        (o2,) = turn(flip[...], [slab(2, g, 2)])
        o_mat[pl.ds(pl.multiple_of(g * 128, 128), 128), :] = jnp.concatenate(
            [o0[:128], o0[128:], o1[:128], o1[128:], o2[:128]], axis=1
        )
        return carry

    turned = gain_cols[...].T

    def by_column(first, count):
        return jnp.concatenate([turned[first + i : first + i + 1] for i in range(count)], axis=1)

    gain_rows[2:3, 0 : 2 * HD] = dot_nt(by_column(10, 4).astype(BF16), head_pick[...])

    key_gain = gain_rows[2:3, HD : 2 * HD]
    query_gain = gain_rows[2:3, 0:HD]
    turned_gain = by_column(0, 5)

    def keys_forward(m, carry):
        rows = pl.ds(pl.multiple_of(m * 256, 256), 256)
        normed_rows = (scaled[rows, :] * turned_gain).astype(BF16)
        normed[rows, :] = normed_rows
        raw = dot(normed_rows, kv_mat[...])
        kv_raw[rows, :] = raw
        key_raw = raw[:, 0:HD]
        key_rot = rotate(key_raw * rms(key_raw) * key_gain, cos_ref[rows, :], sin_ref[rows, :])
        kv_all[rows, :] = jnp.concatenate([key_rot, raw[:, HD:]], axis=1).astype(BF16)
        return carry

    lax.fori_loop(0, KEYS // 256, keys_forward, 0, unroll=4)
    cosines, sines = cos_ref[mine, :], sin_ref[mine, :]
    q_raw[...] = dot(normed[mine, :], q_mat[...])
    for h in range(H):
        raw = q_raw[:, h * HD : (h + 1) * HD]
        rot = rotate(raw * rms(raw) * query_gain, cosines, sines)
        queries[h * TOK : (h + 1) * TOK, :] = rot.astype(BF16)
    for n in (2, 3, 4, 5):
        ga[n].to_pair()

    def attend(h, carry):
        rows = pl.ds(pl.multiple_of(h * TOK, TOK), TOK)
        allowed = allowed_ref[...]
        scores = dot_nt(queries[rows, :], kv_all[:, 0:HD]) * SCORE_SCALE
        scores = jnp.where(allowed > 0.0, scores, NEG)
        peak = jnp.max(scores, axis=-1, keepdims=True)
        expd = jnp.exp(scores - peak) * allowed
        low = (expd * (1.0 / jnp.sum(expd, axis=-1, keepdims=True))).astype(BF16)
        probs[rows, :] = low
        value = dot(low, kv_all[:, HD : 2 * HD])
        attended[rows, :] = value
        attended_low[:, pl.ds(pl.multiple_of(h * HD, HD), HD)] = value.astype(BF16)
        return carry

    lax.fori_loop(0, H, attend, 0, unroll=4)
    ga[2].finish()
    lax.fori_loop(0, 8, unpack_out, 0, unroll=8)
    gain_rows[0:1, :] = dot_nt(by_column(0, 5).astype(BF16), pick[...])
    gain_rows[1:2, :] = dot_nt(by_column(5, 5).astype(BF16), pick[...])
    middle[...] = inputs + dot(attended_low[...], o_mat[...])
    scale_two = rms(middle[...])
    ffn_nat = (middle[...] * scale_two * gain_rows[1:2, :]).astype(BF16)
    ffn_in[...] = dot(ffn_nat, pick[...]).astype(BF16)
    for n in (3, 4, 5):
        ga[n].finish()

    def unpack_b(g, carry):
        for mat, n in ((g_mat, 3), (u_mat, 4)):
            slabs = [slab(n, g, j) for j in range(5)]
            turned_slabs = turn(perm[...], slabs[0:2])
            turned_slabs += turn(perm[...], slabs[2:4])
            turned_slabs += turn(perm[...], slabs[4:5])
            for r in range(5):
                mat[pl.ds(pl.multiple_of(r * 128 + g * 16, 16), 16), :] = tiles_wide(
                    turned_slabs[r], 0, 16
                )
        for d in range(16):
            c, index = block_index(2, g, d)
            block = bufs[5][c, index]
            d_mat[pl.ds(pl.multiple_of(g * 256 + d * 16, 16), 16), :] = tiles_wide(block, 0, 5)
        return carry

    lax.fori_loop(0, 8, unpack_b, 0, unroll=8)

    block_out[...] = middle[...]
    d_acc[...] = jnp.zeros_like(d_acc)
    root = math.sqrt(2.0 / math.pi)

    def feed(n, carry):
        at = pl.ds(pl.multiple_of(n * 512, 512), 512)
        gate = dot(ffn_in[...], g_mat[:, at])
        up = dot(ffn_in[...], u_mat[:, at])
        d_hidden = dot_nt(cotangent[...], d_mat[at, :])
        square = gate * gate
        tanh = jnp.tanh(root * gate * (1.0 + 0.044715 * square))
        lift = 0.5 * (1.0 + tanh)
        act = gate * lift
        slope = lift + 0.5 * gate * (1.0 - tanh * tanh) * root * (1.0 + 3 * 0.044715 * square)
        hid = (act * up).astype(BF16)
        dg = (d_hidden * up * slope).astype(BF16)
        du = (d_hidden * act).astype(BF16)
        hidden[:, at] = hid
        d_gate[:, at] = dg
        d_up[:, at] = du
        block_out[...] += dot(hid, d_mat[at, :])
        d_acc[...] += dot_nt(dg, g_mat[:, at]) + dot_nt(du, u_mat[:, at])
        return carry

    lax.fori_loop(0, 4, feed, 0, unroll=2)

    def put(n, g, j, block):
        for d in range(16):
            c, index = block_index(n % 3, g, d)
            bufs[n][c, index, pl.ds(j * 16, 16), :] = block[d * 16 : (d + 1) * 16]

    def down_grads(g, carry):
        at = pl.ds(pl.multiple_of(g * 256, 256), 256)
        grad = dot_tn(hidden[:, at], cotangent[...]).astype(BF16)
        for d in range(16):
            c, index = block_index(2, g, d)
            rows = grad[d * 16 : (d + 1) * 16]
            bufs[5][c, index] = jnp.concatenate(
                [rows[:, i * 128 : (i + 1) * 128] for i in range(5)], axis=0
            )
        return carry

    def stack(grad, g, count):
        rows = grad[g * 16 : (g + 1) * 16]
        return [rows[:, i * 128 : (i + 1) * 128] for i in range(count)]

    def wide_grads(n, source):
        def loop_r(r, carry):
            at = pl.ds(pl.multiple_of(r * 128, 128), 128)
            grad = dot_tn(ffn_in[:, at], source[...]).astype(BF16)
            for g in range(0, 8, 2):
                one, two = turn(
                    perm[...],
                    [jnp.concatenate(stack(grad, g + i, 16), axis=0) for i in range(2)],
                )
                put(n, g, r, one)
                put(n, g + 1, r, two)
            return carry

        lax.fori_loop(0, 5, loop_r, 0, unroll=5)

    wide_grads(4, d_up)
    sc[4].to_pair()
    wide_grads(3, d_gate)
    sc[3].to_pair()
    sc[4].far()
    lax.fori_loop(0, 8, down_grads, 0, unroll=8)
    sc[5].to_pair()
    sc[3].far()

    d_ffn = split_dot_nt(d_acc[...], pick[...])
    d_norm, grad_two = norm_back(d_ffn, middle[...], scale_two, gain_rows[1:2, :])
    d_middle = cotangent[...].astype(F32) + d_norm
    input_grad[...] = d_middle
    d_branch = d_middle.astype(BF16)
    d_attended_flat = dot_nt(d_branch, o_mat[...]).astype(BF16)
    for h in range(H):
        d_attended[h * TOK : (h + 1) * TOK, :] = d_attended_flat[:, h * HD : (h + 1) * HD]
    sc[5].far()

    def out_grads(g, carry):
        at = pl.ds(pl.multiple_of(g * 128, 128), 128)
        grad = dot_tn(attended_low[:, at], d_branch).astype(BF16)
        cols = [grad[:, i * 128 : (i + 1) * 128] for i in range(5)]
        slabs = [
            jnp.concatenate(cols[0:2], axis=0),
            jnp.concatenate(cols[2:4], axis=0),
            jnp.concatenate([cols[4], jnp.zeros((128, 128), BF16)], axis=0),
        ]
        turned_back = dot_tn(flip[...], jnp.concatenate(slabs, axis=1)).astype(BF16)
        for j in range(3):
            put(2, g, j, turned_back[:, j * 128 : (j + 1) * 128])
        return carry

    lax.fori_loop(0, 8, out_grads, 0, unroll=8)
    sc[2].to_pair()

    def scores_back(h, carry):
        rows = pl.ds(pl.multiple_of(h * TOK, TOK), TOK)
        upstream = d_attended[rows, :]
        delta = jnp.sum(upstream.astype(F32) * attended[rows, :], axis=-1, keepdims=True)
        d_probs = dot_nt(upstream, kv_all[:, HD : 2 * HD])
        d_scores[rows, :] = (probs[rows, :].astype(F32) * (d_probs - delta)).astype(BF16)
        return carry

    lax.fori_loop(0, H, scores_back, 0, unroll=4)

    def keys_back(n, key_gain_grad):
        at = pl.ds(pl.multiple_of(n * 256, 256), 256)
        d_keys = dot_tn(d_scores[:, at], queries[...]) * SCORE_SCALE
        d_values = dot_tn(probs[:, at], d_attended[...])
        d_rot = rotate(d_keys, cos_ref[at, :], -sin_ref[at, :])
        raw = kv_raw[at, 0:HD]
        d_raw, gain_grad = norm_back(d_rot, raw, rms(raw), key_gain)
        low = jnp.concatenate([d_raw, d_values], axis=1).astype(BF16)
        d_kv_low[at, :] = low
        d_kv[0, n] = low[:TOK]
        d_kv[1, n] = low[TOK:]
        return key_gain_grad + gain_grad

    key_gain_grad = lax.fori_loop(0, KEYS // 256, keys_back, jnp.zeros((1, HD), F32), unroll=4)
    sc[2].far()

    query_gain_grad = jnp.zeros((1, HD), F32)
    for h in range(H):
        rows = slice(h * TOK, (h + 1) * TOK)
        d_rot = dot(d_scores[rows, :], kv_all[:, 0:HD]) * SCORE_SCALE
        raw = q_raw[:, h * HD : (h + 1) * HD]
        d_raw, gain_grad = norm_back(
            rotate(d_rot, cosines, -sines), raw, rms(raw), query_gain
        )
        query_gain_grad = query_gain_grad + gain_grad
        d_q_low[:, h * HD : (h + 1) * HD] = d_raw.astype(BF16)
    kv_grad[...] = dot_tn(normed[...], d_kv_low[...]).astype(BF16)
    q_grad[...] = dot_tn(normed[mine, :], d_q_low[...]).astype(BF16)

    d_key_total = jnp.zeros((1, D), F32)
    d_normed_q = dot_nt(d_q_low[...], q_mat[...])

    def norm_one_grad(n, total):
        at = pl.ds(pl.multiple_of(n * 256, 256), 256)
        return total + jnp.sum(
            dot_nt(d_kv_low[at, :], kv_mat[...]) * scaled[at, :], axis=0, keepdims=True
        )

    grad_one = lax.fori_loop(0, KEYS // 256, norm_one_grad, d_key_total, unroll=4)
    grad_one = grad_one + jnp.sum(d_normed_q * scaled[mine, :], axis=0, keepdims=True)

    def by_device(row, count, matrix):
        turned_row = dot(row.astype(BF16), matrix)
        return [turned_row[:, i * 128 : (i + 1) * 128] for i in range(count)]

    heads = jnp.concatenate([query_gain_grad, key_gain_grad], axis=1)
    gain_parts = [grad_one[:, i * 128 : (i + 1) * 128] for i in range(5)]
    gain_parts += by_device(grad_two, 5, pick[...]) + by_device(heads, 4, head_pick[...])
    gain_parts.append(jnp.zeros((114, 128), F32))
    gain_cols[...] = jnp.concatenate(gain_parts, axis=0).T

    def grads_a(g, carry):
        at = pl.ds(pl.multiple_of(g * 16, 16), 16)
        q_tiles, kv_tiles = [], []
        for r in range(5):
            rows = pl.ds(pl.multiple_of(r * 128 + g * 16, 16), 16)
            q_row, kv_row = q_grad[rows, :], kv_grad[rows, :]
            q_tiles += [q_row[:, i * 128 : (i + 1) * 128] for i in range(8)]
            kv_tiles += [kv_row[:, i * 128 : (i + 1) * 128] for i in range(4)]
        kv_tiles += q_tiles[32:40] + [gain_cols[at, :].astype(BF16)]
        kv_tiles += [jnp.zeros((16, 128), BF16)] * 3
        slabs = [
            jnp.concatenate(tiles[i : i + 16], axis=0)
            for tiles in (q_tiles, kv_tiles)
            for i in (0, 16)
        ]
        out = turn(perm[...], slabs[0:2]) + turn(perm[...], slabs[2:4])
        for n in range(2):
            for j in range(2):
                put(n, g, j, out[2 * n + j])
        return carry

    lax.fori_loop(0, 8, grads_a, 0, unroll=8)
    sc[1].to_pair()
    sc[0].to_pair()
    sc[1].far()
    sc[0].far()
    ds.first()
    for n in (4, 3, 5, 2, 1, 0):
        sc[n].mid()
    ds.second()
    for n in (4, 3, 5, 2, 1, 0):
        sc[n].near()

    total = ds.finish()
    d_normed = d_normed_q + dot_nt(total.astype(BF16), kv_mat[...])
    d_normed = split_dot_nt(d_normed, pick[...])
    d_norm, _ = norm_back(d_normed, inputs, scale_one, gain_rows[0:1, :])
    input_grad[...] += d_norm
    for n in (4, 3, 5, 2, 1, 0):
        sc[n].finish()


def finish_kernel(a0, a1, a2, b0, b1, b2, out, grad, block_out, input_grad, *outs):
    query, key, value, output, gate, up, down, norm_one, norm_two, heads = outs
    block_out[...] = out[...].astype(BF16)
    input_grad[...] = grad[...]

    def exact(order, block):
        return lax.dot_general(
            order,
            block,
            (((0,), (0,)), ((), ())),
            precision=lax.Precision.HIGHEST,
            preferred_element_type=F32,
        )

    def spread(ref, stacked, first, count):
        for c in range(count):
            ref[:, c * 128 : (c + 1) * 128] = stacked[(first + c) * 8 : (first + c) * 8 + 5]

    stacked = exact(mixed_order(), a1[...])
    spread(query, exact(query_order(), a0[...]) + stacked[32:], 0, 8)
    spread(key, stacked, 0, 2)
    spread(value, stacked, 2, 2)
    for c in range(5):
        output[:, c * 128 : (c + 1) * 128] = a2[c * 8 : (c + 1) * 8]
        down[:, c * 128 : (c + 1) * 128] = b2[c * 16 : (c + 1) * 16]
    order = wide_order()
    spread(gate, exact(order, b0[...]), 0, 16)
    spread(up, exact(order, b1[...]), 0, 16)
    row = a1[GAIN_ROW]
    norm_one[...] = row[0:5]
    norm_two[...] = row[5:10]
    heads[...] = row[10:14]


def vmem_specs(count):
    return [pl.BlockSpec(memory_space=pltpu.VMEM)] * count


def body(
    tokens,
    w_query,
    w_key,
    w_value,
    w_out,
    w_gate,
    w_up,
    w_down,
    attn_gain,
    ffn_gain,
    head_gains,
    lengths,
    cotangent,
):

    def low(*shape):
        return pltpu.VMEM(shape, BF16)

    def full(*shape):
        return pltpu.VMEM(shape, F32)

    streams = [rows for phase in ROWS for rows in phase]
    scratch = [low(2, 64, rows, 128) for rows in streams]
    scratch += [low(count, rows, 128) for count in (64, 48, 12, 3) for rows in streams]
    scratch += [low(D, 1024), low(D, 512), low(1024, D), low(D, FF), low(D, FF), low(FF, D)]
    scratch += [low(D, 1024), low(D, 512)]
    scratch += [low(256, 256), low(256, 256), low(D, D), low(512, 512)]
    scratch += [full(128, 128), full(8, D)]
    scratch += [full(KEYS, 128), full(KEYS, 128), full(TOK, KEYS)]
    scratch += [low(GROUP, TOK, D), full(KEYS, D), low(KEYS, D)]
    scratch += [low(TOK, D), full(TOK, D)]
    scratch += [full(TOK, 1024), full(KEYS, 512), low(H * TOK, HD), low(KEYS, 2 * HD)]
    scratch += [low(H * TOK, KEYS), full(H * TOK, HD), low(TOK, 1024), low(H * TOK, HD)]
    scratch += [low(H * TOK, KEYS), low(TOK, FF), low(TOK, FF), low(TOK, FF), full(TOK, D)]
    scratch += [low(KEYS, 2 * HD), low(2, 4, TOK, 2 * HD), low(TOK, 1024)]
    half = TOK // 2
    scratch += [low(3, 2, half, 2 * HD), low(4, half, 2 * HD)]
    scratch += [low(3, half, 2 * HD), low(half, 2 * HD)]
    dma = pltpu.SemaphoreType.DMA
    scratch += [dma((6, 13)), dma((6, 13)), dma((6, 13)), dma((6, 13))]
    scratch += [dma((11,)), dma((11,)), dma((8,)), dma((8,))]
    out, grad, *sums = pl.pallas_call(
        block_kernel,
        out_shape=[jax.ShapeDtypeStruct((TOK, D), F32)] * 2
        + [jax.ShapeDtypeStruct((rows, 128), F32) for phase in ROWS for rows in phase],
        in_specs=vmem_specs(2) + [pl.BlockSpec(memory_space=pltpu.SMEM)] + vmem_specs(10),
        out_specs=vmem_specs(8),
        scratch_shapes=scratch,
        compiler_params=pltpu.CompilerParams(
            collective_id=0, has_side_effects=True, vmem_limit_bytes=VMEM_BYTES
        ),
        name="block",
    )(
        tokens,
        cotangent,
        lengths,
        w_query,
        w_key,
        w_value,
        w_out,
        w_gate,
        w_up,
        w_down,
        attn_gain[None],
        ffn_gain[None],
        head_gains[None],
    )
    shards = [
        jax.ShapeDtypeStruct(shape, F32)
        for shape in ((5, 1024), (5, 256), (5, 256), (8, D), (5, FF), (5, FF), (16, D))
    ]
    shards += [jax.ShapeDtypeStruct((count,), F32) for count in (5, 5, 4)]
    return pl.pallas_call(
        finish_kernel,
        out_shape=[jax.ShapeDtypeStruct((TOK, D), BF16), jax.ShapeDtypeStruct((TOK, D), F32)]
        + shards,
        in_specs=vmem_specs(8),
        out_specs=vmem_specs(12),
        name="finish",
    )(*sums, out, grad)


def solution(mesh):
    rows = P(("dp", "fsdp"), None)
    vector = P(("dp", "fsdp"))
    return jax.shard_map(
        body,
        mesh=mesh,
        in_specs=(rows,) * 8 + (vector,) * 3 + (P("dp", None), rows),
        out_specs=(rows,) * 9 + (vector,) * 3,
        check_vma=False,
    )
```
